32 devices in a mesh: section: 2 (over core), dp: 4 (over y, x), seq: 4 (over z).
Axes of the slice: x: 2, y: 2, z: 4, core: 2. Of those that a mesh axis runs over, the one named last changes fastest.
Arguments:
- layer_in: bfloat16 [2, 4, 1024, 1120], P(None, 'dp', 'seq'), may hold values from -6 to 6
- cotangent: bfloat16 [2, 4, 1024, 1120], P(None, 'dp', 'seq'), may hold values from -6 to 6
- lengths: int32 [2, 4], P(None, 'dp'), may hold values from 128 to 1024, as said below
- block_order: int32 [4], replicated, may hold values from 0 to 3, each once
- w_qkv: float32 [2, 1120, 3360], P('section', 'dp'), may hold values from -0.25 to 0.25
- w_out: float32 [2, 1120, 1120], P('section', 'dp'), may hold values from -1.5 to 1.5
- w_fc: float32 [2, 1120, 4480], P('section', 'dp'), may hold values from -0.1875 to 0.1875
- w_proj: float32 [2, 4480, 1120], P('section', 'dp'), may hold values from -0.09375 to 0.09375
- norm_gains: float32 [2, 2, 1120], P('section'), may hold values from 0.5 to 1.5
- norm_biases: float32 [2, 2, 1120], P('section'), may hold values from -1.5 to 1.5
Outputs:
- layer_out: bfloat16 [2, 2, 4, 1024, 1120], P('section', None, 'dp', 'seq')
- input_grad: bfloat16 [2, 2, 4, 1024, 1120], P('section', None, 'dp', 'seq')
- grad_qkv: float32 [2, 1120, 3360], P('section', 'dp')
- grad_out: float32 [2, 1120, 1120], P('section', 'dp')
- grad_fc: float32 [2, 1120, 4480], P('section', 'dp')
- grad_proj: float32 [2, 4480, 1120], P('section', 'dp')
- grad_gains: float32 [2, 2, 1120], P('section', None, 'dp')
- grad_biases: float32 [2, 2, 1120], P('section', None, 'dp')
The draws below stay inside these ranges and needn't reach their ends.
Inputs may be any that keep to these rules, and one draw needn't show every extreme that they name: `lengths`: rows at positions at or past a cell's length are padding. For every cell index, one of the 2 micro-batches has a cell of full length 1024. `block_order`: each block index appears once.
All inputs are finite; a program needn't handle non-finite values.
Results may differ from the reference program's by a relative error of at most 0.02.
Values may be sent and summed in bfloat16 or wider, within the bound.
A program may use at most 384 MiB of HBM per device.

```python
import jax
import jax.numpy as jnp
from jax import lax

HEADS = 20
HEAD_DIM = 56
FF = 4480
D = 1120
LEN = 1024
MICRO = 2
CELLS = 4
TOK_SEQ = 256
N_SECTION = 2
N_SEQ = 4


def draw_lengths(key, part):
    key = jax.random.fold_in(key, 11)
    first_key, second_key = jax.random.split(key)
    lowest = max(LEN // 8, 1)
    drawn = jax.random.randint(first_key, (MICRO, CELLS), lowest, LEN + 1, dtype=jnp.int32)
    chosen = jax.random.randint(second_key, (CELLS,), 0, MICRO, dtype=jnp.int32)
    full_rows = jnp.arange(MICRO, dtype=jnp.int32)[:, None] == chosen[None, :]
    return jnp.where(full_rows, LEN, drawn).astype(jnp.int32)


def level_of(own_key, shape, shards, low, largest):
    level = 1.0
    for dim, parts in shards:
        heights = jax.random.uniform(jax.random.fold_in(jax.random.fold_in(own_key, 6), dim), (parts,), jnp.float32, low / len(shards), largest / len(shards))
        level = level * jnp.repeat(jnp.exp(heights), shape[dim] // parts).reshape((-1,) + (1,) * (len(shape) - 1 - dim))
    return level


def centred(rng, shape, deviation, most, cuts=(), held_as=jnp.bfloat16):
    values = deviation * jax.random.normal(rng, shape, jnp.float32)
    if cuts:
        values = values * level_of(rng, shape, cuts, -0.22, 0.18)
    return jnp.clip(values, -most, most).astype(held_as)


def setup_inputs(seed: int = 0) -> dict:
    splits = jax.random.split(jax.random.key(seed), 11)
    layer_in = centred(splits[0], (MICRO, CELLS, LEN, D), 1.0, 6.0, ((1, 4), (2, 4)))
    cotangent = centred(splits[1], (MICRO, CELLS, LEN, D), 1.0, 6.0, ((1, 4), (2, 4)))
    lengths = draw_lengths(jax.random.fold_in(splits[10], 71), 0)
    block_order = jax.random.permutation(splits[3], N_SEQ).astype(jnp.int32)
    w_qkv = centred(splits[4], (N_SECTION, D, 3 * D), (D // 2) ** -0.5, 0.25, ((0, 2), (1, 4)), jnp.float32)
    w_out = centred(splits[5], (N_SECTION, D, D), (max(D // 64, 1)) ** -0.5, 1.5, ((0, 2), (1, 4)), jnp.float32)
    w_fc = centred(splits[6], (N_SECTION, D, FF), D ** -0.5, 0.1875, ((0, 2), (1, 4)), jnp.float32)
    w_proj = centred(splits[7], (N_SECTION, FF, D), FF ** -0.5, 0.09375, ((0, 2), (1, 4)), jnp.float32)
    norm_gains = jnp.clip(1.0 + 0.1 * jax.random.normal(splits[8], (N_SECTION, 2, D), jnp.float32), 0.5, 1.5)
    norm_biases = centred(splits[9], (N_SECTION, 2, D), 0.3, 1.5, ((0, 2),), jnp.float32)
    return dict(layer_in=layer_in, cotangent=cotangent, lengths=lengths, block_order=block_order, w_qkv=w_qkv, w_out=w_out, w_fc=w_fc, w_proj=w_proj, norm_gains=norm_gains, norm_biases=norm_biases)


EPS = 1e-05
NEG = -1e+30

@jax.custom_vjp
def low(v):
    return lax.optimization_barrier(v.astype(jnp.bfloat16)).astype(jnp.float32)

@jax.custom_vjp
def low_back(v):
    return v

def low_keep(v):
    return (low(v), None)

def low_pass(kept, grad):
    return (grad,)

def back_keep(v):
    return (v, None)

def back_low(kept, grad):
    return (low(grad),)
low.defvjp(low_keep, low_pass)
low_back.defvjp(back_keep, back_low)

def layer_norm(values, gain, bias):
    center = values - lax.optimization_barrier(jnp.mean(values, axis=-1, keepdims=True))
    spread = lax.optimization_barrier(jnp.mean(center * center, axis=-1, keepdims=True))
    return center * lax.rsqrt(spread + EPS) * gain + bias

def product(left, right):
    return jnp.dot(left, right, precision=lax.Precision.HIGHEST)

def attention(queries, keys, values, allowed):
    score_scale = HEAD_DIM ** (-0.5)

    def one_head(operands):
        query_head, key_head, value_head = operands
        raw = jnp.einsum('qd,kd->qk', query_head, key_head, precision=lax.Precision.HIGHEST)
        scores = jnp.where(allowed, low_back(raw) * score_scale, NEG)
        probs = jax.nn.softmax(scores, axis=-1)
        return jnp.einsum('qk,kd->qd', low(probs), value_head, precision=lax.Precision.HIGHEST)
    stacked = lax.map(jax.checkpoint(one_head), (queries.transpose(1, 0, 2), keys.transpose(1, 0, 2), values.transpose(1, 0, 2)))
    return stacked.transpose(1, 0, 2).reshape(LEN, D)

def layer(hidden_in, weights, gain, bias, allowed):
    qkv_weight, out_weight, fc_weight, proj_weight = weights
    normed = low(layer_norm(hidden_in, gain[0], bias[0]))
    projected = low_back(low(product(normed, qkv_weight)))
    queries = projected[:, :D].reshape(LEN, HEADS, HEAD_DIM)
    keys = projected[:, D:2 * D].reshape(LEN, HEADS, HEAD_DIM)
    values = projected[:, 2 * D:].reshape(LEN, HEADS, HEAD_DIM)
    attended = low_back(low(attention(queries, keys, values, allowed)))
    residual = hidden_in + low_back(product(attended, out_weight))
    second = low(layer_norm(residual, gain[1], bias[1]))
    pre_act = low_back(product(second, fc_weight))
    activated = low(jax.nn.gelu(pre_act, approximate=False))
    return residual + low_back(product(activated, proj_weight))

def reference(layer_in, cotangent, lengths, block_order, w_qkv, w_out, w_fc, w_proj, norm_gains, norm_biases):
    cell_count = MICRO * CELLS
    position = (block_order[:, None] * TOK_SEQ + jnp.arange(TOK_SEQ, dtype=jnp.int32)[None, :]).reshape(LEN).astype(jnp.int32)
    flat_lengths = lengths.reshape(cell_count).astype(jnp.int32)
    input_rows = layer_in.astype(jnp.float32).reshape(cell_count, LEN, D)
    probe = jnp.zeros_like(input_rows)

    def model(input_rows, probe, w_qkv, w_out, w_fc, w_proj, norm_gains, norm_biases):
        first = (low(w_qkv[0]), low(w_out[0]), low(w_fc[0]), low(w_proj[0]))
        later = (low(w_qkv[1]), low(w_out[1]), low(w_fc[1]), low(w_proj[1]))

        def one_cell(operands):
            cell_in, cell_probe, length = operands
            allowed = (position[None, :] <= position[:, None]) & (position[None, :] < length)

            def first_layer(values):
                return layer(values, first, norm_gains[0], norm_biases[0], allowed)

            def later_layer(values):
                return layer(values, later, norm_gains[1], norm_biases[1], allowed)
            middle = jax.checkpoint(first_layer)(cell_in)
            middle = low_back(low(middle) + cell_probe)
            final = jax.checkpoint(later_layer)(middle)
            return (middle, final)
        return lax.map(jax.checkpoint(one_cell), (input_rows, probe, flat_lengths))
    (middle, final), back = jax.vjp(model, input_rows, probe, w_qkv, w_out, w_fc, w_proj, norm_gains, norm_biases)
    cot_values = cotangent.astype(jnp.float32).reshape(cell_count, LEN, D)
    all_grads = back((jnp.zeros_like(middle), cot_values))
    d_input, d_probe, g_qkv, g_out, g_fc, g_proj, g_gains, g_biases = all_grads
    full_shape = (MICRO, CELLS, LEN, D)
    layer_out = jnp.stack([middle.reshape(full_shape), final.reshape(full_shape)]).astype(jnp.bfloat16)
    input_grad = jnp.stack([d_input.reshape(full_shape), d_probe.reshape(full_shape)]).astype(jnp.bfloat16)
    return (layer_out, input_grad, g_qkv, g_out, g_fc, g_proj, g_gains, g_biases)
```

```python
import functools
import math

import jax
import jax.numpy as jnp
from jax import lax
from jax.experimental import pallas as pl
from jax.experimental.pallas import tpu as pltpu
from jax.sharding import PartitionSpec as P

HEADS = 20
HEAD_DIM = 56
EPS = 1e-05
NEG = -1e30
LANES = 128
WINDOW = 256
VMEM_LIMIT = 58 * 1024 * 1024
MESH = pl.DeviceIdType.MESH

bf16 = jnp.bfloat16
f32 = jnp.float32


def round_up(size, grain):
    return -(-size // grain) * grain


def dot_nn(left, right):
    return lax.dot_general(left, right, (((1,), (0,)), ((), ())), preferred_element_type=f32)


def dot_nt(left, right):
    return lax.dot_general(left, right, (((1,), (1,)), ((), ())), preferred_element_type=f32)


def dot_tn(left, right):
    return lax.dot_general(left, right, (((0,), (0,)), ((), ())), preferred_element_type=f32)


LINKED = 4


def greet(*places):
    barrier = pltpu.get_barrier_semaphore()
    for place in places:
        pl.semaphore_signal(barrier, inc=1, device_id=place, device_id_type=MESH)
    pl.semaphore_wait(barrier, len(places))


def remote_copy(source, target, send, recv, **place):
    return pltpu.make_async_remote_copy(
        src_ref=source, dst_ref=target, send_sem=send, recv_sem=recv, device_id=place, device_id_type=MESH
    )


def pair_places():
    z = lax.axis_index("seq")
    return {"seq": z + 1 - 2 * lax.rem(z, 2)}, {"section": 1 - lax.axis_index("section")}


def partners():
    core = lax.axis_index("section")
    rank = lax.axis_index("dp")
    x, y = lax.rem(rank, 2), rank // 2
    near = lax.rem(y + core, 2) * 2 + lax.rem(x + 1 - core, 2)
    far = lax.rem(y + 1 - core, 2) * 2 + lax.rem(x + core, 2)
    return near, far, 3 - rank


def vmem_specs(count):
    return [pl.BlockSpec(memory_space=pltpu.VMEM)] * count


def any_specs(count):
    return [pl.BlockSpec(memory_space=pl.ANY)] * count


def sum_of(parts):
    return functools.reduce(jnp.add, parts)


def load_all(copies):
    for copy in copies:
        copy.start()


class Reduction:
    def __init__(self, arrays, parts):
        self.arrays = [(a.shape, a.dtype) for a in arrays]
        self.chunks = []
        for index, (shape, _) in enumerate(self.arrays):
            step = round_up(-(-shape[1] // parts[index]), 16)
            self.chunks += [(index, a, min(step, shape[1] - a)) for a in range(0, shape[1], step)]
        self.count = len(self.chunks)
        self.classes, self.places = {}, []
        for array, _, rows in self.chunks:
            (_, _, columns), dtype = self.arrays[array]
            key = (columns > 2048, str(dtype))
            most = self.classes.setdefault(key, [0, 0, 0, dtype])
            self.places.append((list(self.classes).index(key), most[0]))
            most[:3] = [most[0] + 1, max(most[1], rows), max(most[2], columns)]

    def out_shapes(self):
        return tuple(jax.ShapeDtypeStruct(shape[1:], dtype) for shape, dtype in self.arrays)

    def scratch(self):
        sizes = [((rows, self.arrays[a][0][2]), self.arrays[a][1]) for a, _, rows in self.chunks]
        many = [pltpu.VMEM((4,) + s, t) for s, t in sizes] + [pltpu.VMEM((2,) + s, t) for s, t in sizes]
        single = [pltpu.VMEM(s, t) for s, t in sizes] * 3
        slots = [pltpu.VMEM((4,) + tuple(c[1:3]), c[3]) for c in self.classes.values() for _ in range(2)]
        n = self.count
        dma = pltpu.SemaphoreType.DMA
        sems = [dma((n, 4)), dma((n, 4)), dma((n, 4)), dma((n, 3)), dma((n, 3)), dma((n, 3)), dma((n, 3))]
        return many + single + slots + sems + [pltpu.SemaphoreType.REGULAR((len(self.classes),))]

    def bind(self, kept, given, results, scratch):
        n, k = self.count, len(self.classes)
        self.kept, self.given, self.results = kept, given, results
        self.here, self.came, self.far_in, self.z_in, self.z_mid = (scratch[i * n:(i + 1) * n] for i in range(5))
        self.slots, rest = scratch[5 * n:5 * n + 2 * k], scratch[5 * n + 2 * k:]
        (self.load_sem, self.core_send, self.core_recv, self.dp_send, self.dp_recv, self.z_send, self.z_recv, self.free) = rest
        z = lax.axis_index("seq")
        self.rank = lax.axis_index("dp")
        self.near, self.far, self.across = partners()
        self.inner = (z == 1) | (z == 2)
        self.pair_z, self.other_z = z + 1 - 2 * lax.rem(z, 2), 3 - z
        self.other_core = {"section": 1 - lax.axis_index("section")}
        self.settled = lambda chunk: None

    def peers(self):
        return [{"dp": self.near}, {"dp": self.far}, {"seq": self.pair_z}, {"seq": self.other_z}, self.other_core]

    def loads(self, c):
        array, row, rows = self.chunks[c]
        return [
            pltpu.make_async_copy(
                self.kept[array].at[block, pl.ds(row, rows)], self.here[c].at[i], self.load_sem.at[c, i]
            )
            for i, block in enumerate((self.near, self.across, self.far, self.rank))
        ]

    def slot(self, c, index):
        array, _, rows = self.chunks[c]
        kind, at = self.places[c]
        return self.slots[2 * kind + at % 2].at[index, pl.ds(0, rows), pl.ds(0, self.arrays[array][0][2])]

    def to_core(self, c):
        array, row, rows = self.chunks[c]
        return [
            remote_copy(
                self.given[array].at[block, pl.ds(row, rows)],
                self.slot(c, i),
                self.core_send.at[c, i],
                self.core_recv.at[c, i],
                **self.other_core,
            )
            for i, block in enumerate((self.far, self.across, self.near, self.rank))
        ]

    def nears(self, c):
        return [
            remote_copy(self.here[c].at[i], self.came[c].at[i], self.dp_send.at[c, i], self.dp_recv.at[c, i], dp=self.near)
            for i in range(2)
        ]

    def fars(self, c):
        return remote_copy(self.here[c].at[2], self.far_in[c], self.dp_send.at[c, 2], self.dp_recv.at[c, 2], dp=self.far)

    def along(self, c, k):
        source = self.z_mid[c] if k == 2 else self.here[c].at[3]
        target = self.z_mid[c] if k == 1 else self.z_in[c]
        place = self.other_z if k == 1 else self.pair_z
        return remote_copy(source, target, self.z_send.at[c, k], self.z_recv.at[c, k], seq=place)

    def add(self, c, index, *others):
        here = self.here[c]
        total = here[index].astype(f32)
        for other in others:
            total = total + other[...].astype(f32)
        here[index] = total.astype(here.dtype)

    def store(self, c, value):
        array, row, rows = self.chunks[c]
        self.results[array][pl.ds(row, rows)] = value
        self.settled(c)

    def open(self):
        for c in range(self.count):
            load_all(self.loads(c))

    def give(self, c=0):
        kind, at = self.places[c]
        if at >= 2:
            pl.semaphore_wait(self.free.at[kind], 1)
        load_all(self.to_core(c))

    def begin(self, c):
        for copy in self.loads(c):
            copy.wait()
        for copy in self.to_core(c):
            copy.wait_recv()
        for i in range(2):
            self.add(c, i, self.slot(c, i))
        load_all(self.nears(c))
        for i in (2, 3):
            self.add(c, i, self.slot(c, i))
        kind, at = self.places[c]
        if (kind, at + 2) in self.places:
            pl.semaphore_signal(self.free.at[kind], inc=1, device_id=self.other_core, device_id_type=MESH)
        if c + 2 < self.count:
            self.give(c + 2)

    def after_near(self, c):
        for copy in self.nears(c):
            copy.wait()
        self.add(c, 2, self.came[c].at[1])
        self.fars(c).start()

    def after_far(self, c):
        self.fars(c).wait()
        self.add(c, 3, self.came[c].at[0], self.far_in[c])
        pl.when(jnp.logical_not(self.inner))(self.along(c, 0).start)

    def after_inward(self, c):
        pl.when(jnp.logical_not(self.inner))(self.along(c, 0).wait_send)

        @pl.when(self.inner)
        def add():
            self.along(c, 0).wait_recv()
            self.add(c, 3, self.z_in[c])
            self.along(c, 1).start()

    def after_middle(self, c):
        @pl.when(self.inner)
        def add():
            self.along(c, 1).wait()
            total = self.here[c][3].astype(f32) + self.z_mid[c][...].astype(f32)
            self.z_mid[c][...] = total.astype(self.z_mid[c].dtype)
            self.along(c, 2).start()
            self.store(c, self.z_mid[c][...])

    def after_outward(self, c):
        pl.when(self.inner)(self.along(c, 2).wait_send)

        @pl.when(jnp.logical_not(self.inner))
        def take():
            self.along(c, 2).wait_recv()
            self.store(c, self.z_in[c][...])

        for copy in self.to_core(c):
            copy.wait_send()

    def turns(self):
        steps = (self.begin, self.after_near, self.after_far, self.after_inward, self.after_middle, self.after_outward)

        def turn(number):
            for lag, step in enumerate(steps):
                if 0 <= number - lag < self.count:
                    step(number - lag)

        return [functools.partial(turn, number) for number in range(self.count + len(steps) - 1)]


class Homes:
    def __init__(self, items):
        self.items = items
        self.count = 1 + max(target for _, target in items)

    def out_shapes(self, rows):
        return (jax.ShapeDtypeStruct((2,) + rows.shape, rows.dtype),) * self.count

    def scratch(self):
        dma = pltpu.SemaphoreType.DMA
        n = len(self.items)
        return [dma((n, 2)), dma((n, 2)), dma((n,))]

    def bind(self, rows, homes, scratch):
        self.rows, self.homes = rows, homes
        self.send, self.recv, self.local = scratch
        z = lax.axis_index("seq")
        self.group = z // 2
        self.swapped = z + 2 - 4 * self.group
        self.first_core = lax.axis_index("section") == 0

    def peers(self):
        return [{"section": section, "seq": self.swapped} for section in range(2)]

    def target(self, i):
        return self.homes[self.items[i][1]].at[self.group]

    def stays(self, i):
        return pltpu.make_async_copy(self.rows[i], self.target(i), self.local.at[i])

    def beside(self, i):
        return remote_copy(self.rows[i], self.target(i), self.send.at[i, 0], self.recv.at[i, 0], section=1)

    def away(self, i):
        layer = self.items[i][0]
        return remote_copy(
            self.rows[i], self.target(i), self.send.at[i, 1], self.recv.at[i, 1], section=layer, seq=self.swapped
        )

    def start(self):
        @pl.when(self.first_core)
        def first():
            for i, (layer, _) in enumerate(self.items):
                (self.stays(i) if layer == 0 else self.beside(i)).start()

        @pl.when(jnp.logical_not(self.first_core))
        def second():
            for i in range(len(self.items)):
                self.away(i).start()

    def finish(self):
        @pl.when(self.first_core)
        def first():
            for i, (layer, _) in enumerate(self.items):
                if layer == 0:
                    self.stays(i).wait()
                    self.away(i).wait_recv()
                else:
                    self.beside(i).wait_send()

        @pl.when(jnp.logical_not(self.first_core))
        def second():
            for i, (layer, _) in enumerate(self.items):
                self.away(i).wait_send()
                if layer == 1:
                    self.beside(i).wait_recv()
                    self.away(i).wait_recv()


HEAD_GROUPS = ((0, 6), (6, 6), (12, 6), (18, 2))
LANES_IN = ((0, 384), (384, 384), (768, 256), (1024, 128))
BACKWARD_ORDER = (
    "p", "t", "p", "t", "p", "s0", "t", "p", "p", "t", "p", "s1", "a0", "t", "p", "p", "t", "p", "s2", "a1",
    "t", "a2", "p", "s3", "t", "a3", "t", "z",
)
LANES_OUT = ((0, 256), (256, 384), (640, 256), (896, 256))


def window_in(group, head):
    return head // 3 if group == 0 else (7 * head - 10) // 16


def window_out(group, head):
    return 7 if group == 3 else 7 * head // 16


def head_window(head, tile, rows):
    start = pl.multiple_of(tile * LANES, LANES)
    lane = lax.broadcasted_iota(jnp.int32, (rows, WINDOW), 1) + (start - head * HEAD_DIM)
    return pl.ds(start, WINDOW), (lane >= 0) & (lane < HEAD_DIM)


def two_heads(group, step, work):
    def pair(i, carry):
        work(group, 2 * i)
        work(group, 2 * i + 1)
        return carry

    lax.fori_loop(step, step + 1, pair, 0)


def heads_of(group, work):
    first, count = HEAD_GROUPS[group]

    def pair(step, carry):
        work(group, first + 2 * step)
        work(group, first + 2 * step + 1)
        return carry

    lax.fori_loop(0, count // 2, pair, 0)


def fill_bias(bias, place, row_axis):
    blocks, tokens, _ = bias.shape
    row = lax.broadcasted_iota(jnp.int32, (tokens, tokens), row_axis) + place[1]
    for b in range(blocks):
        column = lax.broadcasted_iota(jnp.int32, (tokens, tokens), 1 - row_axis) + place[1 + b]
        bias[b] = jnp.where((column <= row) & (column < place[0]), 0.0, NEG)


def attention_steps(place, q_ref, kv_refs, o_pad, lse_ref, bias, links):
    tokens, blocks = q_ref.shape[0], len(kv_refs)
    scale = HEAD_DIM ** -0.5
    groups = range(len(HEAD_GROUPS))

    def copies(group):
        send, recv = links
        along, beside = pair_places()
        lanes = (slice(None), slice(None), pl.ds(*LANES_IN[group]))

        def copy(k, source, target, place):
            return remote_copy(
                kv_refs[source].at[lanes], kv_refs[target].at[lanes], send.at[group, k], recv.at[group, k], **place
            )

        return copy(0, 0, 1, along), copy(1, 0, 2, beside), copy(2, 1, 3, beside)

    def start():
        if links:
            for group in groups:
                copies(group)[0].start()
                copies(group)[1].start()
        o_pad[...] = jnp.zeros(o_pad.shape, o_pad.dtype)
        fill_bias(bias, place, 0)
        lse_ref[...] = jnp.zeros(lse_ref.shape, f32)

    def one_head(group, head):
        lse_lane = lax.broadcasted_iota(jnp.int32, lse_ref.shape, 1)
        lanes, inside = head_window(head, window_in(group, head), tokens)
        query = jnp.where(inside, q_ref[:, lanes], 0).astype(bf16)
        scores = [dot_nt(query, kv_refs[b][0, :, lanes]) * scale + bias[b] for b in range(blocks)]
        peak = jnp.max(functools.reduce(jnp.maximum, scores), axis=1, keepdims=True)
        weights = [jnp.exp(s - peak) for s in scores]
        total = jnp.sum(functools.reduce(jnp.add, weights), axis=1, keepdims=True)
        share = 1.0 / total
        out = sum_of([dot_nn((w * share).astype(bf16), kv_refs[b][1, :, lanes]) for b, w in enumerate(weights)])
        o_pad[:, lanes] = jnp.where(inside, out, o_pad[:, lanes].astype(f32)).astype(bf16)
        lse_ref[...] = jnp.where(lse_lane == head, peak + jnp.log(total), lse_ref[...])

    def work(group):
        if links:
            first, second, third = copies(group)
            first.wait_recv()
            third.start()
            second.wait_recv()
            third.wait_recv()
        heads_of(group, one_head)

    def end():
        if links:
            for group in groups:
                for copy in copies(group):
                    copy.wait_send()

    return start, work, end


def attention_forward_kernel(blocks, place, q_ref, *refs):
    o_ref, lse_ref, bias = refs[blocks:]
    start, work, _ = attention_steps(place, q_ref, refs[:blocks], o_ref, lse_ref, bias, ())
    start()
    for group in range(len(HEAD_GROUPS)):
        work(group)


def attention_forward(place, query, kv_blocks, blocks):
    tokens, width = query.shape
    results = pl.pallas_call(
        functools.partial(attention_forward_kernel, blocks),
        out_shape=(
            jax.ShapeDtypeStruct((tokens, width), bf16),
            jax.ShapeDtypeStruct((tokens, LANES), f32),
        ),
        in_specs=[pl.BlockSpec(memory_space=pltpu.SMEM)] + vmem_specs(1 + len(kv_blocks)),
        out_specs=tuple(vmem_specs(2)),
        scratch_shapes=[pltpu.VMEM((blocks, tokens, tokens), f32)],
        compiler_params=pltpu.CompilerParams(vmem_limit_bytes=VMEM_LIMIT),
        cost_estimate=pl.CostEstimate(
            flops=4 * HEADS * tokens * tokens * blocks * WINDOW,
            bytes_accessed=60_000_000,
            transcendentals=HEADS * tokens * tokens * blocks,
        ),
        name="attention_forward",
    )(place, query, *kv_blocks)
    return results[0], results[1], kv_blocks


def attention_backward_kernel(blocks, reduction, going, place, q_ref, d_ref, lse_ref, *refs):
    kv_refs, refs = refs[:blocks], refs[blocks:]
    turns = []
    linked = reduction is not None
    if linked:
        arrays = len(reduction.arrays)
        kept, given, refs = refs[:arrays], refs[arrays:2 * arrays], refs[2 * arrays:]
        rows, refs = refs[:len(going.items)], refs[len(going.items):]
        dq_ref, out_ref, refs = refs[0], refs[1], refs[2:]
        results, refs = refs[:arrays], refs[arrays:]
        homes, refs = refs[:going.count], refs[going.count:]
        dq_pad, bias, grads, from_core, from_pair, send, recv = refs[:7]
        going.bind(rows, homes, refs[7:10])
        reduction.bind(kept, given, results, refs[10:])
        along, beside = pair_places()
        reduction.open()
        greet(*reduction.peers(), *going.peers())
        reduction.give(0)
        reduction.give(1)
        going.start()
        turns = reduction.turns()
    else:
        dq_ref, refs = refs[0], refs[1:]
        out_refs, (dq_pad, bias, grads) = refs[:blocks], refs[blocks:]
    tokens = q_ref.shape[0]
    scale = HEAD_DIM ** -0.5
    dq_pad[...] = jnp.zeros(dq_pad.shape, dq_pad.dtype)
    for b in range(blocks):
        grads[b] = jnp.zeros(grads.shape[1:], grads.dtype)
    fill_bias(bias, place, 1)

    def one_head(group, head):
        lanes, inside = head_window(head, window_out(group, head), tokens)
        query = jnp.where(inside, q_ref[:, lanes], 0).astype(bf16)
        grad = jnp.where(inside, d_ref[:, lanes], 0).astype(bf16)
        lse = lse_ref[pl.ds(head, 1), :]
        probs = [
            jnp.exp(dot_nt(kv_refs[b][0, :, lanes], query) * scale + bias[b] - lse) for b in range(blocks)
        ]
        d_probs = [dot_nt(kv_refs[b][1, :, lanes], grad) for b in range(blocks)]
        inner = jnp.sum(sum_of([p * dp for p, dp in zip(probs, d_probs)]), axis=0, keepdims=True)
        d_query = None
        for b in range(blocks):
            d_score = (probs[b] * (d_probs[b] - inner) * scale).astype(bf16)
            grads[b, 0, :, lanes] = grads[b, 0, :, lanes] + dot_nn(d_score, query).astype(bf16)
            grads[b, 1, :, lanes] = grads[b, 1, :, lanes] + dot_nn(probs[b].astype(bf16), grad).astype(bf16)
            part = dot_tn(d_score, kv_refs[b][0, :, lanes])
            d_query = part if d_query is None else d_query + part
        dq_pad[:, lanes] = jnp.where(inside, d_query, dq_pad[:, lanes].astype(f32)).astype(bf16)

    def lanes_of(group):
        return (slice(None), slice(None), pl.ds(*LANES_OUT[group]))

    def to_core(group, k):
        lanes = lanes_of(group)
        return remote_copy(
            grads.at[2 + k].at[lanes], from_core.at[k].at[lanes], send.at[group, k], recv.at[group, k], **beside
        )

    def to_pair(group):
        lanes = lanes_of(group)
        return remote_copy(
            grads.at[1].at[lanes], from_pair.at[lanes], send.at[group, 2], recv.at[group, 2], **along
        )

    def add_core(group):
        lanes = lanes_of(group)
        for k in (1, 0):
            to_core(group, k).wait_recv()
            mine = grads.at[k]
            mine[lanes] = (mine[lanes].astype(f32) + from_core.at[k][lanes].astype(f32)).astype(bf16)
            if k == 1:
                to_pair(group).start()

    groups = range(len(HEAD_GROUPS))
    if not linked:
        for group in groups:
            heads_of(group, one_head)
        dq_ref[...] = dq_pad[...]
        for b in range(blocks):
            out_refs[b][...] = grads[b]
        return

    def last_add():
        for group in groups:
            lanes = lanes_of(group)
            to_pair(group).wait_recv()
            out_ref[lanes] = (grads.at[0][lanes].astype(f32) + from_pair[lanes].astype(f32)).astype(bf16)

    heads = [(group, (first + h) // 2) for group, (first, count) in enumerate(HEAD_GROUPS) for h in range(0, count, 2)]
    for step in BACKWARD_ORDER:
        if step == "p":
            two_heads(*heads.pop(0), one_head)
        elif step == "t":
            turns.pop(0)()
        elif step == "z":
            last_add()
        elif step[0] == "s":
            to_core(int(step[1]), 1).start()
            to_core(int(step[1]), 0).start()
        else:
            add_core(int(step[1]))
    for turn in turns:
        turn()
    dq_ref[...] = dq_pad[...]
    for group in groups:
        to_core(group, 0).wait_send()
        to_core(group, 1).wait_send()
        to_pair(group).wait_send()
    going.finish()


def attention_backward(place, query, d_out, lse_rows, kv_blocks, kept=(), given=(), parts=(), layers=(), rows=()):
    blocks = len(kv_blocks)
    tokens, width = query.shape
    one = jax.ShapeDtypeStruct((2, tokens, width), bf16)
    reduction = Reduction(kept, parts) if kept else None
    going = Homes([(layer, 0) for layer in layers]) if kept else None
    own = [one] * (1 if kept else blocks)
    dma = pltpu.SemaphoreType.DMA((len(HEAD_GROUPS), 3))
    linked = []
    if kept:
        linked = [pltpu.VMEM((2, 2, tokens, width), bf16), pltpu.VMEM((2, tokens, width), bf16), dma, dma]
        linked += going.scratch() + reduction.scratch()
    results = pl.pallas_call(
        functools.partial(attention_backward_kernel, blocks, reduction, going),
        out_shape=(jax.ShapeDtypeStruct((tokens, width), bf16),)
        + tuple(own)
        + (reduction.out_shapes() + going.out_shapes(rows[0]) if kept else ()),
        in_specs=[pl.BlockSpec(memory_space=pltpu.SMEM)] + vmem_specs(3 + blocks) + any_specs(2 * len(kept) + len(rows)),
        out_specs=tuple(vmem_specs(1 + len(own) + len(kept)) + any_specs(1 if kept else 0)),
        scratch_shapes=[
            pltpu.VMEM((tokens, width), bf16),
            pltpu.VMEM((blocks, tokens, tokens), f32),
            pltpu.VMEM((blocks, 2, tokens, width), bf16),
        ]
        + linked,
        compiler_params=pltpu.CompilerParams(
            vmem_limit_bytes=VMEM_LIMIT, **(dict(collective_id=4 + len(rows), has_side_effects=True) if kept else {})
        ),
        cost_estimate=pl.CostEstimate(
            flops=10 * HEADS * tokens * tokens * blocks * WINDOW,
            bytes_accessed=400_000_000 if kept else 100_000_000,
            transcendentals=HEADS * tokens * tokens * blocks,
        ),
        name="attention_backward",
    )(place, query, d_out, lse_rows, *kv_blocks, *kept, *given, *rows)
    first = 1 + len(own)
    return results[0], list(results[1:first]), list(results[first:first + len(kept)]), results[-1]


def last_kernel(reduction, going, early, layers, *refs):
    arrays, items = len(reduction.arrays), len(going.items)
    kept, given, refs = refs[:arrays], refs[arrays:2 * arrays], refs[2 * arrays:]
    rows, refs = refs[:items], refs[items:]
    sums, refs = (refs[:early], refs[early:2 * early]), refs[2 * early:]
    results, refs = refs[:arrays], refs[arrays:]
    homes, refs = refs[:going.count], refs[going.count:]
    other_half, refs = refs[:early + 1], refs[early + 1:]
    half_send, half_recv, chunk_send, chunk_recv = refs[:4]
    going.bind(rows, homes, refs[4:7])
    reduction.bind(kept, given, results, refs[7:])
    core = lax.axis_index("section")
    first_core = core == 0
    reduction.open()
    greet(*reduction.peers(), *going.peers())
    reduction.give(0)
    reduction.give(1)

    def half(i, layer):
        return remote_copy(sums[layer][i], other_half[i], half_send.at[i], half_recv.at[i], section=1 - core)

    def late_half(c):
        array, row, size = reduction.chunks[c]
        return remote_copy(
            results[array].at[pl.ds(row, size)],
            other_half[early].at[pl.ds(row, size)],
            chunk_send.at[c],
            chunk_recv.at[c],
            section=1 - core,
        )

    def settled(c):
        layer = layers[reduction.chunks[c][0]]
        if layer is not None:
            pl.when(core != layer)(late_half(c).start)

    reduction.settled = settled

    @pl.when(first_core)
    def second_layer():
        for i in range(early):
            half(i, 1).start()

    @pl.when(jnp.logical_not(first_core))
    def first_layer():
        for i in range(early):
            half(i, 0).start()

    going.start()
    for turn in reduction.turns():
        turn()
    for i in range(early):
        half(i, 0).wait()
    for c, (array, _, _) in enumerate(reduction.chunks):
        layer = layers[array]
        if layer is not None:
            pl.when(core != layer)(late_half(c).wait_send)
            pl.when(core == layer)(late_half(c).wait_recv)

    going.finish()


def reduce_last(kept, given, parts, layers, rows, first_sums, second_sums):
    reduction = Reduction(kept, parts)
    going = Homes([(0, 0)])
    early = len(first_sums)
    late = kept[layers.index(0)]
    halves = [jax.ShapeDtypeStruct(v.shape, v.dtype) for v in first_sums]
    halves.append(jax.ShapeDtypeStruct(late.shape[1:], late.dtype))
    n = reduction.count
    dma = pltpu.SemaphoreType.DMA
    out = pl.pallas_call(
        functools.partial(last_kernel, reduction, going, early, layers),
        out_shape=reduction.out_shapes() + going.out_shapes(rows) + tuple(halves),
        in_specs=any_specs(2 * len(kept) + 1 + 2 * early),
        out_specs=tuple(vmem_specs(len(kept)) + any_specs(early + 2)),
        scratch_shapes=[dma((early,)), dma((early,)), dma((n,)), dma((n,))] + going.scratch() + reduction.scratch(),
        compiler_params=pltpu.CompilerParams(
            collective_id=2, has_side_effects=True, vmem_limit_bytes=VMEM_LIMIT
        ),
        cost_estimate=pl.CostEstimate(flops=0, bytes_accessed=400_000_000, transcendentals=0),
        name="reduce_last",
    )(*kept, *given, rows, *first_sums, *second_sums)
    out = list(out)
    return out[:len(kept)], out[len(kept)], out[len(kept) + 1:]


def finish_kernel(parts, *refs):
    kinds = len(parts)
    first, second, other, targets, refs = refs[:kinds], refs[kinds:2 * kinds], refs[2 * kinds:3 * kinds], refs[3 * kinds:4 * kinds], refs[4 * kinds:]
    own, rest, stages, refs = refs[:kinds], refs[kinds:2 * kinds], refs[2 * kinds:3 * kinds], refs[3 * kinds:]
    sems, own_sems, rest_sems = refs
    first_core = lax.axis_index("section") == 0
    for k in range(kinds):
        pl.when(first_core)(pltpu.make_async_copy(first[k], own[k], own_sems.at[k]).start)
        pl.when(jnp.logical_not(first_core))(pltpu.make_async_copy(second[k], own[k], own_sems.at[k]).start)
        pltpu.make_async_copy(other[k], rest[k], rest_sems.at[k]).start()
    for k in range(kinds):
        rows, columns = targets[k].shape
        blocks = max(parts[k], 1)
        half, padded = first[k].shape[0], first[k].shape[1] // blocks
        size = columns // blocks
        pltpu.make_async_copy(first[k], own[k], own_sems.at[k]).wait()
        pltpu.make_async_copy(other[k], rest[k], rest_sems.at[k]).wait()

        def put(top, bottom, k=k, rows=rows, blocks=blocks, half=half, padded=padded, size=size):
            for b in range(blocks):
                here = pl.ds(b * size, size)
                stages[k][pl.ds(0, half), here] = top[:, pl.ds(b * padded, padded)].astype(f32)[:, :size]
                stages[k][pl.ds(half, rows - half), here] = bottom[:, pl.ds(b * padded, padded)].astype(f32)[:rows - half, :size]

        pl.when(first_core)(functools.partial(put, own[k], rest[k]))
        pl.when(jnp.logical_not(first_core))(functools.partial(put, rest[k], own[k]))
        pltpu.make_async_copy(stages[k], targets[k], sems.at[k]).start()
    for k in range(kinds):
        pltpu.make_async_copy(stages[k], targets[k], sems.at[k]).wait()


def finish(first, second, other, shapes, parts):
    kinds = len(first)
    return pl.pallas_call(
        functools.partial(finish_kernel, parts),
        out_shape=tuple(jax.ShapeDtypeStruct(s, f32) for s in shapes),
        in_specs=any_specs(3 * kinds),
        out_specs=tuple(any_specs(kinds)),
        scratch_shapes=[pltpu.VMEM(v.shape, bf16) for v in first] * 2
        + [pltpu.VMEM(s, f32) for s in shapes]
        + [pltpu.SemaphoreType.DMA((kinds,))] * 3,
        compiler_params=pltpu.CompilerParams(vmem_limit_bytes=VMEM_LIMIT),
        name="finish",
    )(*first, *second, *other)


def padded_shape(weight, parts):
    rows, columns = weight.shape
    rows = round_up(rows, LANES) if parts == 0 else round_up(rows, 32)
    return rows, columns if parts < 2 else parts * round_up(columns // parts, LANES)


STAGE_ROWS = 9


class Gather:
    def __init__(self, masters, parts, over_seq):
        self.parts, self.kinds, self.over_seq = parts, len(masters), over_seq
        self.shapes = [padded_shape(m, p) for m, p in zip(masters, parts)]
        self.wide_shapes = []
        for m in masters:
            rows = round_up(-(-m.shape[0] // STAGE_ROWS), 16)
            self.wide_shapes.append((2, rows, m.shape[1]))

    def out_shapes(self, ranks):
        return tuple(jax.ShapeDtypeStruct((ranks,) + s, bf16) for s in self.shapes) * 2

    def scratch(self):
        dma = pltpu.SemaphoreType.DMA
        n = 2 * self.kinds
        return (
            [pltpu.VMEM(s, f32) for s in self.wide_shapes]
            + [pltpu.VMEM(s, bf16) for s in self.shapes] * 2
            + [dma((self.kinds, 2)), dma((n,)), dma((n, 10)), dma((n, 10))]
        )

    def bind(self, masters, whole, scratch):
        n = self.kinds
        self.masters, self.whole = masters, whole
        self.wide, self.shares, self.got = scratch[:n], scratch[n:2 * n], scratch[2 * n:3 * n]
        self.wide_sem, self.own_sem, self.send, self.recv = scratch[3 * n:]
        self.core = lax.axis_index("section")
        self.rank = lax.axis_index("dp")
        z = lax.axis_index("seq")
        self.near, self.far, self.across = partners()
        self.parity = lax.rem(z, 2)
        self.pair_z = z + 1 - 2 * self.parity

    def peers(self):
        return [{"dp": self.near}, {"dp": self.far}, {"seq": self.pair_z}, {"section": 1 - self.core}]

    def rows_of(self, u, start, size):
        half = self.whole[u].shape[1] // 2
        return pl.ds(pl.multiple_of(self.core * half + start, 16), size)

    def copy(self, u, k, block, start, size, **place):
        ref = self.whole[u].at[block, self.rows_of(u, start, size)]
        return remote_copy(ref, ref, self.send.at[u, k], self.recv.at[u, k], **place)

    def sizes(self, u):
        half = self.whole[u].shape[1] // 2
        rest = round_up(half * self.over_seq[u] // 9, 16)
        return half - rest, rest

    def to_dp(self, u, k, source=None):
        size, rest = self.sizes(u)
        block, place = ((self.rank, self.near), (self.rank, self.far), (self.far, self.near))[k]
        rows = self.rows_of(u, self.parity * rest, size)
        target = self.whole[u].at[block, rows]
        source = target if source is None else source.at[rows]
        return remote_copy(source, target, self.send.at[u, k], self.recv.at[u, k], dp=place)

    def to_pair(self, u, k):
        size, rest = self.sizes(u)
        block = (self.near, self.far, self.across)[k]
        return self.copy(u, 3 + k, block, self.parity * size, rest, seq=self.pair_z)

    def to_core(self, u, k):
        half = self.whole[u].shape[1] // 2
        return self.copy(u, 6 + k, (self.near, self.far, self.across)[k], 0, half, section=1 - self.core)

    def given(self, u):
        kind = u % self.kinds
        return remote_copy(
            self.shares[kind], self.got[kind], self.send.at[u, 9], self.recv.at[u, 9], section=1 - self.core
        )

    def kept(self, u, source):
        return pltpu.make_async_copy(source[u % self.kinds], self.whole[u].at[self.rank], self.own_sem.at[u])

    def stages(self, kind):
        rows, step = self.masters[kind].shape[0], self.wide_shapes[kind][1]
        return [(i % 2, a, min(step, rows - a)) for i, a in enumerate(range(0, rows, step))]

    def load(self, kind, stage):
        slot, first, size = stage
        return pltpu.make_async_copy(
            self.masters[kind].at[pl.ds(first, size)],
            self.wide[kind].at[slot, pl.ds(0, size)],
            self.wide_sem.at[kind, slot],
        )

    def open(self):
        for kind in range(self.kinds):
            for stage in self.stages(kind)[:2]:
                self.load(kind, stage).start()

    def cast(self, kind):
        share, wide = self.shares[kind], self.wide[kind]
        blocks = max(self.parts[kind], 1)
        size, padded = wide.shape[2] // blocks, share.shape[1] // blocks
        share[...] = jnp.zeros(share.shape, bf16)
        stages = self.stages(kind)
        for i, (slot, first, count) in enumerate(stages):
            self.load(kind, stages[i]).wait()
            for b in range(blocks):
                value = wide[slot, pl.ds(0, count), b * size:(b + 1) * size]
                share[pl.ds(first, count), pl.ds(b * padded, size)] = value.astype(bf16)
            if i + 2 < len(stages):
                self.load(kind, stages[i + 2]).start()

    def first(self, u):
        if u < self.kinds:
            self.cast(u)
            pl.when(self.core == 0)(self.given(u).start)
        if 2 <= u < self.kinds + 2:
            pl.when(self.core == 1)(self.given(u + 2).start)

        def send_from(source):
            self.to_dp(u, 1, source[u % self.kinds]).start()
            self.to_dp(u, 0, source[u % self.kinds]).start()
            self.kept(u, source).start()

        @pl.when(self.core == u // self.kinds)
        def own():
            send_from(self.shares)

        @pl.when(self.core != u // self.kinds)
        def other():
            self.given(u).wait_recv()
            send_from(self.got)

    def second(self, u):
        self.to_dp(u, 1).wait_recv()
        self.to_dp(u, 2).start()
        self.to_pair(u, 1).start()
        self.to_dp(u, 0).wait_recv()
        self.to_pair(u, 0).start()

    def third(self, u):
        self.to_dp(u, 2).wait_recv()
        self.to_pair(u, 2).start()
        for k in (1, 0):
            self.to_pair(u, k).wait_recv()
            self.to_core(u, k).start()

    def fourth(self, u):
        self.to_pair(u, 2).wait_recv()
        self.to_core(u, 2).start()

    def last(self, u):
        for k in range(3):
            self.to_core(u, k).wait()
            self.to_pair(u, k).wait_send()
        self.to_dp(u, 0, self.shares[u % self.kinds]).wait_send()
        self.to_dp(u, 1, self.shares[u % self.kinds]).wait_send()
        self.to_dp(u, 2).wait_send()
        self.kept(u, self.shares).wait()

        @pl.when(self.core == u // self.kinds)
        def gave():
            self.given(u).wait_send()

    def turns(self):
        steps = (self.first, self.second, self.third, self.fourth, self.last)
        units = 2 * self.kinds

        def turn(number):
            for lag, step in enumerate(steps):
                if 0 <= number - lag < units:
                    step(number - lag)

        return [functools.partial(turn, number) for number in range(units + len(steps) - 1)]


def gather_kernel(gather, *refs):
    kinds = gather.kinds
    gather.bind(refs[:kinds], refs[kinds:3 * kinds], refs[3 * kinds:])
    gather.open()
    greet(*gather.peers())
    for turn in gather.turns():
        turn()


def gather_weights(masters, parts, ranks):
    kinds = len(masters)
    gather = Gather(masters, parts, (3,) * (2 * kinds))
    results = pl.pallas_call(
        functools.partial(gather_kernel, gather),
        out_shape=gather.out_shapes(ranks),
        in_specs=any_specs(kinds),
        out_specs=tuple(any_specs(2 * kinds)),
        scratch_shapes=gather.scratch(),
        compiler_params=pltpu.CompilerParams(
            collective_id=1, has_side_effects=True, vmem_limit_bytes=VMEM_LIMIT
        ),
        cost_estimate=pl.CostEstimate(flops=0, bytes_accessed=700_000_000, transcendentals=0),
        name="gather_weights",
    )(*masters)
    return results[:kinds], results[kinds:]


def norm_parts(values):
    center = values - jnp.mean(values, axis=-1, keepdims=True)
    inverse = lax.rsqrt(jnp.mean(center * center, axis=-1, keepdims=True) + EPS)
    return center * inverse, inverse


def norm_back(values, gain, upstream):
    unit, inverse = norm_parts(values)
    weighted = upstream * gain
    grad = inverse * (
        weighted
        - jnp.mean(weighted, axis=-1, keepdims=True)
        - unit * jnp.mean(weighted * unit, axis=-1, keepdims=True)
    )
    return grad, jnp.sum(upstream * unit, axis=0, keepdims=True), jnp.sum(upstream, axis=0, keepdims=True)


def block_loads(source, target, sems, row):
    return [
        pltpu.make_async_copy(source.at[b], target.at[b], sems.at[row, b]) for b in range(source.shape[0])
    ]


def split_columns(target, value):
    ranks, _, padded = target.shape
    share = value.shape[1] // ranks
    target[...] = jnp.zeros(target.shape, target.dtype)
    for b in range(ranks):
        target[b, :, pl.ds(0, share)] = value[:, b * share:(b + 1) * share]


def join_columns(target, parts):
    share = target.shape[1] // len(parts)
    for b, part in enumerate(parts):
        target[:, b * share:(b + 1) * share] = part[:, :share]


def qkv_kernel(h_ref, norm_ref, w_ref, a_ref, q_ref, kv_ref, w_mem, sems):
    ranks = w_ref.shape[0]
    loads = block_loads(w_ref, w_mem, sems, 0)
    load_all(loads)
    unit, _ = norm_parts(h_ref[...].astype(f32))
    split_columns(a_ref, (unit * norm_ref[0:1] + norm_ref[2:3]).astype(bf16))
    block = q_ref.shape[1]
    for copy in loads:
        copy.wait()
    for part, target in enumerate((q_ref, kv_ref.at[0], kv_ref.at[1])):
        total = sum_of([dot_nn(a_ref[b], w_mem[b, :, pl.ds(part * block, block)]) for b in range(ranks)])
        target[...] = total.astype(bf16)


def project_qkv(hidden, norm, weight):
    tokens = hidden.shape[0]
    ranks, rows, columns = weight.shape
    return pl.pallas_call(
        qkv_kernel,
        out_shape=(
            jax.ShapeDtypeStruct((ranks, tokens, rows), bf16),
            jax.ShapeDtypeStruct((tokens, columns // 3), bf16),
            jax.ShapeDtypeStruct((2, tokens, columns // 3), bf16),
        ),
        in_specs=vmem_specs(2) + any_specs(1),
        out_specs=tuple(vmem_specs(3)),
        scratch_shapes=[pltpu.VMEM(weight.shape, bf16), pltpu.SemaphoreType.DMA((1, ranks))],
        compiler_params=pltpu.CompilerParams(vmem_limit_bytes=VMEM_LIMIT),
        cost_estimate=pl.CostEstimate(
            flops=2 * tokens * weight.size, bytes_accessed=2 * weight.size, transcendentals=tokens
        ),
        name="project_qkv",
    )(hidden, norm, weight)


def mlp_kernel(
    o_ref, h_ref, norm_ref, wo_ref, wf_ref, wp_ref,
    ob_ref, r_ref, c_ref, slope_ref, g_ref, out_ref,
    wo, wf, wp, sems,
):
    ranks = wo.shape[0]
    loads = [block_loads(s, t, sems, i) for i, (s, t) in enumerate(((wo_ref, wo), (wf_ref, wf), (wp_ref, wp)))]
    for some in loads:
        load_all(some)
    split_columns(ob_ref, o_ref[:, pl.ds(0, h_ref.shape[1])])
    for copy in loads[0]:
        copy.wait()
    r_ref[...] = h_ref[...].astype(f32) + sum_of([dot_nn(ob_ref[b], wo[b]) for b in range(ranks)])
    unit, _ = norm_parts(r_ref[...])
    split_columns(c_ref, (unit * norm_ref[1:2] + norm_ref[3:4]).astype(bf16))
    for copy in loads[1]:
        copy.wait()
    block = g_ref.shape[2]
    step = block // 3

    def columns(i, carry):
        at = pl.multiple_of(i * step, LANES)
        pre = sum_of([dot_nn(c_ref[b], wf[b, :, pl.ds(at, step)]) for b in range(ranks)])
        within = pl.ds(pl.multiple_of(lax.rem(i, 3) * step, LANES), step)
        g_ref[i // 3, :, within], slope_ref[i // 3, :, within] = gelu_parts(pre)
        return carry

    lax.fori_loop(0, 3 * ranks, columns, 0)
    for copy in loads[2]:
        copy.wait()
    out_ref[...] = (r_ref[...] + sum_of([dot_nn(g_ref[b], wp[b]) for b in range(ranks)])).astype(bf16)


def out_and_mlp(attended, hidden, norm, w_out, w_fc, w_proj):
    tokens, width = hidden.shape
    ranks, rows, _ = w_out.shape
    ff = w_proj.shape[1]
    flat = jax.ShapeDtypeStruct((ranks, tokens, rows), bf16)
    size = w_out.size + w_fc.size + w_proj.size
    return pl.pallas_call(
        mlp_kernel,
        out_shape=(
            flat,
            jax.ShapeDtypeStruct((tokens, width), f32),
            flat,
            jax.ShapeDtypeStruct((ranks, tokens, ff), f32),
            jax.ShapeDtypeStruct((ranks, tokens, ff), bf16),
            jax.ShapeDtypeStruct((tokens, width), bf16),
        ),
        in_specs=vmem_specs(3) + any_specs(3),
        out_specs=tuple(vmem_specs(6)),
        scratch_shapes=[
            pltpu.VMEM(w_out.shape, bf16),
            pltpu.VMEM(w_fc.shape, bf16),
            pltpu.VMEM(w_proj.shape, bf16),
            pltpu.SemaphoreType.DMA((3, ranks)),
        ],
        compiler_params=pltpu.CompilerParams(vmem_limit_bytes=VMEM_LIMIT),
        cost_estimate=pl.CostEstimate(
            flops=2 * tokens * size, bytes_accessed=2 * size, transcendentals=2 * tokens * ff * ranks
        ),
        name="out_and_mlp",
    )(attended, hidden, norm, w_out, w_fc, w_proj)


def gelu_parts(pre):
    below = 0.5 * (1.0 + lax.erf(pre * math.sqrt(0.5)))
    slope = below + pre * (jnp.exp(-0.5 * pre * pre) * (1.0 / math.sqrt(2.0 * math.pi)))
    return (pre * below).astype(bf16), slope


FORWARD_ORDER = (
    "f0", "f1", "s0", "f2", "t0", "s1", "40", "s2", "f3", "l0", "Q0", "f4", "S0", "t1", "A00", "f5", "s3",
    "s4", "f6", "A01", "t2", "A02", "41", "s5", "f7", "A03", "t3", "43", "l1", "O", "s6", "42", "l2", "l3",
    "W", "M", "B0", "t4", "B1", "B2", "44", "t5", "s7", "B3", "l4", "t6", "45", "Q1", "t7", "S1", "46", "47",
    "l6", "l5", "A10", "l7", "A11", "A12", "A13",
)
FORWARD_OVER_SEQ = (3, 2, 3, 2, 3, 2, 2, 2)


def forward_kernel(gather, place, in_ref, cot_in, norm_ref, *refs):
    kinds = gather.kinds
    masters, refs = refs[:kinds], refs[kinds:]
    whole, refs = refs[:2 * kinds], refs[2 * kinds:]
    (a_ref, q_ref, kv_ref, *others), refs = refs[:6], refs[6:]
    (lse_ref, ob_ref, r_ref, c_ref, slope_ref, g_ref, out_ref), refs = refs[:7], refs[7:]
    (h_ref, cot_ref, next_a, next_q, next_kv, *next_others), refs = refs[:8], refs[8:]
    (next_lse, next_o), refs = refs[:2], refs[2:]
    (rows_send, rows_recv, bias, links_send, links_recv, next_send, next_recv, total, columns_mem, rows_mem, wo, slopes, gs), refs = refs[:13], refs[13:]
    (columns_sem, rows_sem, wo_sem, out_sem), refs = refs[:4], refs[4:]
    gather.bind(masters, whole, refs)
    gather.open()
    core = lax.axis_index("section")
    z = lax.axis_index("seq")
    group = z // 2
    swapped = z + 2 - 4 * group
    greet(*gather.peers(), {"seq": swapped})
    moves = ((in_ref, h_ref), (cot_in, cot_ref))

    def stay(i):
        return pltpu.make_async_copy(moves[i][0].at[group], moves[i][1], rows_send.at[i])

    def move(i):
        return remote_copy(moves[i][0].at[1 - group], moves[i][1], rows_send.at[i], rows_recv.at[i], seq=swapped)

    def rows_arrive(i):
        pl.when(core == 0)(stay(i).wait)
        pl.when(core == 1)(move(i).wait)

    for i in range(2):
        pl.when(core == 0)(stay(i).start)
        pl.when(core == 1)(move(i).start)
    ranks, tokens, rows = a_ref.shape
    block = q_ref.shape[1]

    def load_columns(weight, part):
        slot = part % 2
        return [
            pltpu.make_async_copy(
                weight.at[b, :, pl.ds(part * block, block)], columns_mem.at[slot, b], columns_sem.at[slot, b]
            )
            for b in range(ranks)
        ]

    def load_rows(weight, b):
        return [pltpu.make_async_copy(weight.at[b], rows_mem.at[b % 2], rows_sem.at[b % 2])]

    def wait_all(copies):
        for copy in copies:
            copy.wait()

    def project(hidden, norms, weight, a, q, kv):
        for part in range(2):
            load_all(load_columns(weight, part))
        unit, _ = norm_parts(hidden)
        split_columns(a, (unit * norms[0:1] + norms[2:3]).astype(bf16))
        for part, target in enumerate((q, kv.at[0], kv.at[1])):
            wait_all(load_columns(weight, part))
            target[...] = sum_of([dot_nn(a[b], columns_mem[part % 2, b]) for b in range(ranks)]).astype(bf16)
            if part == 0:
                load_all(load_columns(weight, 2))

    def put_out(b):
        slot = b % 2
        return [
            pltpu.make_async_copy(slopes.at[slot], slope_ref.at[b], out_sem.at[slot, 0]),
            pltpu.make_async_copy(gs.at[slot], g_ref.at[b], out_sem.at[slot, 1]),
        ]

    def mlp_block(b):
        slot = b % 2
        if b >= 2:
            wait_all(put_out(b - 2))
        wait_all(load_columns(whole[2], b))
        third = block // 3

        def some_columns(i, carry):
            at = pl.ds(pl.multiple_of(i * third, LANES), third)
            pre = sum_of([dot_nn(c_ref[k], columns_mem[slot, k, :, at]) for k in range(ranks)])
            gs[slot, :, at], slopes[slot, :, at] = gelu_parts(pre)
            return carry

        lax.fori_loop(0, 3, some_columns, 0)
        load_all(put_out(b))
        if b + 2 < ranks:
            load_all(load_columns(whole[2], b + 2))
        wait_all(load_rows(whole[3], b))
        total[...] = total[...] + dot_nn(gs[slot], rows_mem[slot])
        if b + 2 < ranks:
            load_all(load_rows(whole[3], b + 2))

    def attention(layer):
        if layer == 0:
            return attention_steps(
                place, q_ref, [kv_ref] + others, next_o, lse_ref, bias, (links_send, links_recv)
            )
        return attention_steps(
            place, next_q, [next_kv] + next_others, next_o, next_lse, bias, (next_send, next_recv)
        )

    out_loads = [pltpu.make_async_copy(whole[1].at[b], wo.at[b], wo_sem.at[b]) for b in range(ranks)]

    def middle():
        split_columns(ob_ref, next_o[:, pl.ds(0, h_ref.shape[1])])
        wait_all(out_loads)
        r_ref[...] = h_ref[...].astype(f32) + sum_of([dot_nn(ob_ref[b], wo[b]) for b in range(ranks)])
        unit, _ = norm_parts(r_ref[...])
        split_columns(c_ref, (unit * norm_ref[0, 1:2] + norm_ref[0, 3:4]).astype(bf16))
        total[...] = r_ref[...]

    def qkv(layer):
        if layer == 0:
            rows_arrive(0)
            project(h_ref[...].astype(f32), norm_ref.at[0], whole[0], a_ref, q_ref, kv_ref)
            return
        for b in range(2, ranks):
            wait_all(put_out(b))
        out_ref[...] = total[...].astype(bf16)
        project(out_ref[...].astype(f32), norm_ref.at[1], whole[kinds], next_a, next_q, next_kv)

    steps = {"f": gather.first, "s": gather.second, "t": gather.third, "4": gather.fourth, "l": gather.last}
    steps.update({"Q": qkv, "S": lambda layer: attention(layer)[0](), "B": mlp_block})
    for step in FORWARD_ORDER:
        if step == "M":
            middle()
        elif step == "O":
            load_all(out_loads)
        elif step == "W":
            for b in range(2):
                load_all(load_columns(whole[2], b))
                load_all(load_rows(whole[3], b))
        elif step[0] == "A":
            attention(int(step[1]))[1](int(step[2]))
        else:
            steps[step[0]](int(step[1]))
    for layer in range(2):
        attention(layer)[2]()
    rows_arrive(1)


def gather_and_forward(place, rows_in, rows_cot, norms, masters, parts, ranks):
    _, tokens, width = rows_in.shape
    kinds = len(masters)
    gather = Gather(masters, parts, FORWARD_OVER_SEQ)
    shapes = gather.shapes
    rows, block = shapes[1][0], shapes[0][1] // 3
    ff = shapes[3][0]

    def array(dtype, *shape):
        return jax.ShapeDtypeStruct(shape, dtype)

    flat, two = array(bf16, ranks, tokens, rows), array(bf16, 2, tokens, block)
    one = array(bf16, tokens, block)
    saved = (flat, one, two, two, two, two, array(f32, tokens, LANES), flat, array(f32, tokens, width), flat)
    wide = (array(f32, ranks, tokens, ff), array(bf16, ranks, tokens, ff))
    hidden = array(bf16, tokens, width)
    after = (hidden, hidden, hidden, flat, one, two, two, two, two, array(f32, tokens, LANES), one)
    dma = pltpu.SemaphoreType.DMA
    links = dma((len(HEAD_GROUPS), 3))
    out = pl.pallas_call(
        functools.partial(forward_kernel, gather),
        out_shape=gather.out_shapes(ranks) + saved + wide + after,
        in_specs=[pl.BlockSpec(memory_space=pltpu.SMEM)] + any_specs(2) + vmem_specs(1) + any_specs(kinds),
        out_specs=tuple(
            any_specs(2 * kinds)
            + vmem_specs(len(saved))
            + any_specs(2)
            + vmem_specs(2)
            + any_specs(1)
            + vmem_specs(len(after) - 3)
        ),
        scratch_shapes=[
            dma((2,)),
            dma((2,)),
            pltpu.VMEM((LINKED, tokens, tokens), f32),
            links,
            links,
            links,
            links,
            pltpu.VMEM((tokens, width), f32),
            pltpu.VMEM((2, ranks, rows, block), bf16),
            pltpu.VMEM((2, ff, width), bf16),
            pltpu.VMEM((ranks, rows, width), bf16),
            pltpu.VMEM((2, tokens, ff), f32),
            pltpu.VMEM((2, tokens, ff), bf16),
            dma((2, ranks)),
            dma((2,)),
            dma((ranks,)),
            dma((2, 2)),
        ]
        + gather.scratch(),
        compiler_params=pltpu.CompilerParams(
            collective_id=1, has_side_effects=True, vmem_limit_bytes=VMEM_LIMIT
        ),
        cost_estimate=pl.CostEstimate(flops=0, bytes_accessed=700_000_000, transcendentals=0),
        name="gather_and_forward",
    )(place, rows_in, rows_cot, norms, *masters)
    weights, out = (out[:kinds], out[kinds:2 * kinds]), out[2 * kinds:]
    normed, query, own, along, beside, both, lse, attended, residual, second, slope, activated, *out = out
    result, hidden, cotangent, *out = out
    saved = (hidden, normed, query, [own, along, beside, both], attended, lse, residual, second, slope, activated)
    normed, query, own, along, beside, both, lse, attended = out
    return weights, cotangent, saved, result, (normed, query, [own, along, beside, both], lse, attended)


class Writer:
    def __init__(self, slots, sems):
        self.slots, self.sems, self.last = slots, sems, [(), ()]
        self.turn = 0

    def put(self, make, keep, give):
        slot = self.turn % 2
        self.turn += 1
        for copy in self.last[slot]:
            copy.wait()
        make(self.slots.at[slot])
        core = lax.axis_index("section")
        half = self.slots.shape[1] // 2
        copies = []
        for i, (target, which) in enumerate(((keep, core), (give, 1 - core))):
            part = self.slots.at[slot, pl.ds(pl.multiple_of(which * half, 16), half)]
            copies.append(pltpu.make_async_copy(part, target, self.sems.at[slot, i]))
        load_all(copies)
        self.last[slot] = copies

    def finish(self):
        for copies in self.last:
            for copy in copies:
                copy.wait()


def all_rows(value, weight):
    ranks, rows, columns = weight.shape
    product = dot_nt(value, weight[...].reshape(ranks * rows, columns))
    return [product[:, b * rows:(b + 1) * rows] for b in range(ranks)]


def product_into(stage, left, right, step):
    columns = right.shape[1]
    for a in range(0, columns, step):
        n = min(step, columns - a)
        stage[:, pl.ds(a, n)] = dot_tn(left[...], right[:, pl.ds(a, n)]).astype(bf16)


def mlp_back_kernel(
    e_ref, slope_ref, g_ref, c_ref, ob_ref, r_ref, norm_ref, wo_ref, wf_ref, wp_ref,
    res_ref, att_ref, vec_ref, p_keep, p_give, f_keep, f_give, o_keep, o_give,
    wo, wf, wp, slopes, gs, block_sems, pre, d_sec, branch, att_mem, p_slots, f_slots, o_slots, sems, p_sems, f_sems, o_sems,
):
    ranks = wo.shape[0]
    loads = [block_loads(s, t, sems, i) for i, (s, t) in enumerate(((wp_ref, wp), (wf_ref, wf), (wo_ref, wo)))]
    others = [block_loads(s, t, block_sems, i) for i, (s, t) in enumerate(((slope_ref, slopes), (g_ref, gs)))]
    for b in range(ranks):
        load_all([loads[0][b], others[0][b], others[1][b]])
    for some in loads[1:]:
        load_all(some)
    writer = Writer(p_slots, p_sems)
    rows, ff = c_ref.shape[2], g_ref.shape[2]
    width = e_ref.shape[1]
    for b in range(ranks):
        loads[0][b].wait()
        others[0][b].wait()
        others[1][b].wait()
        pre[:, pl.ds(b * ff, ff)] = (dot_nt(e_ref[...], wp[b]) * slopes[b]).astype(bf16)
        writer.put(
            lambda s, b=b: product_into(s, gs.at[b], e_ref, width), p_keep.at[b], p_give.at[b]
        )
    for b in range(ranks):
        loads[1][b].wait()
    join_columns(d_sec, all_rows(pre[...], wf))
    grad, gain, bias = norm_back(r_ref[...], norm_ref[1:2], d_sec[...])
    vec_ref[0:1] = gain
    vec_ref[1:2] = bias
    total = e_ref[...].astype(f32) + grad
    res_ref[...] = total
    branch[...] = total.astype(bf16)
    for b in range(ranks):
        loads[2][b].wait()
    join_columns(att_mem, all_rows(branch[...], wo))
    att_ref[...] = jnp.zeros(att_ref.shape, bf16)
    att_ref[:, pl.ds(0, width)] = att_mem[...].astype(bf16)
    f_writer = Writer(f_slots, f_sems)
    o_writer = Writer(o_slots, o_sems)
    for b in range(ranks):
        f_writer.put(
            lambda s, b=b: product_into(s, c_ref.at[b], pre, ff), f_keep.at[b], f_give.at[b]
        )
        o_writer.put(
            lambda s, b=b: product_into(s, ob_ref.at[b], branch, width), o_keep.at[b], o_give.at[b]
        )
    writer.finish()
    f_writer.finish()
    o_writer.finish()


def half_rows(weight):
    return jax.ShapeDtypeStruct((weight.shape[0], weight.shape[1] // 2, weight.shape[2]), bf16)


def mlp_back(upstream, slope, activated, second, attended, residual, norm, w_out, w_fc, w_proj):
    tokens, width = upstream.shape
    ranks, rows, _ = w_out.shape
    size = w_out.size + w_fc.size + w_proj.size
    return pl.pallas_call(
        mlp_back_kernel,
        out_shape=(
            jax.ShapeDtypeStruct((tokens, width), f32),
            jax.ShapeDtypeStruct((tokens, round_up(width, LANES)), bf16),
            jax.ShapeDtypeStruct((2, width), f32),
        )
        + tuple(half_rows(w) for w in (w_proj, w_proj, w_fc, w_fc, w_out, w_out)),
        in_specs=vmem_specs(1) + any_specs(2) + vmem_specs(4) + any_specs(3),
        out_specs=tuple(vmem_specs(3) + any_specs(6)),
        scratch_shapes=[
            pltpu.VMEM(w_out.shape, bf16),
            pltpu.VMEM(w_fc.shape, bf16),
            pltpu.VMEM(w_proj.shape, bf16),
            pltpu.VMEM(slope.shape, f32),
            pltpu.VMEM(activated.shape, bf16),
            pltpu.SemaphoreType.DMA((2, ranks)),
            pltpu.VMEM((tokens, w_fc.shape[2]), bf16),
            pltpu.VMEM((tokens, width), f32),
            pltpu.VMEM((tokens, width), bf16),
            pltpu.VMEM((tokens, width), f32),
            pltpu.VMEM((2,) + w_proj.shape[1:], bf16),
            pltpu.VMEM((2,) + w_fc.shape[1:], bf16),
            pltpu.VMEM((2,) + w_out.shape[1:], bf16),
            pltpu.SemaphoreType.DMA((3, ranks)),
            pltpu.SemaphoreType.DMA((2, 2)),
            pltpu.SemaphoreType.DMA((2, 2)),
            pltpu.SemaphoreType.DMA((2, 2)),
        ],
        compiler_params=pltpu.CompilerParams(vmem_limit_bytes=VMEM_LIMIT),
        cost_estimate=pl.CostEstimate(
            flops=4 * tokens * size, bytes_accessed=4 * size, transcendentals=tokens
        ),
        name="mlp_backward",
    )(upstream, slope, activated, second, attended, residual, norm, w_out, w_fc, w_proj)


def qkv_back_kernel(
    dq_ref, dkv_ref, a_ref, h_ref, res_ref, norm_ref, w_ref,
    sent_ref, vec_ref, keep, give,
    w_mem, d_proj, d_normed, slots, sems, out_sems,
):
    ranks, rows, columns = w_ref.shape
    loads = block_loads(w_ref, w_mem, sems, 0)
    load_all(loads)
    writer = Writer(slots, out_sems)
    block = columns // 3
    d_proj[:, pl.ds(0, block)] = dq_ref[...]
    d_proj[:, pl.ds(block, block)] = dkv_ref[0]
    d_proj[:, pl.ds(2 * block, block)] = dkv_ref[1]
    for b in range(ranks):
        writer.put(
            lambda s, b=b: product_into(s, a_ref.at[b], d_proj, block), keep.at[b], give.at[b]
        )
    for copy in loads:
        copy.wait()
    join_columns(d_normed, all_rows(d_proj[...], w_mem))
    grad, gain, bias = norm_back(h_ref[...].astype(f32), norm_ref[0:1], d_normed[...])
    vec_ref[0:1] = gain
    vec_ref[1:2] = bias
    sent_ref[...] = (res_ref[...] + grad).astype(bf16)
    writer.finish()


def qkv_back(d_query, d_pair, normed, hidden, residual_grad, norm, weight):
    tokens, width = hidden.shape
    ranks, rows, columns = weight.shape
    return pl.pallas_call(
        qkv_back_kernel,
        out_shape=(
            jax.ShapeDtypeStruct((tokens, width), bf16),
            jax.ShapeDtypeStruct((2, width), f32),
            half_rows(weight),
            half_rows(weight),
        ),
        in_specs=vmem_specs(6) + any_specs(1),
        out_specs=tuple(vmem_specs(2) + any_specs(2)),
        scratch_shapes=[
            pltpu.VMEM(weight.shape, bf16),
            pltpu.VMEM((tokens, columns), bf16),
            pltpu.VMEM((tokens, width), f32),
            pltpu.VMEM((2, rows, columns), bf16),
            pltpu.SemaphoreType.DMA((1, ranks)),
            pltpu.SemaphoreType.DMA((2, 2)),
        ],
        compiler_params=pltpu.CompilerParams(vmem_limit_bytes=VMEM_LIMIT),
        cost_estimate=pl.CostEstimate(
            flops=4 * tokens * weight.size, bytes_accessed=4 * weight.size, transcendentals=tokens
        ),
        name="qkv_backward",
    )(d_query, d_pair, normed, hidden, residual_grad, norm, weight)


def swap_cores(value):
    return lax.ppermute(value, "section", [(0, 1), (1, 0)])


def send_joint(value, axis, route):
    size = lax.axis_size(axis)
    pairs = []
    for core in range(2):
        for index in range(size):
            to = route(core, index)
            if to is not None:
                pairs.append((core * size + index, to[0] * size + to[1]))
    return lax.ppermute(value, ("section", axis), pairs)


def on_device(
    layer_in, cotangent, lengths, block_order, w_qkv, w_out, w_fc, w_proj, norm_gains, norm_biases
):
    tokens, width = layer_in.shape[2:]
    blocks = lax.axis_size("seq")
    ranks = lax.axis_size("dp")
    half = blocks // 2
    core = lax.axis_index("section")
    place_dp = lax.axis_index("dp")
    place_seq = lax.axis_index("seq")
    first_core = core == 0
    group = place_seq // half
    linked = blocks == LINKED and ranks == LINKED

    def per_core(left, right):
        return jnp.where(first_core, left, right)

    def after(value, *others):
        return lax.optimization_barrier((value, others))[0]

    def own_rows(value):
        value = value[:, 0]
        mine = lax.dynamic_index_in_dim(value, group, 0, False)
        other = lax.dynamic_index_in_dim(value, 1 - group, 0, False)
        moved = send_joint(other, "seq", lambda c, z: (1, z ^ half) if c == 1 else None)
        return per_core(mine, moved)

    def back_home(first, second):
        crossed = send_joint(
            per_core(second, first), "seq", lambda c, z: (1, z) if c == 0 else (0, z ^ half)
        )
        along = send_joint(second, "seq", lambda c, z: (1, z ^ half) if c == 1 else None)
        mine = per_core(first, crossed)
        other = per_core(crossed, along)
        return jnp.where(group == 0, jnp.stack([mine, other]), jnp.stack([other, mine]))

    steps = []
    bit = 1
    while bit < half:
        steps.append(bit)
        bit *= 2
    my_block = per_core(place_seq, place_seq ^ half)
    block_ids = [my_block]
    for bit in steps:
        block_ids = block_ids + [b ^ bit for b in block_ids]
    block_ids = block_ids + [b ^ half for b in block_ids]
    limit = lax.dynamic_index_in_dim(lengths[:, 0], group, 0, False)
    starts = block_order[jnp.stack(block_ids)] * tokens
    place = jnp.concatenate([limit[None], starts]).astype(jnp.int32)

    def gather_keys(own):
        parts = [own]
        for bit in steps:
            route = [(z, z ^ bit) for z in range(blocks)]
            parts = parts + [lax.ppermute(p, "seq", route) for p in parts]
        return parts + [swap_cores(p) for p in parts]

    def scatter_keys(parts):
        cut = len(parts) // 2
        moved = [swap_cores(p) for p in parts[cut:]]
        parts = [(p.astype(f32) + m.astype(f32)).astype(bf16) for p, m in zip(parts[:cut], moved)]
        for bit in reversed(steps):
            cut = len(parts) // 2
            route = [(z, z ^ bit) for z in range(blocks)]
            moved = [lax.ppermute(p, "seq", route) for p in parts[cut:]]
            parts = [(p.astype(f32) + m.astype(f32)).astype(bf16) for p, m in zip(parts[:cut], moved)]
        return parts[0]

    masters = (w_qkv[0], w_out[0], w_fc[0], w_proj[0])
    parts = (3, 1, ranks, 0)
    own_norms = jnp.concatenate([norm_gains[0], norm_biases[0]])
    other_norms = swap_cores(own_norms)
    norms = [per_core(own_norms, other_norms), per_core(other_norms, own_norms)]

    def attend(projected):
        normed, query, own_keys = projected
        keys = gather_keys(own_keys)
        attended, lse, keys = attention_forward(place, query, keys, blocks)
        return normed, query, keys, lse, attended

    def forward(hidden, layer, attention):
        _, wout, wfc, wproj = weights[layer]
        normed, query, keys, lse, attended = attention
        attended, residual, second, slope, activated, result = out_and_mlp(
            attended, hidden, norms[layer], wout, wfc, wproj
        )
        return result, (hidden, normed, query, keys, attended, lse, residual, second, slope, activated)

    if linked:
        weights, rows_cot, saved_first, first_out, attention = gather_and_forward(
            place, layer_in[:, 0], cotangent[:, 0], jnp.stack(norms), masters, parts, ranks
        )
    else:
        rows_in, rows_cot = own_rows(layer_in), own_rows(cotangent)
        weights = gather_weights(masters, parts, ranks)
        first_out, saved_first = forward(rows_in, 0, attend(project_qkv(rows_in, norms[0], weights[0][0])))
        attention = attend(project_qkv(first_out, norms[1], weights[1][0]))
    second_out, saved_second = forward(first_out, 1, attention)

    def backward(upstream, saved, layer, layers, rows):
        wqkv, wout, wfc, wproj = weights[layer]
        hidden, normed, query, keys, attended, lse, residual, second, slope, activated = saved
        d_residual, d_att, vectors_two, *mlp_grads = mlp_back(
            upstream, slope, activated, second, attended, residual, norms[layer], wout, wfc, wproj
        )
        kept, given = mlp_grads[0::2], mlp_grads[1::2]
        if linked:
            d_query, d_keys, sums, home = attention_backward(
                place, query, d_att, lse.T, keys, kept, given, (6, 5, 3), layers, rows
            )
            d_pair = d_keys[0]
        else:
            d_query, d_keys, _, home = attention_backward(place, query, d_att, lse.T, keys)
            d_pair = scatter_keys(d_keys)
            sums = plain_sums(kept, given)
        sent, vectors_one, *qkv_grads = qkv_back(d_query, d_pair, normed, hidden, d_residual, norms[layer], wqkv)
        return sent, sums, home, qkv_grads, jnp.stack([vectors_one[0], vectors_two[0], vectors_one[1], vectors_two[1]])

    def plain_sums(kept, given):
        total = [(k.astype(f32) + swap_cores(g).astype(f32)).astype(k.dtype) for k, g in zip(kept, given)]
        return [lax.psum(lax.psum_scatter(t, "dp", scatter_dimension=0), "seq") for t in total]

    def by_rank(vectors):
        return vectors.reshape(4, ranks, -1).transpose(1, 0, 2)

    second_grad, second_sums, layer_results, second_qkv, second_vectors = backward(
        rows_cot, saved_second, 1, (0, 1), (first_out, second_out)
    )
    first_grad, first_sums, grad_home, first_qkv, first_vectors = backward(
        second_grad, saved_first, 0, (1,), (second_grad,)
    )
    kept = [second_qkv[0], by_rank(per_core(first_vectors, second_vectors)), first_qkv[0]]
    given = [second_qkv[1], by_rank(per_core(second_vectors, first_vectors)), first_qkv[1]]
    if linked:
        (second_last, vectors, first_last), first_home, other = reduce_last(
            kept, given, (5, 1, 5), (1, None, 0), first_grad, first_sums, second_sums
        )
        grad_results = per_core(first_home, grad_home)
    else:
        second_last, vectors, first_last = plain_sums(kept, given)
        layer_results = back_home(first_out, second_out)
        grad_results = back_home(first_grad, second_grad)
    first_sums = list(first_sums) + [first_last]
    second_sums = list(second_sums) + [second_last]
    if not linked:
        other = [swap_cores(per_core(b, a)) for a, b in zip(first_sums, second_sums)]
    shapes = [w_proj.shape[1:], w_fc.shape[1:], w_out.shape[1:], w_qkv.shape[1:]]
    g_proj, g_fc, g_out, g_qkv = finish(first_sums, second_sums, other, shapes, (1, ranks, 1, 3))
    return (
        layer_results[None, :, None],
        grad_results[None, :, None],
        g_qkv[None],
        g_out[None],
        g_fc[None],
        g_proj[None],
        vectors[:2][None],
        vectors[2:][None],
    )


def solution(mesh):
    return jax.shard_map(
        on_device,
        mesh=mesh,
        in_specs=(
            P(None, "dp", "seq", None),
            P(None, "dp", "seq", None),
            P(None, "dp"),
            P(),
            P("section", "dp", None),
            P("section", "dp", None),
            P("section", "dp", None),
            P("section", "dp", None),
            P("section", None, None),
            P("section", None, None),
        ),
        out_specs=(
            P("section", None, "dp", "seq", None),
            P("section", None, "dp", "seq", None),
            P("section", "dp", None),
            P("section", "dp", None),
            P("section", "dp", None),
            P("section", "dp", None),
            P("section", None, "dp"),
            P("section", None, "dp"),
        ),
        check_vma=False,
    )
```

```python
import functools
import math

import jax
import jax.numpy as jnp
from jax import lax
from jax.experimental import pallas as pl
from jax.experimental.pallas import tpu as pltpu
from jax.sharding import PartitionSpec as P

HEADS = 20
HEAD_DIM = 56
EPS = 1e-05
NEG = -1e30
LANES = 128
WINDOW = 256
VMEM_LIMIT = 58 * 1024 * 1024
MESH = pl.DeviceIdType.MESH

bf16 = jnp.bfloat16
f32 = jnp.float32


def round_up(size, grain):
    return -(-size // grain) * grain


def dot_nn(left, right):
    return lax.dot_general(left, right, (((1,), (0,)), ((), ())), preferred_element_type=f32)


def dot_nt(left, right):
    return lax.dot_general(left, right, (((1,), (1,)), ((), ())), preferred_element_type=f32)


def dot_tn(left, right):
    return lax.dot_general(left, right, (((0,), (0,)), ((), ())), preferred_element_type=f32)


LINKED = 4


def greet(*places):
    barrier = pltpu.get_barrier_semaphore()
    for place in places:
        pl.semaphore_signal(barrier, inc=1, device_id=place, device_id_type=MESH)
    pl.semaphore_wait(barrier, len(places))


def remote_copy(source, target, send, recv, **place):
    return pltpu.make_async_remote_copy(
        src_ref=source, dst_ref=target, send_sem=send, recv_sem=recv, device_id=place, device_id_type=MESH
    )


def pair_places():
    z = lax.axis_index("seq")
    return {"seq": z + 1 - 2 * lax.rem(z, 2)}, {"section": 1 - lax.axis_index("section")}


def partners():
    core = lax.axis_index("section")
    rank = lax.axis_index("dp")
    x, y = lax.rem(rank, 2), rank // 2
    near = lax.rem(y + core, 2) * 2 + lax.rem(x + 1 - core, 2)
    far = lax.rem(y + 1 - core, 2) * 2 + lax.rem(x + core, 2)
    return near, far, 3 - rank


def vmem_specs(count):
    return [pl.BlockSpec(memory_space=pltpu.VMEM)] * count


def any_specs(count):
    return [pl.BlockSpec(memory_space=pl.ANY)] * count


def sum_of(parts):
    return functools.reduce(jnp.add, parts)


def load_all(copies):
    for copy in copies:
        copy.start()


class Reduction:
    def __init__(self, arrays, parts):
        self.arrays = [(a.shape, a.dtype) for a in arrays]
        self.chunks = []
        for index, (shape, _) in enumerate(self.arrays):
            step = round_up(-(-shape[1] // parts[index]), 16)
            self.chunks += [(index, a, min(step, shape[1] - a)) for a in range(0, shape[1], step)]
        self.count = len(self.chunks)
        self.classes, self.places = {}, []
        for array, _, rows in self.chunks:
            (_, _, columns), dtype = self.arrays[array]
            key = (columns > 2048, str(dtype))
            most = self.classes.setdefault(key, [0, 0, 0, dtype])
            self.places.append((list(self.classes).index(key), most[0]))
            most[:3] = [most[0] + 1, max(most[1], rows), max(most[2], columns)]

    def out_shapes(self):
        return tuple(jax.ShapeDtypeStruct(shape[1:], dtype) for shape, dtype in self.arrays)

    def scratch(self):
        sizes = [((rows, self.arrays[a][0][2]), self.arrays[a][1]) for a, _, rows in self.chunks]
        many = [pltpu.VMEM((4,) + s, t) for s, t in sizes] + [pltpu.VMEM((2,) + s, t) for s, t in sizes]
        single = [pltpu.VMEM(s, t) for s, t in sizes] * 3
        slots = [pltpu.VMEM((4,) + tuple(c[1:3]), c[3]) for c in self.classes.values() for _ in range(2)]
        n = self.count
        dma = pltpu.SemaphoreType.DMA
        sems = [dma((n, 4)), dma((n, 4)), dma((n, 4)), dma((n, 3)), dma((n, 3)), dma((n, 3)), dma((n, 3))]
        return many + single + slots + sems + [pltpu.SemaphoreType.REGULAR((len(self.classes),))]

    def bind(self, kept, given, results, scratch):
        n, k = self.count, len(self.classes)
        self.kept, self.given, self.results = kept, given, results
        self.here, self.came, self.far_in, self.z_in, self.z_mid = (scratch[i * n:(i + 1) * n] for i in range(5))
        self.slots, rest = scratch[5 * n:5 * n + 2 * k], scratch[5 * n + 2 * k:]
        (self.load_sem, self.core_send, self.core_recv, self.dp_send, self.dp_recv, self.z_send, self.z_recv, self.free) = rest
        z = lax.axis_index("seq")
        self.rank = lax.axis_index("dp")
        self.near, self.far, self.across = partners()
        self.inner = (z == 1) | (z == 2)
        self.pair_z, self.other_z = z + 1 - 2 * lax.rem(z, 2), 3 - z
        self.other_core = {"section": 1 - lax.axis_index("section")}
        self.settled = lambda chunk: None

    def peers(self):
        return [{"dp": self.near}, {"dp": self.far}, {"seq": self.pair_z}, {"seq": self.other_z}, self.other_core]

    def loads(self, c):
        array, row, rows = self.chunks[c]
        return [
            pltpu.make_async_copy(
                self.kept[array].at[block, pl.ds(row, rows)], self.here[c].at[i], self.load_sem.at[c, i]
            )
            for i, block in enumerate((self.near, self.across, self.far, self.rank))
        ]

    def slot(self, c, index):
        array, _, rows = self.chunks[c]
        kind, at = self.places[c]
        return self.slots[2 * kind + at % 2].at[index, pl.ds(0, rows), pl.ds(0, self.arrays[array][0][2])]

    def to_core(self, c):
        array, row, rows = self.chunks[c]
        return [
            remote_copy(
                self.given[array].at[block, pl.ds(row, rows)],
                self.slot(c, i),
                self.core_send.at[c, i],
                self.core_recv.at[c, i],
                **self.other_core,
            )
            for i, block in enumerate((self.far, self.across, self.near, self.rank))
        ]

    def nears(self, c):
        return [
            remote_copy(self.here[c].at[i], self.came[c].at[i], self.dp_send.at[c, i], self.dp_recv.at[c, i], dp=self.near)
            for i in range(2)
        ]

    def fars(self, c):
        return remote_copy(self.here[c].at[2], self.far_in[c], self.dp_send.at[c, 2], self.dp_recv.at[c, 2], dp=self.far)

    def along(self, c, k):
        source = self.z_mid[c] if k == 2 else self.here[c].at[3]
        target = self.z_mid[c] if k == 1 else self.z_in[c]
        place = self.other_z if k == 1 else self.pair_z
        return remote_copy(source, target, self.z_send.at[c, k], self.z_recv.at[c, k], seq=place)

    def add(self, c, index, *others):
        here = self.here[c]
        total = here[index].astype(f32)
        for other in others:
            total = total + other[...].astype(f32)
        here[index] = total.astype(here.dtype)

    def store(self, c, value):
        array, row, rows = self.chunks[c]
        self.results[array][pl.ds(row, rows)] = value
        self.settled(c)

    def open(self):
        for c in range(self.count):
            load_all(self.loads(c))

    def give(self, c=0):
        kind, at = self.places[c]
        if at >= 2:
            pl.semaphore_wait(self.free.at[kind], 1)
        load_all(self.to_core(c))

    def begin(self, c):
        for copy in self.loads(c):
            copy.wait()
        for copy in self.to_core(c):
            copy.wait_recv()
        for i in range(2):
            self.add(c, i, self.slot(c, i))
        load_all(self.nears(c))
        for i in (2, 3):
            self.add(c, i, self.slot(c, i))
        kind, at = self.places[c]
        if (kind, at + 2) in self.places:
            pl.semaphore_signal(self.free.at[kind], inc=1, device_id=self.other_core, device_id_type=MESH)
        if c + 2 < self.count:
            self.give(c + 2)

    def after_near(self, c):
        for copy in self.nears(c):
            copy.wait()
        self.add(c, 2, self.came[c].at[1])
        self.fars(c).start()

    def after_far(self, c):
        self.fars(c).wait()
        self.add(c, 3, self.came[c].at[0], self.far_in[c])
        pl.when(jnp.logical_not(self.inner))(self.along(c, 0).start)

    def after_inward(self, c):
        pl.when(jnp.logical_not(self.inner))(self.along(c, 0).wait_send)

        @pl.when(self.inner)
        def add():
            self.along(c, 0).wait_recv()
            self.add(c, 3, self.z_in[c])
            self.along(c, 1).start()

    def after_middle(self, c):
        @pl.when(self.inner)
        def add():
            self.along(c, 1).wait()
            total = self.here[c][3].astype(f32) + self.z_mid[c][...].astype(f32)
            self.z_mid[c][...] = total.astype(self.z_mid[c].dtype)
            self.along(c, 2).start()
            self.store(c, self.z_mid[c][...])

    def after_outward(self, c):
        pl.when(self.inner)(self.along(c, 2).wait_send)

        @pl.when(jnp.logical_not(self.inner))
        def take():
            self.along(c, 2).wait_recv()
            self.store(c, self.z_in[c][...])

        for copy in self.to_core(c):
            copy.wait_send()

    def turns(self):
        steps = (self.begin, self.after_near, self.after_far, self.after_inward, self.after_middle, self.after_outward)

        def turn(number):
            for lag, step in enumerate(steps):
                if 0 <= number - lag < self.count:
                    step(number - lag)

        return [functools.partial(turn, number) for number in range(self.count + len(steps) - 1)]


class Homes:
    def __init__(self, items):
        self.items = items
        self.count = 1 + max(target for _, target in items)

    def out_shapes(self, rows):
        return (jax.ShapeDtypeStruct((2,) + rows.shape, rows.dtype),) * self.count

    def scratch(self):
        dma = pltpu.SemaphoreType.DMA
        n = len(self.items)
        return [dma((n, 2)), dma((n, 2)), dma((n,))]

    def bind(self, rows, homes, scratch):
        self.rows, self.homes = rows, homes
        self.send, self.recv, self.local = scratch
        z = lax.axis_index("seq")
        self.group = z // 2
        self.swapped = z + 2 - 4 * self.group
        self.first_core = lax.axis_index("section") == 0

    def peers(self):
        return [{"section": section, "seq": self.swapped} for section in range(2)]

    def target(self, i):
        return self.homes[self.items[i][1]].at[self.group]

    def stays(self, i):
        return pltpu.make_async_copy(self.rows[i], self.target(i), self.local.at[i])

    def beside(self, i):
        return remote_copy(self.rows[i], self.target(i), self.send.at[i, 0], self.recv.at[i, 0], section=1)

    def away(self, i):
        layer = self.items[i][0]
        return remote_copy(
            self.rows[i], self.target(i), self.send.at[i, 1], self.recv.at[i, 1], section=layer, seq=self.swapped
        )

    def start(self):
        @pl.when(self.first_core)
        def first():
            for i, (layer, _) in enumerate(self.items):
                (self.stays(i) if layer == 0 else self.beside(i)).start()

        @pl.when(jnp.logical_not(self.first_core))
        def second():
            for i in range(len(self.items)):
                self.away(i).start()

    def finish(self):
        @pl.when(self.first_core)
        def first():
            for i, (layer, _) in enumerate(self.items):
                if layer == 0:
                    self.stays(i).wait()
                    self.away(i).wait_recv()
                else:
                    self.beside(i).wait_send()

        @pl.when(jnp.logical_not(self.first_core))
        def second():
            for i, (layer, _) in enumerate(self.items):
                self.away(i).wait_send()
                if layer == 1:
                    self.beside(i).wait_recv()
                    self.away(i).wait_recv()


HEAD_GROUPS = ((0, 6), (6, 6), (12, 6), (18, 2))
LANES_IN = ((0, 384), (384, 384), (768, 256), (1024, 128))
BACKWARD_ORDER = (
    "p", "p", "t", "p", "s0", "p", "t", "p", "a0", "p", "t", "s1", "p", "a1", "p", "t", "p", "s2", "p", "a2",
    "s3", "t", "t", "a3", "t", "t", "t", "z",
)
LANES_OUT = ((0, 256), (256, 384), (640, 256), (896, 256))


def window_in(group, head):
    return head // 3 if group == 0 else (7 * head - 10) // 16


def window_out(group, head):
    return 7 if group == 3 else 7 * head // 16


def head_window(head, tile, rows):
    start = pl.multiple_of(tile * LANES, LANES)
    lane = lax.broadcasted_iota(jnp.int32, (rows, WINDOW), 1) + (start - head * HEAD_DIM)
    return pl.ds(start, WINDOW), (lane >= 0) & (lane < HEAD_DIM)


def two_heads(group, step, work):
    def pair(i, carry):
        work(group, 2 * i)
        work(group, 2 * i + 1)
        return carry

    lax.fori_loop(step, step + 1, pair, 0)


def heads_of(group, work):
    first, count = HEAD_GROUPS[group]

    def pair(step, carry):
        work(group, first + 2 * step)
        work(group, first + 2 * step + 1)
        return carry

    lax.fori_loop(0, count // 2, pair, 0)


def fill_bias(bias, place, row_axis):
    blocks, tokens, _ = bias.shape
    row = lax.broadcasted_iota(jnp.int32, (tokens, tokens), row_axis) + place[1]
    for b in range(blocks):
        column = lax.broadcasted_iota(jnp.int32, (tokens, tokens), 1 - row_axis) + place[1 + b]
        bias[b] = jnp.where((column <= row) & (column < place[0]), 0.0, NEG)


def attention_steps(place, q_ref, kv_refs, o_pad, lse_rows, lse_ref, bias, links):
    tokens, blocks = q_ref.shape[0], len(kv_refs)
    scale = HEAD_DIM ** -0.5
    groups = range(len(HEAD_GROUPS))

    def copies(group):
        send, recv = links
        along, beside = pair_places()
        lanes = (slice(None), slice(None), pl.ds(*LANES_IN[group]))

        def copy(k, source, target, place):
            return remote_copy(
                kv_refs[source].at[lanes], kv_refs[target].at[lanes], send.at[group, k], recv.at[group, k], **place
            )

        return copy(0, 0, 1, along), copy(1, 0, 2, beside), copy(2, 1, 3, beside)

    def start():
        if links:
            for group in groups:
                copies(group)[0].start()
                copies(group)[1].start()
        o_pad[...] = jnp.zeros(o_pad.shape, o_pad.dtype)
        fill_bias(bias, place, 0)
        lse_ref[...] = jnp.zeros(lse_ref.shape, f32)

    def one_head(group, head):
        lse_lane = lax.broadcasted_iota(jnp.int32, lse_ref.shape, 1)
        lanes, inside = head_window(head, window_in(group, head), tokens)
        query = jnp.where(inside, q_ref[:, lanes], 0).astype(bf16)
        scores = [dot_nt(query, kv_refs[b][0, :, lanes]) * scale + bias[b] for b in range(blocks)]
        peak = jnp.max(functools.reduce(jnp.maximum, scores), axis=1, keepdims=True)
        weights = [jnp.exp(s - peak) for s in scores]
        total = jnp.sum(functools.reduce(jnp.add, weights), axis=1, keepdims=True)
        share = 1.0 / total
        out = sum_of([dot_nn((w * share).astype(bf16), kv_refs[b][1, :, lanes]) for b, w in enumerate(weights)])
        o_pad[:, lanes] = jnp.where(inside, out, o_pad[:, lanes].astype(f32)).astype(bf16)
        lse_ref[...] = jnp.where(lse_lane == head, peak + jnp.log(total), lse_ref[...])

    def work(group):
        if links:
            first, second, third = copies(group)
            first.wait_recv()
            third.start()
            second.wait_recv()
            third.wait_recv()
        heads_of(group, one_head)

    def end():
        lse_rows[...] = jnp.transpose(lse_ref[...])
        if links:
            for group in groups:
                for copy in copies(group):
                    copy.wait_send()

    return start, work, end


def attention_forward_kernel(blocks, place, q_ref, *refs):
    o_ref, lse_rows, lse_ref, bias = refs[blocks:]
    start, work, end = attention_steps(place, q_ref, refs[:blocks], o_ref, lse_rows, lse_ref, bias, ())
    start()
    for group in range(len(HEAD_GROUPS)):
        work(group)
    end()


def attention_forward(place, query, kv_blocks, blocks):
    tokens, width = query.shape
    results = pl.pallas_call(
        functools.partial(attention_forward_kernel, blocks),
        out_shape=(
            jax.ShapeDtypeStruct((tokens, width), bf16),
            jax.ShapeDtypeStruct((LANES, tokens), f32),
        ),
        in_specs=[pl.BlockSpec(memory_space=pltpu.SMEM)] + vmem_specs(1 + len(kv_blocks)),
        out_specs=tuple(vmem_specs(2)),
        scratch_shapes=[pltpu.VMEM((tokens, LANES), f32), pltpu.VMEM((blocks, tokens, tokens), f32)],
        compiler_params=pltpu.CompilerParams(vmem_limit_bytes=VMEM_LIMIT),
        cost_estimate=pl.CostEstimate(
            flops=4 * HEADS * tokens * tokens * blocks * WINDOW,
            bytes_accessed=60_000_000,
            transcendentals=HEADS * tokens * tokens * blocks,
        ),
        name="attention_forward",
    )(place, query, *kv_blocks)
    return results[0], results[1], kv_blocks


def attention_backward_kernel(blocks, reduction, going, place, q_ref, d_ref, lse_ref, *refs):
    kv_refs, refs = refs[:blocks], refs[blocks:]
    turns = []
    linked = reduction is not None
    if linked:
        arrays = len(reduction.arrays)
        kept, given, refs = refs[:arrays], refs[arrays:2 * arrays], refs[2 * arrays:]
        rows, refs = refs[:len(going.items)], refs[len(going.items):]
        dq_ref, out_ref, refs = refs[0], refs[1], refs[2:]
        results, refs = refs[:arrays], refs[arrays:]
        homes, refs = refs[:going.count], refs[going.count:]
        dq_pad, bias, grads, from_core, from_pair, send, recv = refs[:7]
        going.bind(rows, homes, refs[7:10])
        reduction.bind(kept, given, results, refs[10:])
        along, beside = pair_places()
        reduction.open()
        greet(*reduction.peers(), *going.peers())
        reduction.give(0)
        reduction.give(1)
        going.start()
        turns = reduction.turns()
    else:
        dq_ref, refs = refs[0], refs[1:]
        out_refs, (dq_pad, bias, grads) = refs[:blocks], refs[blocks:]
    tokens = q_ref.shape[0]
    scale = HEAD_DIM ** -0.5
    dq_pad[...] = jnp.zeros(dq_pad.shape, dq_pad.dtype)
    for b in range(blocks):
        grads[b] = jnp.zeros(grads.shape[1:], grads.dtype)
    fill_bias(bias, place, 1)

    def one_head(group, head):
        lanes, inside = head_window(head, window_out(group, head), tokens)
        query = jnp.where(inside, q_ref[:, lanes], 0).astype(bf16)
        grad = jnp.where(inside, d_ref[:, lanes], 0).astype(bf16)
        lse = lse_ref[pl.ds(head, 1), :]
        probs = [
            jnp.exp(dot_nt(kv_refs[b][0, :, lanes], query) * scale + bias[b] - lse) for b in range(blocks)
        ]
        d_probs = [dot_nt(kv_refs[b][1, :, lanes], grad) for b in range(blocks)]
        inner = jnp.sum(sum_of([p * dp for p, dp in zip(probs, d_probs)]), axis=0, keepdims=True)
        d_query = None
        for b in range(blocks):
            d_score = (probs[b] * (d_probs[b] - inner) * scale).astype(bf16)
            grads[b, 0, :, lanes] = grads[b, 0, :, lanes] + dot_nn(d_score, query).astype(bf16)
            grads[b, 1, :, lanes] = grads[b, 1, :, lanes] + dot_nn(probs[b].astype(bf16), grad).astype(bf16)
            part = dot_tn(d_score, kv_refs[b][0, :, lanes])
            d_query = part if d_query is None else d_query + part
        dq_pad[:, lanes] = jnp.where(inside, d_query, dq_pad[:, lanes].astype(f32)).astype(bf16)

    def lanes_of(group):
        return (slice(None), slice(None), pl.ds(*LANES_OUT[group]))

    def to_core(group, k):
        lanes = lanes_of(group)
        return remote_copy(
            grads.at[2 + k].at[lanes], from_core.at[k].at[lanes], send.at[group, k], recv.at[group, k], **beside
        )

    def to_pair(group):
        lanes = lanes_of(group)
        return remote_copy(
            grads.at[1].at[lanes], from_pair.at[lanes], send.at[group, 2], recv.at[group, 2], **along
        )

    def add_core(group):
        lanes = lanes_of(group)
        for k in (1, 0):
            to_core(group, k).wait_recv()
            mine = grads.at[k]
            mine[lanes] = (mine[lanes].astype(f32) + from_core.at[k][lanes].astype(f32)).astype(bf16)
            if k == 1:
                to_pair(group).start()

    groups = range(len(HEAD_GROUPS))
    if not linked:
        for group in groups:
            heads_of(group, one_head)
        dq_ref[...] = dq_pad[...]
        for b in range(blocks):
            out_refs[b][...] = grads[b]
        return

    def last_add():
        for group in groups:
            lanes = lanes_of(group)
            to_pair(group).wait_recv()
            out_ref[lanes] = (grads.at[0][lanes].astype(f32) + from_pair[lanes].astype(f32)).astype(bf16)

    heads = [(group, (first + h) // 2) for group, (first, count) in enumerate(HEAD_GROUPS) for h in range(0, count, 2)]
    for step in BACKWARD_ORDER:
        if step == "p":
            two_heads(*heads.pop(0), one_head)
        elif step == "t":
            turns.pop(0)()
        elif step == "z":
            last_add()
        elif step[0] == "s":
            to_core(int(step[1]), 1).start()
            to_core(int(step[1]), 0).start()
        else:
            add_core(int(step[1]))
    for turn in turns:
        turn()
    dq_ref[...] = dq_pad[...]
    for group in groups:
        to_core(group, 0).wait_send()
        to_core(group, 1).wait_send()
        to_pair(group).wait_send()
    going.finish()


def attention_backward(place, query, d_out, lse_rows, kv_blocks, kept=(), given=(), parts=(), layers=(), rows=()):
    blocks = len(kv_blocks)
    tokens, width = query.shape
    one = jax.ShapeDtypeStruct((2, tokens, width), bf16)
    reduction = Reduction(kept, parts) if kept else None
    going = Homes([(layer, 0) for layer in layers]) if kept else None
    own = [one] * (1 if kept else blocks)
    dma = pltpu.SemaphoreType.DMA((len(HEAD_GROUPS), 3))
    linked = []
    if kept:
        linked = [pltpu.VMEM((2, 2, tokens, width), bf16), pltpu.VMEM((2, tokens, width), bf16), dma, dma]
        linked += going.scratch() + reduction.scratch()
    results = pl.pallas_call(
        functools.partial(attention_backward_kernel, blocks, reduction, going),
        out_shape=(jax.ShapeDtypeStruct((tokens, width), bf16),)
        + tuple(own)
        + (reduction.out_shapes() + going.out_shapes(rows[0]) if kept else ()),
        in_specs=[pl.BlockSpec(memory_space=pltpu.SMEM)] + vmem_specs(3 + blocks) + any_specs(2 * len(kept) + len(rows)),
        out_specs=tuple(vmem_specs(1 + len(own) + len(kept)) + any_specs(1 if kept else 0)),
        scratch_shapes=[
            pltpu.VMEM((tokens, width), bf16),
            pltpu.VMEM((blocks, tokens, tokens), f32),
            pltpu.VMEM((blocks, 2, tokens, width), bf16),
        ]
        + linked,
        compiler_params=pltpu.CompilerParams(
            vmem_limit_bytes=VMEM_LIMIT, **(dict(collective_id=4 + len(rows), has_side_effects=True) if kept else {})
        ),
        cost_estimate=pl.CostEstimate(
            flops=10 * HEADS * tokens * tokens * blocks * WINDOW,
            bytes_accessed=400_000_000 if kept else 100_000_000,
            transcendentals=HEADS * tokens * tokens * blocks,
        ),
        name="attention_backward",
    )(place, query, d_out, lse_rows, *kv_blocks, *kept, *given, *rows)
    first = 1 + len(own)
    return results[0], list(results[1:first]), list(results[first:first + len(kept)]), results[-1]


def last_kernel(reduction, going, early, layers, *refs):
    arrays, items = len(reduction.arrays), len(going.items)
    kept, given, refs = refs[:arrays], refs[arrays:2 * arrays], refs[2 * arrays:]
    rows, refs = refs[:items], refs[items:]
    sums, refs = (refs[:early], refs[early:2 * early]), refs[2 * early:]
    results, refs = refs[:arrays], refs[arrays:]
    homes, refs = refs[:going.count], refs[going.count:]
    other_half, refs = refs[:early + 1], refs[early + 1:]
    half_send, half_recv, chunk_send, chunk_recv = refs[:4]
    going.bind(rows, homes, refs[4:7])
    reduction.bind(kept, given, results, refs[7:])
    core = lax.axis_index("section")
    first_core = core == 0
    reduction.open()
    greet(*reduction.peers(), *going.peers())
    reduction.give(0)
    reduction.give(1)

    def half(i, layer):
        return remote_copy(sums[layer][i], other_half[i], half_send.at[i], half_recv.at[i], section=1 - core)

    def late_half(c):
        array, row, size = reduction.chunks[c]
        return remote_copy(
            results[array].at[pl.ds(row, size)],
            other_half[early].at[pl.ds(row, size)],
            chunk_send.at[c],
            chunk_recv.at[c],
            section=1 - core,
        )

    def settled(c):
        layer = layers[reduction.chunks[c][0]]
        if layer is not None:
            pl.when(core != layer)(late_half(c).start)

    reduction.settled = settled

    @pl.when(first_core)
    def second_layer():
        for i in range(early):
            half(i, 1).start()

    @pl.when(jnp.logical_not(first_core))
    def first_layer():
        for i in range(early):
            half(i, 0).start()

    going.start()
    for turn in reduction.turns():
        turn()
    for i in range(early):
        half(i, 0).wait()
    for c, (array, _, _) in enumerate(reduction.chunks):
        layer = layers[array]
        if layer is not None:
            pl.when(core != layer)(late_half(c).wait_send)
            pl.when(core == layer)(late_half(c).wait_recv)

    going.finish()


def reduce_last(kept, given, parts, layers, rows, first_sums, second_sums):
    reduction = Reduction(kept, parts)
    going = Homes([(0, 0)])
    early = len(first_sums)
    late = kept[layers.index(0)]
    halves = [jax.ShapeDtypeStruct(v.shape, v.dtype) for v in first_sums]
    halves.append(jax.ShapeDtypeStruct(late.shape[1:], late.dtype))
    n = reduction.count
    dma = pltpu.SemaphoreType.DMA
    out = pl.pallas_call(
        functools.partial(last_kernel, reduction, going, early, layers),
        out_shape=reduction.out_shapes() + going.out_shapes(rows) + tuple(halves),
        in_specs=any_specs(2 * len(kept) + 1 + 2 * early),
        out_specs=tuple(vmem_specs(len(kept)) + any_specs(early + 2)),
        scratch_shapes=[dma((early,)), dma((early,)), dma((n,)), dma((n,))] + going.scratch() + reduction.scratch(),
        compiler_params=pltpu.CompilerParams(
            collective_id=2, has_side_effects=True, vmem_limit_bytes=VMEM_LIMIT
        ),
        cost_estimate=pl.CostEstimate(flops=0, bytes_accessed=400_000_000, transcendentals=0),
        name="reduce_last",
    )(*kept, *given, rows, *first_sums, *second_sums)
    out = list(out)
    return out[:len(kept)], out[len(kept)], out[len(kept) + 1:]


def finish_kernel(parts, *refs):
    kinds = len(parts)
    first, second, other, targets, refs = refs[:kinds], refs[kinds:2 * kinds], refs[2 * kinds:3 * kinds], refs[3 * kinds:4 * kinds], refs[4 * kinds:]
    own, rest, stages, refs = refs[:kinds], refs[kinds:2 * kinds], refs[2 * kinds:3 * kinds], refs[3 * kinds:]
    sems, own_sems, rest_sems = refs
    first_core = lax.axis_index("section") == 0
    for k in range(kinds):
        pl.when(first_core)(pltpu.make_async_copy(first[k], own[k], own_sems.at[k]).start)
        pl.when(jnp.logical_not(first_core))(pltpu.make_async_copy(second[k], own[k], own_sems.at[k]).start)
        pltpu.make_async_copy(other[k], rest[k], rest_sems.at[k]).start()
    for k in range(kinds):
        rows, columns = targets[k].shape
        blocks = max(parts[k], 1)
        half, padded = first[k].shape[0], first[k].shape[1] // blocks
        size = columns // blocks
        pltpu.make_async_copy(first[k], own[k], own_sems.at[k]).wait()
        pltpu.make_async_copy(other[k], rest[k], rest_sems.at[k]).wait()

        def put(top, bottom, k=k, rows=rows, blocks=blocks, half=half, padded=padded, size=size):
            for b in range(blocks):
                here = pl.ds(b * size, size)
                stages[k][pl.ds(0, half), here] = top[:, pl.ds(b * padded, padded)].astype(f32)[:, :size]
                stages[k][pl.ds(half, rows - half), here] = bottom[:, pl.ds(b * padded, padded)].astype(f32)[:rows - half, :size]

        pl.when(first_core)(functools.partial(put, own[k], rest[k]))
        pl.when(jnp.logical_not(first_core))(functools.partial(put, rest[k], own[k]))
        pltpu.make_async_copy(stages[k], targets[k], sems.at[k]).start()
    for k in range(kinds):
        pltpu.make_async_copy(stages[k], targets[k], sems.at[k]).wait()


def finish(first, second, other, shapes, parts):
    kinds = len(first)
    return pl.pallas_call(
        functools.partial(finish_kernel, parts),
        out_shape=tuple(jax.ShapeDtypeStruct(s, f32) for s in shapes),
        in_specs=any_specs(3 * kinds),
        out_specs=tuple(any_specs(kinds)),
        scratch_shapes=[pltpu.VMEM(v.shape, bf16) for v in first] * 2
        + [pltpu.VMEM(s, f32) for s in shapes]
        + [pltpu.SemaphoreType.DMA((kinds,))] * 3,
        compiler_params=pltpu.CompilerParams(vmem_limit_bytes=VMEM_LIMIT),
        name="finish",
    )(*first, *second, *other)


def padded_shape(weight, parts):
    rows, columns = weight.shape
    rows = round_up(rows, LANES) if parts == 0 else round_up(rows, 32)
    return rows, columns if parts < 2 else parts * round_up(columns // parts, LANES)


STAGE_ROWS = 9


class Gather:
    def __init__(self, masters, parts, over_seq):
        self.parts, self.kinds, self.over_seq = parts, len(masters), over_seq
        self.shapes = [padded_shape(m, p) for m, p in zip(masters, parts)]
        self.wide_shapes = []
        for m in masters:
            rows = round_up(-(-m.shape[0] // STAGE_ROWS), 16)
            self.wide_shapes.append((2, rows, m.shape[1]))

    def out_shapes(self, ranks):
        return tuple(jax.ShapeDtypeStruct((ranks,) + s, bf16) for s in self.shapes) * 2

    def scratch(self):
        dma = pltpu.SemaphoreType.DMA
        n = 2 * self.kinds
        return (
            [pltpu.VMEM(s, f32) for s in self.wide_shapes]
            + [pltpu.VMEM(s, bf16) for s in self.shapes] * 2
            + [dma((self.kinds, 2)), dma((n,)), dma((n, 10)), dma((n, 10))]
        )

    def bind(self, masters, whole, scratch):
        n = self.kinds
        self.masters, self.whole = masters, whole
        self.wide, self.shares, self.got = scratch[:n], scratch[n:2 * n], scratch[2 * n:3 * n]
        self.wide_sem, self.own_sem, self.send, self.recv = scratch[3 * n:]
        self.core = lax.axis_index("section")
        self.rank = lax.axis_index("dp")
        z = lax.axis_index("seq")
        self.near, self.far, self.across = partners()
        self.parity = lax.rem(z, 2)
        self.pair_z = z + 1 - 2 * self.parity

    def peers(self):
        return [{"dp": self.near}, {"dp": self.far}, {"seq": self.pair_z}, {"section": 1 - self.core}]

    def rows_of(self, u, start, size):
        half = self.whole[u].shape[1] // 2
        return pl.ds(pl.multiple_of(self.core * half + start, 16), size)

    def copy(self, u, k, block, start, size, **place):
        ref = self.whole[u].at[block, self.rows_of(u, start, size)]
        return remote_copy(ref, ref, self.send.at[u, k], self.recv.at[u, k], **place)

    def sizes(self, u):
        half = self.whole[u].shape[1] // 2
        rest = round_up(half * self.over_seq[u] // 9, 16)
        return half - rest, rest

    def to_dp(self, u, k, source=None):
        size, rest = self.sizes(u)
        block, place = ((self.rank, self.near), (self.rank, self.far), (self.far, self.near))[k]
        rows = self.rows_of(u, self.parity * rest, size)
        target = self.whole[u].at[block, rows]
        source = target if source is None else source.at[rows]
        return remote_copy(source, target, self.send.at[u, k], self.recv.at[u, k], dp=place)

    def to_pair(self, u, k):
        size, rest = self.sizes(u)
        block = (self.near, self.far, self.across)[k]
        return self.copy(u, 3 + k, block, self.parity * size, rest, seq=self.pair_z)

    def to_core(self, u, k):
        half = self.whole[u].shape[1] // 2
        return self.copy(u, 6 + k, (self.near, self.far, self.across)[k], 0, half, section=1 - self.core)

    def given(self, u):
        kind = u % self.kinds
        return remote_copy(
            self.shares[kind], self.got[kind], self.send.at[u, 9], self.recv.at[u, 9], section=1 - self.core
        )

    def kept(self, u, source):
        return pltpu.make_async_copy(source[u % self.kinds], self.whole[u].at[self.rank], self.own_sem.at[u])

    def stages(self, kind):
        rows, step = self.masters[kind].shape[0], self.wide_shapes[kind][1]
        return [(i % 2, a, min(step, rows - a)) for i, a in enumerate(range(0, rows, step))]

    def load(self, kind, stage):
        slot, first, size = stage
        return pltpu.make_async_copy(
            self.masters[kind].at[pl.ds(first, size)],
            self.wide[kind].at[slot, pl.ds(0, size)],
            self.wide_sem.at[kind, slot],
        )

    def open(self):
        for kind in range(self.kinds):
            for stage in self.stages(kind)[:2]:
                self.load(kind, stage).start()

    def cast(self, kind):
        share, wide = self.shares[kind], self.wide[kind]
        blocks = max(self.parts[kind], 1)
        size, padded = wide.shape[2] // blocks, share.shape[1] // blocks
        share[...] = jnp.zeros(share.shape, bf16)
        stages = self.stages(kind)
        for i, (slot, first, count) in enumerate(stages):
            self.load(kind, stages[i]).wait()
            for b in range(blocks):
                value = wide[slot, pl.ds(0, count), b * size:(b + 1) * size]
                share[pl.ds(first, count), pl.ds(b * padded, size)] = value.astype(bf16)
            if i + 2 < len(stages):
                self.load(kind, stages[i + 2]).start()

    def first(self, u):
        if u < self.kinds:
            self.cast(u)
            pl.when(self.core == 0)(self.given(u).start)
        if 2 <= u < self.kinds + 2:
            pl.when(self.core == 1)(self.given(u + 2).start)

        def send_from(source):
            self.to_dp(u, 1, source[u % self.kinds]).start()
            self.to_dp(u, 0, source[u % self.kinds]).start()
            self.kept(u, source).start()

        @pl.when(self.core == u // self.kinds)
        def own():
            send_from(self.shares)

        @pl.when(self.core != u // self.kinds)
        def other():
            self.given(u).wait_recv()
            send_from(self.got)

    def second(self, u):
        self.to_dp(u, 1).wait_recv()
        self.to_dp(u, 2).start()
        self.to_pair(u, 1).start()
        self.to_dp(u, 0).wait_recv()
        self.to_pair(u, 0).start()

    def third(self, u):
        self.to_dp(u, 2).wait_recv()
        self.to_pair(u, 2).start()
        for k in (1, 0):
            self.to_pair(u, k).wait_recv()
            self.to_core(u, k).start()

    def fourth(self, u):
        self.to_pair(u, 2).wait_recv()
        self.to_core(u, 2).start()

    def last(self, u):
        for k in range(3):
            self.to_core(u, k).wait()
            self.to_pair(u, k).wait_send()
        self.to_dp(u, 0, self.shares[u % self.kinds]).wait_send()
        self.to_dp(u, 1, self.shares[u % self.kinds]).wait_send()
        self.to_dp(u, 2).wait_send()
        self.kept(u, self.shares).wait()

        @pl.when(self.core == u // self.kinds)
        def gave():
            self.given(u).wait_send()

    def turns(self):
        steps = (self.first, self.second, self.third, self.fourth, self.last)
        units = 2 * self.kinds

        def turn(number):
            for lag, step in enumerate(steps):
                if 0 <= number - lag < units:
                    step(number - lag)

        return [functools.partial(turn, number) for number in range(units + len(steps) - 1)]


def gather_kernel(gather, *refs):
    kinds = gather.kinds
    gather.bind(refs[:kinds], refs[kinds:3 * kinds], refs[3 * kinds:])
    gather.open()
    greet(*gather.peers())
    for turn in gather.turns():
        turn()


def gather_weights(masters, parts, ranks):
    kinds = len(masters)
    gather = Gather(masters, parts, (3,) * (2 * kinds))
    results = pl.pallas_call(
        functools.partial(gather_kernel, gather),
        out_shape=gather.out_shapes(ranks),
        in_specs=any_specs(kinds),
        out_specs=tuple(any_specs(2 * kinds)),
        scratch_shapes=gather.scratch(),
        compiler_params=pltpu.CompilerParams(
            collective_id=1, has_side_effects=True, vmem_limit_bytes=VMEM_LIMIT
        ),
        cost_estimate=pl.CostEstimate(flops=0, bytes_accessed=700_000_000, transcendentals=0),
        name="gather_weights",
    )(*masters)
    return results[:kinds], results[kinds:]


def norm_parts(values):
    center = values - jnp.mean(values, axis=-1, keepdims=True)
    inverse = lax.rsqrt(jnp.mean(center * center, axis=-1, keepdims=True) + EPS)
    return center * inverse, inverse


def norm_back(values, gain, upstream):
    unit, inverse = norm_parts(values)
    weighted = upstream * gain
    grad = inverse * (
        weighted
        - jnp.mean(weighted, axis=-1, keepdims=True)
        - unit * jnp.mean(weighted * unit, axis=-1, keepdims=True)
    )
    return grad, jnp.sum(upstream * unit, axis=0, keepdims=True), jnp.sum(upstream, axis=0, keepdims=True)


def block_loads(source, target, sems, row):
    return [
        pltpu.make_async_copy(source.at[b], target.at[b], sems.at[row, b]) for b in range(source.shape[0])
    ]


def split_columns(target, value):
    ranks, _, padded = target.shape
    share = value.shape[1] // ranks
    target[...] = jnp.zeros(target.shape, target.dtype)
    for b in range(ranks):
        target[b, :, pl.ds(0, share)] = value[:, b * share:(b + 1) * share]


def join_columns(target, parts):
    share = target.shape[1] // len(parts)
    for b, part in enumerate(parts):
        target[:, b * share:(b + 1) * share] = part[:, :share]


def qkv_kernel(h_ref, norm_ref, w_ref, a_ref, q_ref, kv_ref, w_mem, sems):
    ranks = w_ref.shape[0]
    loads = block_loads(w_ref, w_mem, sems, 0)
    load_all(loads)
    unit, _ = norm_parts(h_ref[...].astype(f32))
    split_columns(a_ref, (unit * norm_ref[0:1] + norm_ref[2:3]).astype(bf16))
    block = q_ref.shape[1]
    for copy in loads:
        copy.wait()
    for part, target in enumerate((q_ref, kv_ref.at[0], kv_ref.at[1])):
        total = sum_of([dot_nn(a_ref[b], w_mem[b, :, pl.ds(part * block, block)]) for b in range(ranks)])
        target[...] = total.astype(bf16)


def project_qkv(hidden, norm, weight):
    tokens = hidden.shape[0]
    ranks, rows, columns = weight.shape
    return pl.pallas_call(
        qkv_kernel,
        out_shape=(
            jax.ShapeDtypeStruct((ranks, tokens, rows), bf16),
            jax.ShapeDtypeStruct((tokens, columns // 3), bf16),
            jax.ShapeDtypeStruct((2, tokens, columns // 3), bf16),
        ),
        in_specs=vmem_specs(2) + any_specs(1),
        out_specs=tuple(vmem_specs(3)),
        scratch_shapes=[pltpu.VMEM(weight.shape, bf16), pltpu.SemaphoreType.DMA((1, ranks))],
        compiler_params=pltpu.CompilerParams(vmem_limit_bytes=VMEM_LIMIT),
        cost_estimate=pl.CostEstimate(
            flops=2 * tokens * weight.size, bytes_accessed=2 * weight.size, transcendentals=tokens
        ),
        name="project_qkv",
    )(hidden, norm, weight)


def mlp_kernel(
    o_ref, h_ref, norm_ref, wo_ref, wf_ref, wp_ref,
    ob_ref, r_ref, c_ref, slope_ref, g_ref, out_ref,
    wo, wf, wp, sems,
):
    ranks = wo.shape[0]
    loads = [block_loads(s, t, sems, i) for i, (s, t) in enumerate(((wo_ref, wo), (wf_ref, wf), (wp_ref, wp)))]
    for some in loads:
        load_all(some)
    split_columns(ob_ref, o_ref[:, pl.ds(0, h_ref.shape[1])])
    for copy in loads[0]:
        copy.wait()
    r_ref[...] = h_ref[...].astype(f32) + sum_of([dot_nn(ob_ref[b], wo[b]) for b in range(ranks)])
    unit, _ = norm_parts(r_ref[...])
    split_columns(c_ref, (unit * norm_ref[1:2] + norm_ref[3:4]).astype(bf16))
    for copy in loads[1]:
        copy.wait()
    block = g_ref.shape[2]
    step = block // 3

    def columns(i, carry):
        at = pl.multiple_of(i * step, LANES)
        pre = sum_of([dot_nn(c_ref[b], wf[b, :, pl.ds(at, step)]) for b in range(ranks)])
        within = pl.ds(pl.multiple_of(lax.rem(i, 3) * step, LANES), step)
        g_ref[i // 3, :, within], slope_ref[i // 3, :, within] = gelu_parts(pre)
        return carry

    lax.fori_loop(0, 3 * ranks, columns, 0)
    for copy in loads[2]:
        copy.wait()
    out_ref[...] = (r_ref[...] + sum_of([dot_nn(g_ref[b], wp[b]) for b in range(ranks)])).astype(bf16)


def out_and_mlp(attended, hidden, norm, w_out, w_fc, w_proj):
    tokens, width = hidden.shape
    ranks, rows, _ = w_out.shape
    ff = w_proj.shape[1]
    flat = jax.ShapeDtypeStruct((ranks, tokens, rows), bf16)
    size = w_out.size + w_fc.size + w_proj.size
    return pl.pallas_call(
        mlp_kernel,
        out_shape=(
            flat,
            jax.ShapeDtypeStruct((tokens, width), f32),
            flat,
            jax.ShapeDtypeStruct((ranks, tokens, ff), f32),
            jax.ShapeDtypeStruct((ranks, tokens, ff), bf16),
            jax.ShapeDtypeStruct((tokens, width), bf16),
        ),
        in_specs=vmem_specs(3) + any_specs(3),
        out_specs=tuple(vmem_specs(6)),
        scratch_shapes=[
            pltpu.VMEM(w_out.shape, bf16),
            pltpu.VMEM(w_fc.shape, bf16),
            pltpu.VMEM(w_proj.shape, bf16),
            pltpu.SemaphoreType.DMA((3, ranks)),
        ],
        compiler_params=pltpu.CompilerParams(vmem_limit_bytes=VMEM_LIMIT),
        cost_estimate=pl.CostEstimate(
            flops=2 * tokens * size, bytes_accessed=2 * size, transcendentals=2 * tokens * ff * ranks
        ),
        name="out_and_mlp",
    )(attended, hidden, norm, w_out, w_fc, w_proj)


def gelu_parts(pre):
    below = 0.5 * (1.0 + lax.erf(pre * math.sqrt(0.5)))
    slope = below + pre * (jnp.exp(-0.5 * pre * pre) * (1.0 / math.sqrt(2.0 * math.pi)))
    return (pre * below).astype(bf16), slope


FORWARD_ORDER = (
    "f0", "f1", "s0", "f2", "t0", "s1", "40", "s2", "f3", "l0", "Q0", "f4", "S0", "t1", "A00", "f5", "s3",
    "s4", "f6", "A01", "t2", "A02", "41", "s5", "f7", "A03", "t3", "43", "l1", "O", "s6", "42", "l2", "l3",
    "W", "M", "B0", "t4", "B1", "B2", "44", "t5", "s7", "B3", "l4", "t6", "45", "Q1", "t7", "S1", "46", "47",
    "l6", "l5", "A10", "l7", "A11", "A12", "A13",
)
FORWARD_OVER_SEQ = (3, 2, 3, 2, 3, 2, 2, 2)


def forward_kernel(gather, place, in_ref, cot_in, own_norms, *refs):
    kinds = gather.kinds
    masters, refs = refs[:kinds], refs[kinds:]
    whole, refs = refs[:2 * kinds], refs[2 * kinds:]
    (a_ref, q_ref, kv_ref, *others), refs = refs[:6], refs[6:]
    (lse_ref, ob_ref, r_ref, c_ref, slope_ref, g_ref, out_ref), refs = refs[:7], refs[7:]
    (norm_ref, h_ref, cot_ref, next_a, next_q, next_kv, *next_others), refs = refs[:9], refs[9:]
    (next_lse, next_o), refs = refs[:2], refs[2:]
    (rows_send, rows_recv, norm_sem, lse_mem, bias, links_send, links_recv, next_send, next_recv, total, columns_mem, rows_mem, wo, slopes, gs), refs = refs[:15], refs[15:]
    (columns_sem, rows_sem, wo_sem, out_sem), refs = refs[:4], refs[4:]
    gather.bind(masters, whole, refs)
    gather.open()
    core = lax.axis_index("section")
    z = lax.axis_index("seq")
    group = z // 2
    swapped = z + 2 - 4 * group
    greet(*gather.peers(), {"seq": swapped})
    moves = ((in_ref, h_ref), (cot_in, cot_ref))

    def stay(i):
        return pltpu.make_async_copy(moves[i][0].at[group, 0], moves[i][1], rows_send.at[i])

    def move(i):
        return remote_copy(moves[i][0].at[1 - group, 0], moves[i][1], rows_send.at[i], rows_recv.at[i], seq=swapped)

    norms_here = pltpu.make_async_copy(own_norms, norm_ref.at[core], norm_sem.at[0])
    norms_there = remote_copy(own_norms, norm_ref.at[core], norm_sem.at[1], norm_sem.at[2], section=1 - core)
    norms_here.start()
    norms_there.start()

    def rows_arrive(i):
        pl.when(core == 0)(stay(i).wait)
        pl.when(core == 1)(move(i).wait)

    for i in range(2):
        pl.when(core == 0)(stay(i).start)
        pl.when(core == 1)(move(i).start)
    ranks, tokens, rows = a_ref.shape
    block = q_ref.shape[1]

    def load_columns(weight, part):
        slot = part % 2
        return [
            pltpu.make_async_copy(
                weight.at[b, :, pl.ds(part * block, block)], columns_mem.at[slot, b], columns_sem.at[slot, b]
            )
            for b in range(ranks)
        ]

    def load_rows(weight, b):
        return [pltpu.make_async_copy(weight.at[b], rows_mem.at[b % 2], rows_sem.at[b % 2])]

    def wait_all(copies):
        for copy in copies:
            copy.wait()

    def project(hidden, norms, weight, a, q, kv):
        for part in range(2):
            load_all(load_columns(weight, part))
        unit, _ = norm_parts(hidden)
        split_columns(a, (unit * norms[0:1] + norms[2:3]).astype(bf16))
        for part, target in enumerate((q, kv.at[0], kv.at[1])):
            wait_all(load_columns(weight, part))
            target[...] = sum_of([dot_nn(a[b], columns_mem[part % 2, b]) for b in range(ranks)]).astype(bf16)
            if part == 0:
                load_all(load_columns(weight, 2))

    def put_out(b):
        slot = b % 2
        return [
            pltpu.make_async_copy(slopes.at[slot], slope_ref.at[b], out_sem.at[slot, 0]),
            pltpu.make_async_copy(gs.at[slot], g_ref.at[b], out_sem.at[slot, 1]),
        ]

    def mlp_block(b):
        slot = b % 2
        if b >= 2:
            wait_all(put_out(b - 2))
        wait_all(load_columns(whole[2], b))
        third = block // 3

        def some_columns(i, carry):
            at = pl.ds(pl.multiple_of(i * third, LANES), third)
            pre = sum_of([dot_nn(c_ref[k], columns_mem[slot, k, :, at]) for k in range(ranks)])
            gs[slot, :, at], slopes[slot, :, at] = gelu_parts(pre)
            return carry

        lax.fori_loop(0, 3, some_columns, 0)
        load_all(put_out(b))
        if b + 2 < ranks:
            load_all(load_columns(whole[2], b + 2))
        wait_all(load_rows(whole[3], b))
        total[...] = total[...] + dot_nn(gs[slot], rows_mem[slot])
        if b + 2 < ranks:
            load_all(load_rows(whole[3], b + 2))

    def attention(layer):
        if layer == 0:
            return attention_steps(
                place, q_ref, [kv_ref] + others, next_o, lse_ref, lse_mem, bias, (links_send, links_recv)
            )
        return attention_steps(
            place, next_q, [next_kv] + next_others, next_o, next_lse, lse_mem, bias, (next_send, next_recv)
        )

    out_loads = [pltpu.make_async_copy(whole[1].at[b], wo.at[b], wo_sem.at[b]) for b in range(ranks)]

    def middle():
        attention(0)[2]()
        split_columns(ob_ref, next_o[:, pl.ds(0, h_ref.shape[1])])
        wait_all(out_loads)
        r_ref[...] = h_ref[...].astype(f32) + sum_of([dot_nn(ob_ref[b], wo[b]) for b in range(ranks)])
        unit, _ = norm_parts(r_ref[...])
        split_columns(c_ref, (unit * norm_ref[0, 1:2] + norm_ref[0, 3:4]).astype(bf16))
        total[...] = r_ref[...]

    def qkv(layer):
        if layer == 0:
            rows_arrive(0)
            norms_here.wait()
            norms_there.wait()
            project(h_ref[...].astype(f32), norm_ref.at[0], whole[0], a_ref, q_ref, kv_ref)
            return
        for b in range(2, ranks):
            wait_all(put_out(b))
        out_ref[...] = total[...].astype(bf16)
        project(out_ref[...].astype(f32), norm_ref.at[1], whole[kinds], next_a, next_q, next_kv)

    steps = {"f": gather.first, "s": gather.second, "t": gather.third, "4": gather.fourth, "l": gather.last}
    steps.update({"Q": qkv, "S": lambda layer: attention(layer)[0](), "B": mlp_block})
    for step in FORWARD_ORDER:
        if step == "M":
            middle()
        elif step == "O":
            load_all(out_loads)
        elif step == "W":
            for b in range(2):
                load_all(load_columns(whole[2], b))
                load_all(load_rows(whole[3], b))
        elif step[0] == "A":
            attention(int(step[1]))[1](int(step[2]))
        else:
            steps[step[0]](int(step[1]))
    attention(1)[2]()
    rows_arrive(1)


def gather_and_forward(place, layer_in, cotangent, norms, masters, parts, ranks):
    tokens, width = layer_in.shape[2:]
    kinds = len(masters)
    gather = Gather(masters, parts, FORWARD_OVER_SEQ)
    shapes = gather.shapes
    rows, block = shapes[1][0], shapes[0][1] // 3
    ff = shapes[3][0]

    def array(dtype, *shape):
        return jax.ShapeDtypeStruct(shape, dtype)

    flat, two = array(bf16, ranks, tokens, rows), array(bf16, 2, tokens, block)
    one = array(bf16, tokens, block)
    saved = (flat, one, two, two, two, two, array(f32, LANES, tokens), flat, array(f32, tokens, width), flat)
    wide = (array(f32, ranks, tokens, ff), array(bf16, ranks, tokens, ff))
    hidden = array(bf16, tokens, width)
    after = (hidden, array(f32, 2, 4, width), hidden, hidden, flat, one, two, two, two, two, array(f32, LANES, tokens), one)
    dma = pltpu.SemaphoreType.DMA
    links = dma((len(HEAD_GROUPS), 3))
    out = pl.pallas_call(
        functools.partial(forward_kernel, gather),
        out_shape=gather.out_shapes(ranks) + saved + wide + after,
        in_specs=[pl.BlockSpec(memory_space=pltpu.SMEM)] + any_specs(2) + vmem_specs(1) + any_specs(kinds),
        out_specs=tuple(
            any_specs(2 * kinds)
            + vmem_specs(len(saved))
            + any_specs(2)
            + vmem_specs(3)
            + any_specs(1)
            + vmem_specs(len(after) - 4)
        ),
        scratch_shapes=[
            dma((2,)),
            dma((2,)),
            dma((3,)),
            pltpu.VMEM((tokens, LANES), f32),
            pltpu.VMEM((LINKED, tokens, tokens), f32),
            links,
            links,
            links,
            links,
            pltpu.VMEM((tokens, width), f32),
            pltpu.VMEM((2, ranks, rows, block), bf16),
            pltpu.VMEM((2, ff, width), bf16),
            pltpu.VMEM((ranks, rows, width), bf16),
            pltpu.VMEM((2, tokens, ff), f32),
            pltpu.VMEM((2, tokens, ff), bf16),
            dma((2, ranks)),
            dma((2,)),
            dma((ranks,)),
            dma((2, 2)),
        ]
        + gather.scratch(),
        compiler_params=pltpu.CompilerParams(
            collective_id=1, has_side_effects=True, vmem_limit_bytes=VMEM_LIMIT
        ),
        cost_estimate=pl.CostEstimate(flops=0, bytes_accessed=700_000_000, transcendentals=0),
        name="gather_and_forward",
    )(place, layer_in, cotangent, norms, *masters)
    weights, out = (out[:kinds], out[kinds:2 * kinds]), out[2 * kinds:]
    normed, query, own, along, beside, both, lse, attended, residual, second, slope, activated, *out = out
    result, norms, hidden, cotangent, *out = out
    saved = (hidden, normed, query, [own, along, beside, both], attended, lse, residual, second, slope, activated)
    normed, query, own, along, beside, both, lse, attended = out
    return weights, norms, cotangent, saved, result, (normed, query, [own, along, beside, both], lse, attended)


class Writer:
    def __init__(self, slots, sems):
        self.slots, self.sems, self.last = slots, sems, [(), ()]
        self.turn = 0

    def put(self, make, keep, give):
        slot = self.turn % 2
        self.turn += 1
        for copy in self.last[slot]:
            copy.wait()
        make(self.slots.at[slot])
        core = lax.axis_index("section")
        half = self.slots.shape[1] // 2
        copies = []
        for i, (target, which) in enumerate(((keep, core), (give, 1 - core))):
            part = self.slots.at[slot, pl.ds(pl.multiple_of(which * half, 16), half)]
            copies.append(pltpu.make_async_copy(part, target, self.sems.at[slot, i]))
        load_all(copies)
        self.last[slot] = copies

    def finish(self):
        for copies in self.last:
            for copy in copies:
                copy.wait()


def all_rows(value, weight):
    ranks, rows, columns = weight.shape
    product = dot_nt(value, weight[...].reshape(ranks * rows, columns))
    return [product[:, b * rows:(b + 1) * rows] for b in range(ranks)]


def product_into(stage, left, right, step):
    columns = right.shape[1]
    for a in range(0, columns, step):
        n = min(step, columns - a)
        stage[:, pl.ds(a, n)] = dot_tn(left[...], right[:, pl.ds(a, n)]).astype(bf16)


def mlp_back_kernel(
    e_ref, slope_ref, g_ref, c_ref, ob_ref, r_ref, norm_ref, wo_ref, wf_ref, wp_ref,
    res_ref, att_ref, vec_ref, p_keep, p_give, f_keep, f_give, o_keep, o_give,
    wo, wf, wp, pre, d_sec, branch, att_mem, p_slots, f_slots, o_slots, sems, p_sems, f_sems, o_sems,
):
    ranks = wo.shape[0]
    loads = [block_loads(s, t, sems, i) for i, (s, t) in enumerate(((wp_ref, wp), (wf_ref, wf), (wo_ref, wo)))]
    for some in loads:
        load_all(some)
    writer = Writer(p_slots, p_sems)
    rows, ff = c_ref.shape[2], g_ref.shape[2]
    width = e_ref.shape[1]
    for b in range(ranks):
        loads[0][b].wait()
        pre[:, pl.ds(b * ff, ff)] = (dot_nt(e_ref[...], wp[b]) * slope_ref[b]).astype(bf16)
        writer.put(
            lambda s, b=b: product_into(s, g_ref.at[b], e_ref, width), p_keep.at[b], p_give.at[b]
        )
    for b in range(ranks):
        loads[1][b].wait()
    join_columns(d_sec, all_rows(pre[...], wf))
    grad, gain, bias = norm_back(r_ref[...], norm_ref[1:2], d_sec[...])
    vec_ref[0:1] = gain
    vec_ref[1:2] = bias
    total = e_ref[...].astype(f32) + grad
    res_ref[...] = total
    branch[...] = total.astype(bf16)
    for b in range(ranks):
        loads[2][b].wait()
    join_columns(att_mem, all_rows(branch[...], wo))
    att_ref[...] = jnp.zeros(att_ref.shape, bf16)
    att_ref[:, pl.ds(0, width)] = att_mem[...].astype(bf16)
    f_writer = Writer(f_slots, f_sems)
    o_writer = Writer(o_slots, o_sems)
    for b in range(ranks):
        f_writer.put(
            lambda s, b=b: product_into(s, c_ref.at[b], pre, ff), f_keep.at[b], f_give.at[b]
        )
        o_writer.put(
            lambda s, b=b: product_into(s, ob_ref.at[b], branch, width), o_keep.at[b], o_give.at[b]
        )
    writer.finish()
    f_writer.finish()
    o_writer.finish()


def half_rows(weight):
    return jax.ShapeDtypeStruct((weight.shape[0], weight.shape[1] // 2, weight.shape[2]), bf16)


def mlp_back(upstream, slope, activated, second, attended, residual, norm, w_out, w_fc, w_proj):
    tokens, width = upstream.shape
    ranks, rows, _ = w_out.shape
    size = w_out.size + w_fc.size + w_proj.size
    return pl.pallas_call(
        mlp_back_kernel,
        out_shape=(
            jax.ShapeDtypeStruct((tokens, width), f32),
            jax.ShapeDtypeStruct((tokens, round_up(width, LANES)), bf16),
            jax.ShapeDtypeStruct((2, width), f32),
        )
        + tuple(half_rows(w) for w in (w_proj, w_proj, w_fc, w_fc, w_out, w_out)),
        in_specs=vmem_specs(7) + any_specs(3),
        out_specs=tuple(vmem_specs(3) + any_specs(6)),
        scratch_shapes=[
            pltpu.VMEM(w_out.shape, bf16),
            pltpu.VMEM(w_fc.shape, bf16),
            pltpu.VMEM(w_proj.shape, bf16),
            pltpu.VMEM((tokens, w_fc.shape[2]), bf16),
            pltpu.VMEM((tokens, width), f32),
            pltpu.VMEM((tokens, width), bf16),
            pltpu.VMEM((tokens, width), f32),
            pltpu.VMEM((2,) + w_proj.shape[1:], bf16),
            pltpu.VMEM((2,) + w_fc.shape[1:], bf16),
            pltpu.VMEM((2,) + w_out.shape[1:], bf16),
            pltpu.SemaphoreType.DMA((3, ranks)),
            pltpu.SemaphoreType.DMA((2, 2)),
            pltpu.SemaphoreType.DMA((2, 2)),
            pltpu.SemaphoreType.DMA((2, 2)),
        ],
        compiler_params=pltpu.CompilerParams(vmem_limit_bytes=VMEM_LIMIT),
        cost_estimate=pl.CostEstimate(
            flops=4 * tokens * size, bytes_accessed=4 * size, transcendentals=tokens
        ),
        name="mlp_backward",
    )(upstream, slope, activated, second, attended, residual, norm, w_out, w_fc, w_proj)


def qkv_back_kernel(
    dq_ref, dkv_ref, a_ref, h_ref, res_ref, norm_ref, w_ref,
    sent_ref, vec_ref, keep, give,
    w_mem, d_proj, d_normed, slots, sems, out_sems,
):
    ranks, rows, columns = w_ref.shape
    loads = block_loads(w_ref, w_mem, sems, 0)
    load_all(loads)
    writer = Writer(slots, out_sems)
    block = columns // 3
    d_proj[:, pl.ds(0, block)] = dq_ref[...]
    d_proj[:, pl.ds(block, block)] = dkv_ref[0]
    d_proj[:, pl.ds(2 * block, block)] = dkv_ref[1]
    for b in range(ranks):
        writer.put(
            lambda s, b=b: product_into(s, a_ref.at[b], d_proj, block), keep.at[b], give.at[b]
        )
    for copy in loads:
        copy.wait()
    join_columns(d_normed, all_rows(d_proj[...], w_mem))
    grad, gain, bias = norm_back(h_ref[...].astype(f32), norm_ref[0:1], d_normed[...])
    vec_ref[0:1] = gain
    vec_ref[1:2] = bias
    sent_ref[...] = (res_ref[...] + grad).astype(bf16)
    writer.finish()


def qkv_back(d_query, d_pair, normed, hidden, residual_grad, norm, weight):
    tokens, width = hidden.shape
    ranks, rows, columns = weight.shape
    return pl.pallas_call(
        qkv_back_kernel,
        out_shape=(
            jax.ShapeDtypeStruct((tokens, width), bf16),
            jax.ShapeDtypeStruct((2, width), f32),
            half_rows(weight),
            half_rows(weight),
        ),
        in_specs=vmem_specs(6) + any_specs(1),
        out_specs=tuple(vmem_specs(2) + any_specs(2)),
        scratch_shapes=[
            pltpu.VMEM(weight.shape, bf16),
            pltpu.VMEM((tokens, columns), bf16),
            pltpu.VMEM((tokens, width), f32),
            pltpu.VMEM((2, rows, columns), bf16),
            pltpu.SemaphoreType.DMA((1, ranks)),
            pltpu.SemaphoreType.DMA((2, 2)),
        ],
        compiler_params=pltpu.CompilerParams(vmem_limit_bytes=VMEM_LIMIT),
        cost_estimate=pl.CostEstimate(
            flops=4 * tokens * weight.size, bytes_accessed=4 * weight.size, transcendentals=tokens
        ),
        name="qkv_backward",
    )(d_query, d_pair, normed, hidden, residual_grad, norm, weight)


def swap_cores(value):
    return lax.ppermute(value, "section", [(0, 1), (1, 0)])


def send_joint(value, axis, route):
    size = lax.axis_size(axis)
    pairs = []
    for core in range(2):
        for index in range(size):
            to = route(core, index)
            if to is not None:
                pairs.append((core * size + index, to[0] * size + to[1]))
    return lax.ppermute(value, ("section", axis), pairs)


def on_device(
    layer_in, cotangent, lengths, block_order, w_qkv, w_out, w_fc, w_proj, norm_gains, norm_biases
):
    tokens, width = layer_in.shape[2:]
    blocks = lax.axis_size("seq")
    ranks = lax.axis_size("dp")
    half = blocks // 2
    core = lax.axis_index("section")
    place_dp = lax.axis_index("dp")
    place_seq = lax.axis_index("seq")
    first_core = core == 0
    group = place_seq // half
    linked = blocks == LINKED and ranks == LINKED

    def per_core(left, right):
        return jnp.where(first_core, left, right)

    def after(value, *others):
        return lax.optimization_barrier((value, others))[0]

    def own_rows(value):
        value = value[:, 0]
        mine = lax.dynamic_index_in_dim(value, group, 0, False)
        other = lax.dynamic_index_in_dim(value, 1 - group, 0, False)
        moved = send_joint(other, "seq", lambda c, z: (1, z ^ half) if c == 1 else None)
        return per_core(mine, moved)

    def back_home(first, second):
        crossed = send_joint(
            per_core(second, first), "seq", lambda c, z: (1, z) if c == 0 else (0, z ^ half)
        )
        along = send_joint(second, "seq", lambda c, z: (1, z ^ half) if c == 1 else None)
        mine = per_core(first, crossed)
        other = per_core(crossed, along)
        return jnp.where(group == 0, jnp.stack([mine, other]), jnp.stack([other, mine]))

    steps = []
    bit = 1
    while bit < half:
        steps.append(bit)
        bit *= 2
    my_block = per_core(place_seq, place_seq ^ half)
    block_ids = [my_block]
    for bit in steps:
        block_ids = block_ids + [b ^ bit for b in block_ids]
    block_ids = block_ids + [b ^ half for b in block_ids]
    limit = lax.dynamic_index_in_dim(lengths[:, 0], group, 0, False)
    starts = block_order[jnp.stack(block_ids)] * tokens
    place = jnp.concatenate([limit[None], starts]).astype(jnp.int32)

    def gather_keys(own):
        parts = [own]
        for bit in steps:
            route = [(z, z ^ bit) for z in range(blocks)]
            parts = parts + [lax.ppermute(p, "seq", route) for p in parts]
        return parts + [swap_cores(p) for p in parts]

    def scatter_keys(parts):
        cut = len(parts) // 2
        moved = [swap_cores(p) for p in parts[cut:]]
        parts = [(p.astype(f32) + m.astype(f32)).astype(bf16) for p, m in zip(parts[:cut], moved)]
        for bit in reversed(steps):
            cut = len(parts) // 2
            route = [(z, z ^ bit) for z in range(blocks)]
            moved = [lax.ppermute(p, "seq", route) for p in parts[cut:]]
            parts = [(p.astype(f32) + m.astype(f32)).astype(bf16) for p, m in zip(parts[:cut], moved)]
        return parts[0]

    masters = (w_qkv[0], w_out[0], w_fc[0], w_proj[0])
    parts = (3, 1, ranks, 0)
    own_norms = jnp.concatenate([norm_gains[0], norm_biases[0]])

    def attend(projected):
        normed, query, own_keys = projected
        keys = gather_keys(own_keys)
        attended, lse, keys = attention_forward(place, query, keys, blocks)
        return normed, query, keys, lse, attended

    def forward(hidden, layer, attention):
        _, wout, wfc, wproj = weights[layer]
        normed, query, keys, lse, attended = attention
        attended, residual, second, slope, activated, result = out_and_mlp(
            attended, hidden, norms[layer], wout, wfc, wproj
        )
        return result, (hidden, normed, query, keys, attended, lse, residual, second, slope, activated)

    if linked:
        weights, norms, rows_cot, saved_first, first_out, attention = gather_and_forward(
            place, layer_in, cotangent, own_norms, masters, parts, ranks
        )
        norms = (norms[0], norms[1])
    else:
        other_norms = swap_cores(own_norms)
        norms = (per_core(own_norms, other_norms), per_core(other_norms, own_norms))
        rows_in, rows_cot = own_rows(layer_in), own_rows(cotangent)
        weights = gather_weights(masters, parts, ranks)
        first_out, saved_first = forward(rows_in, 0, attend(project_qkv(rows_in, norms[0], weights[0][0])))
        attention = attend(project_qkv(first_out, norms[1], weights[1][0]))
    second_out, saved_second = forward(first_out, 1, attention)

    def backward(upstream, saved, layer, layers, rows):
        wqkv, wout, wfc, wproj = weights[layer]
        hidden, normed, query, keys, attended, lse, residual, second, slope, activated = saved
        d_residual, d_att, vectors_two, *mlp_grads = mlp_back(
            upstream, slope, activated, second, attended, residual, norms[layer], wout, wfc, wproj
        )
        kept, given = mlp_grads[0::2], mlp_grads[1::2]
        if linked:
            d_query, d_keys, sums, home = attention_backward(
                place, query, d_att, lse, keys, kept, given, (4, 5, 2), layers, rows
            )
            d_pair = d_keys[0]
        else:
            d_query, d_keys, _, home = attention_backward(place, query, d_att, lse, keys)
            d_pair = scatter_keys(d_keys)
            sums = plain_sums(kept, given)
        sent, vectors_one, *qkv_grads = qkv_back(d_query, d_pair, normed, hidden, d_residual, norms[layer], wqkv)
        return sent, sums, home, qkv_grads, jnp.stack([vectors_one[0], vectors_two[0], vectors_one[1], vectors_two[1]])

    def plain_sums(kept, given):
        total = [(k.astype(f32) + swap_cores(g).astype(f32)).astype(k.dtype) for k, g in zip(kept, given)]
        return [lax.psum(lax.psum_scatter(t, "dp", scatter_dimension=0), "seq") for t in total]

    def by_rank(vectors):
        return vectors.reshape(4, ranks, -1).transpose(1, 0, 2)

    second_grad, second_sums, layer_results, second_qkv, second_vectors = backward(
        rows_cot, saved_second, 1, (0, 1), (first_out, second_out)
    )
    first_grad, first_sums, grad_home, first_qkv, first_vectors = backward(
        second_grad, saved_first, 0, (1,), (second_grad,)
    )
    kept = [second_qkv[0], by_rank(per_core(first_vectors, second_vectors)), first_qkv[0]]
    given = [second_qkv[1], by_rank(per_core(second_vectors, first_vectors)), first_qkv[1]]
    if linked:
        (second_last, vectors, first_last), first_home, other = reduce_last(
            kept, given, (5, 1, 5), (1, None, 0), first_grad, first_sums, second_sums
        )
        grad_results = per_core(first_home, grad_home)
    else:
        second_last, vectors, first_last = plain_sums(kept, given)
        layer_results = back_home(first_out, second_out)
        grad_results = back_home(first_grad, second_grad)
    first_sums = list(first_sums) + [first_last]
    second_sums = list(second_sums) + [second_last]
    if not linked:
        other = [swap_cores(per_core(b, a)) for a, b in zip(first_sums, second_sums)]
    shapes = [w_proj.shape[1:], w_fc.shape[1:], w_out.shape[1:], w_qkv.shape[1:]]
    g_proj, g_fc, g_out, g_qkv = finish(first_sums, second_sums, other, shapes, (1, ranks, 1, 3))
    return (
        layer_results[None, :, None],
        grad_results[None, :, None],
        g_qkv[None],
        g_out[None],
        g_fc[None],
        g_proj[None],
        vectors[:2][None],
        vectors[2:][None],
    )


def solution(mesh):
    return jax.shard_map(
        on_device,
        mesh=mesh,
        in_specs=(
            P(None, "dp", "seq", None),
            P(None, "dp", "seq", None),
            P(None, "dp"),
            P(),
            P("section", "dp", None),
            P("section", "dp", None),
            P("section", "dp", None),
            P("section", "dp", None),
            P("section", None, None),
            P("section", None, None),
        ),
        out_specs=(
            P("section", None, "dp", "seq", None),
            P("section", None, "dp", "seq", None),
            P("section", "dp", None),
            P("section", "dp", None),
            P("section", "dp", None),
            P("section", "dp", None),
            P("section", None, "dp"),
            P("section", None, "dp"),
        ),
        check_vma=False,
    )
```

```python
import functools
import math

import jax
import jax.numpy as jnp
from jax import lax
from jax.experimental import pallas as pl
from jax.experimental.pallas import tpu as pltpu
from jax.sharding import PartitionSpec as P

HEADS = 20
HEAD_DIM = 56
EPS = 1e-05
NEG = -1e30
LANES = 128
WINDOW = 256
VMEM_LIMIT = 58 * 1024 * 1024
MESH = pl.DeviceIdType.MESH

bf16 = jnp.bfloat16
f32 = jnp.float32


def round_up(size, grain):
    return -(-size // grain) * grain


def dot_nn(left, right):
    return lax.dot_general(left, right, (((1,), (0,)), ((), ())), preferred_element_type=f32)


def dot_nt(left, right):
    return lax.dot_general(left, right, (((1,), (1,)), ((), ())), preferred_element_type=f32)


def dot_tn(left, right):
    return lax.dot_general(left, right, (((0,), (0,)), ((), ())), preferred_element_type=f32)


LINKED = 4


def greet(*places):
    barrier = pltpu.get_barrier_semaphore()
    for place in places:
        pl.semaphore_signal(barrier, inc=1, device_id=place, device_id_type=MESH)
    pl.semaphore_wait(barrier, len(places))


def remote_copy(source, target, send, recv, **place):
    return pltpu.make_async_remote_copy(
        src_ref=source, dst_ref=target, send_sem=send, recv_sem=recv, device_id=place, device_id_type=MESH
    )


def pair_places():
    z = lax.axis_index("seq")
    return {"seq": z + 1 - 2 * lax.rem(z, 2)}, {"section": 1 - lax.axis_index("section")}


def partners():
    core = lax.axis_index("section")
    rank = lax.axis_index("dp")
    x, y = lax.rem(rank, 2), rank // 2
    near = lax.rem(y + core, 2) * 2 + lax.rem(x + 1 - core, 2)
    far = lax.rem(y + 1 - core, 2) * 2 + lax.rem(x + core, 2)
    return near, far, 3 - rank


def vmem_specs(count):
    return [pl.BlockSpec(memory_space=pltpu.VMEM)] * count


def any_specs(count):
    return [pl.BlockSpec(memory_space=pl.ANY)] * count


def sum_of(parts):
    return functools.reduce(jnp.add, parts)


def load_all(copies):
    for copy in copies:
        copy.start()


class Reduction:
    def __init__(self, arrays, parts):
        self.arrays = [(a.shape, a.dtype) for a in arrays]
        self.chunks = []
        for index, (shape, _) in enumerate(self.arrays):
            step = round_up(-(-shape[1] // parts[index]), 16)
            self.chunks += [(index, a, min(step, shape[1] - a)) for a in range(0, shape[1], step)]
        self.count = len(self.chunks)
        self.classes, self.places = {}, []
        for array, _, rows in self.chunks:
            (_, _, columns), dtype = self.arrays[array]
            key = (columns > 2048, str(dtype))
            most = self.classes.setdefault(key, [0, 0, 0, dtype])
            self.places.append((list(self.classes).index(key), most[0]))
            most[:3] = [most[0] + 1, max(most[1], rows), max(most[2], columns)]

    def out_shapes(self):
        return tuple(jax.ShapeDtypeStruct(shape[1:], dtype) for shape, dtype in self.arrays)

    def scratch(self):
        sizes = [((rows, self.arrays[a][0][2]), self.arrays[a][1]) for a, _, rows in self.chunks]
        many = [pltpu.VMEM((4,) + s, t) for s, t in sizes] + [pltpu.VMEM((2,) + s, t) for s, t in sizes]
        single = [pltpu.VMEM(s, t) for s, t in sizes] * 3
        slots = [pltpu.VMEM((4,) + tuple(c[1:3]), c[3]) for c in self.classes.values() for _ in range(2)]
        n = self.count
        dma = pltpu.SemaphoreType.DMA
        sems = [dma((n, 4)), dma((n, 4)), dma((n, 4)), dma((n, 3)), dma((n, 3)), dma((n, 3)), dma((n, 3))]
        return many + single + slots + sems + [pltpu.SemaphoreType.REGULAR((len(self.classes),))]

    def bind(self, kept, given, results, scratch):
        n, k = self.count, len(self.classes)
        self.kept, self.given, self.results = kept, given, results
        self.here, self.came, self.far_in, self.z_in, self.z_mid = (scratch[i * n:(i + 1) * n] for i in range(5))
        self.slots, rest = scratch[5 * n:5 * n + 2 * k], scratch[5 * n + 2 * k:]
        (self.load_sem, self.core_send, self.core_recv, self.dp_send, self.dp_recv, self.z_send, self.z_recv, self.free) = rest
        z = lax.axis_index("seq")
        self.rank = lax.axis_index("dp")
        self.near, self.far, self.across = partners()
        self.inner = (z == 1) | (z == 2)
        self.pair_z, self.other_z = z + 1 - 2 * lax.rem(z, 2), 3 - z
        self.other_core = {"section": 1 - lax.axis_index("section")}
        self.settled = lambda chunk: None

    def peers(self):
        return [{"dp": self.near}, {"dp": self.far}, {"seq": self.pair_z}, {"seq": self.other_z}, self.other_core]

    def loads(self, c):
        array, row, rows = self.chunks[c]
        return [
            pltpu.make_async_copy(
                self.kept[array].at[block, pl.ds(row, rows)], self.here[c].at[i], self.load_sem.at[c, i]
            )
            for i, block in enumerate((self.near, self.across, self.far, self.rank))
        ]

    def slot(self, c, index):
        array, _, rows = self.chunks[c]
        kind, at = self.places[c]
        return self.slots[2 * kind + at % 2].at[index, pl.ds(0, rows), pl.ds(0, self.arrays[array][0][2])]

    def to_core(self, c):
        array, row, rows = self.chunks[c]
        return [
            remote_copy(
                self.given[array].at[block, pl.ds(row, rows)],
                self.slot(c, i),
                self.core_send.at[c, i],
                self.core_recv.at[c, i],
                **self.other_core,
            )
            for i, block in enumerate((self.far, self.across, self.near, self.rank))
        ]

    def nears(self, c):
        return [
            remote_copy(self.here[c].at[i], self.came[c].at[i], self.dp_send.at[c, i], self.dp_recv.at[c, i], dp=self.near)
            for i in range(2)
        ]

    def fars(self, c):
        return remote_copy(self.here[c].at[2], self.far_in[c], self.dp_send.at[c, 2], self.dp_recv.at[c, 2], dp=self.far)

    def along(self, c, k):
        source = self.z_mid[c] if k == 2 else self.here[c].at[3]
        target = self.z_mid[c] if k == 1 else self.z_in[c]
        place = self.other_z if k == 1 else self.pair_z
        return remote_copy(source, target, self.z_send.at[c, k], self.z_recv.at[c, k], seq=place)

    def add(self, c, index, *others):
        here = self.here[c]
        total = here[index].astype(f32)
        for other in others:
            total = total + other[...].astype(f32)
        here[index] = total.astype(here.dtype)

    def store(self, c, value):
        array, row, rows = self.chunks[c]
        self.results[array][pl.ds(row, rows)] = value
        self.settled(c)

    def open(self):
        for c in range(self.count):
            load_all(self.loads(c))

    def give(self, c=0):
        kind, at = self.places[c]
        if at >= 2:
            pl.semaphore_wait(self.free.at[kind], 1)
        load_all(self.to_core(c))

    def begin(self, c):
        for copy in self.loads(c):
            copy.wait()
        for copy in self.to_core(c):
            copy.wait_recv()
        for i in range(2):
            self.add(c, i, self.slot(c, i))
        load_all(self.nears(c))
        for i in (2, 3):
            self.add(c, i, self.slot(c, i))
        kind, at = self.places[c]
        if (kind, at + 2) in self.places:
            pl.semaphore_signal(self.free.at[kind], inc=1, device_id=self.other_core, device_id_type=MESH)
        if c + 2 < self.count:
            self.give(c + 2)

    def after_near(self, c):
        for copy in self.nears(c):
            copy.wait()
        self.add(c, 2, self.came[c].at[1])
        self.fars(c).start()

    def after_far(self, c):
        self.fars(c).wait()
        self.add(c, 3, self.came[c].at[0], self.far_in[c])
        pl.when(jnp.logical_not(self.inner))(self.along(c, 0).start)

    def after_inward(self, c):
        pl.when(jnp.logical_not(self.inner))(self.along(c, 0).wait_send)

        @pl.when(self.inner)
        def add():
            self.along(c, 0).wait_recv()
            self.add(c, 3, self.z_in[c])
            self.along(c, 1).start()

    def after_middle(self, c):
        @pl.when(self.inner)
        def add():
            self.along(c, 1).wait()
            total = self.here[c][3].astype(f32) + self.z_mid[c][...].astype(f32)
            self.z_mid[c][...] = total.astype(self.z_mid[c].dtype)
            self.along(c, 2).start()
            self.store(c, self.z_mid[c][...])

    def after_outward(self, c):
        pl.when(self.inner)(self.along(c, 2).wait_send)

        @pl.when(jnp.logical_not(self.inner))
        def take():
            self.along(c, 2).wait_recv()
            self.store(c, self.z_in[c][...])

        for copy in self.to_core(c):
            copy.wait_send()

    def turns(self):
        steps = (self.begin, self.after_near, self.after_far, self.after_inward, self.after_middle, self.after_outward)

        def turn(number):
            for lag, step in enumerate(steps):
                if 0 <= number - lag < self.count:
                    step(number - lag)

        return [functools.partial(turn, number) for number in range(self.count + len(steps) - 1)]


class Homes:
    def __init__(self, items):
        self.items = items
        self.count = 1 + max(target for _, target in items)

    def out_shapes(self, rows):
        return (jax.ShapeDtypeStruct((2,) + rows.shape, rows.dtype),) * self.count

    def scratch(self):
        dma = pltpu.SemaphoreType.DMA
        n = len(self.items)
        return [dma((n, 2)), dma((n, 2)), dma((n,))]

    def bind(self, rows, homes, scratch):
        self.rows, self.homes = rows, homes
        self.send, self.recv, self.local = scratch
        z = lax.axis_index("seq")
        self.group = z // 2
        self.swapped = z + 2 - 4 * self.group
        self.first_core = lax.axis_index("section") == 0

    def peers(self):
        return [{"section": section, "seq": self.swapped} for section in range(2)]

    def target(self, i):
        return self.homes[self.items[i][1]].at[self.group]

    def stays(self, i):
        return pltpu.make_async_copy(self.rows[i], self.target(i), self.local.at[i])

    def beside(self, i):
        return remote_copy(self.rows[i], self.target(i), self.send.at[i, 0], self.recv.at[i, 0], section=1)

    def away(self, i):
        layer = self.items[i][0]
        return remote_copy(
            self.rows[i], self.target(i), self.send.at[i, 1], self.recv.at[i, 1], section=layer, seq=self.swapped
        )

    def start(self):
        @pl.when(self.first_core)
        def first():
            for i, (layer, _) in enumerate(self.items):
                (self.stays(i) if layer == 0 else self.beside(i)).start()

        @pl.when(jnp.logical_not(self.first_core))
        def second():
            for i in range(len(self.items)):
                self.away(i).start()

    def finish(self):
        @pl.when(self.first_core)
        def first():
            for i, (layer, _) in enumerate(self.items):
                if layer == 0:
                    self.stays(i).wait()
                    self.away(i).wait_recv()
                else:
                    self.beside(i).wait_send()

        @pl.when(jnp.logical_not(self.first_core))
        def second():
            for i, (layer, _) in enumerate(self.items):
                self.away(i).wait_send()
                if layer == 1:
                    self.beside(i).wait_recv()
                    self.away(i).wait_recv()


HEAD_GROUPS = ((0, 6), (6, 6), (12, 6), (18, 2))
LANES_IN = ((0, 384), (384, 384), (768, 256), (1024, 128))
BACKWARD_ORDER = (
    "p", "p", "t", "p", "s0", "p", "t", "p", "a0", "p", "t", "s1", "p", "a1", "p", "t", "p", "s2", "p", "a2",
    "s3", "t", "t", "a3", "t", "t", "t", "z",
)
LANES_OUT = ((0, 256), (256, 384), (640, 256), (896, 256))


def window_in(group, head):
    return head // 3 if group == 0 else (7 * head - 10) // 16


def window_out(group, head):
    return 7 if group == 3 else 7 * head // 16


def head_window(head, tile, rows):
    start = pl.multiple_of(tile * LANES, LANES)
    lane = lax.broadcasted_iota(jnp.int32, (rows, WINDOW), 1) + (start - head * HEAD_DIM)
    return pl.ds(start, WINDOW), (lane >= 0) & (lane < HEAD_DIM)


def two_heads(group, step, work):
    def pair(i, carry):
        work(group, 2 * i)
        work(group, 2 * i + 1)
        return carry

    lax.fori_loop(step, step + 1, pair, 0)


def heads_of(group, work):
    first, count = HEAD_GROUPS[group]

    def pair(step, carry):
        work(group, first + 2 * step)
        work(group, first + 2 * step + 1)
        return carry

    lax.fori_loop(0, count // 2, pair, 0)


def fill_bias(bias, place, row_axis):
    blocks, tokens, _ = bias.shape
    row = lax.broadcasted_iota(jnp.int32, (tokens, tokens), row_axis) + place[1]
    for b in range(blocks):
        column = lax.broadcasted_iota(jnp.int32, (tokens, tokens), 1 - row_axis) + place[1 + b]
        bias[b] = jnp.where((column <= row) & (column < place[0]), 0.0, NEG)


def attention_steps(place, q_ref, kv_refs, o_pad, lse_rows, lse_ref, bias, links):
    tokens, blocks = q_ref.shape[0], len(kv_refs)
    scale = HEAD_DIM ** -0.5
    groups = range(len(HEAD_GROUPS))

    def copies(group):
        send, recv = links
        along, beside = pair_places()
        lanes = (slice(None), slice(None), pl.ds(*LANES_IN[group]))

        def copy(k, source, target, place):
            return remote_copy(
                kv_refs[source].at[lanes], kv_refs[target].at[lanes], send.at[group, k], recv.at[group, k], **place
            )

        return copy(0, 0, 1, along), copy(1, 0, 2, beside), copy(2, 1, 3, beside)

    def start():
        if links:
            for group in groups:
                copies(group)[0].start()
                copies(group)[1].start()
        o_pad[...] = jnp.zeros(o_pad.shape, o_pad.dtype)
        fill_bias(bias, place, 0)
        lse_ref[...] = jnp.zeros(lse_ref.shape, f32)

    def one_head(group, head):
        lse_lane = lax.broadcasted_iota(jnp.int32, lse_ref.shape, 1)
        lanes, inside = head_window(head, window_in(group, head), tokens)
        query = jnp.where(inside, q_ref[:, lanes], 0).astype(bf16)
        scores = [dot_nt(query, kv_refs[b][0, :, lanes]) * scale + bias[b] for b in range(blocks)]
        peak = jnp.max(functools.reduce(jnp.maximum, scores), axis=1, keepdims=True)
        weights = [jnp.exp(s - peak) for s in scores]
        total = jnp.sum(functools.reduce(jnp.add, weights), axis=1, keepdims=True)
        share = 1.0 / total
        out = sum_of([dot_nn((w * share).astype(bf16), kv_refs[b][1, :, lanes]) for b, w in enumerate(weights)])
        o_pad[:, lanes] = jnp.where(inside, out, o_pad[:, lanes].astype(f32)).astype(bf16)
        lse_ref[...] = jnp.where(lse_lane == head, peak + jnp.log(total), lse_ref[...])

    def work(group):
        if links:
            first, second, third = copies(group)
            first.wait_recv()
            third.start()
            second.wait_recv()
            third.wait_recv()
        heads_of(group, one_head)

    def end():
        lse_rows[...] = jnp.transpose(lse_ref[...])
        if links:
            for group in groups:
                for copy in copies(group):
                    copy.wait_send()

    return start, work, end


def attention_forward_kernel(blocks, place, q_ref, *refs):
    o_ref, lse_rows, lse_ref, bias = refs[blocks:]
    start, work, end = attention_steps(place, q_ref, refs[:blocks], o_ref, lse_rows, lse_ref, bias, ())
    start()
    for group in range(len(HEAD_GROUPS)):
        work(group)
    end()


def attention_forward(place, query, kv_blocks, blocks):
    tokens, width = query.shape
    results = pl.pallas_call(
        functools.partial(attention_forward_kernel, blocks),
        out_shape=(
            jax.ShapeDtypeStruct((tokens, width), bf16),
            jax.ShapeDtypeStruct((LANES, tokens), f32),
        ),
        in_specs=[pl.BlockSpec(memory_space=pltpu.SMEM)] + vmem_specs(1 + len(kv_blocks)),
        out_specs=tuple(vmem_specs(2)),
        scratch_shapes=[pltpu.VMEM((tokens, LANES), f32), pltpu.VMEM((blocks, tokens, tokens), f32)],
        compiler_params=pltpu.CompilerParams(vmem_limit_bytes=VMEM_LIMIT),
        cost_estimate=pl.CostEstimate(
            flops=4 * HEADS * tokens * tokens * blocks * WINDOW,
            bytes_accessed=60_000_000,
            transcendentals=HEADS * tokens * tokens * blocks,
        ),
        name="attention_forward",
    )(place, query, *kv_blocks)
    return results[0], results[1], kv_blocks


def attention_backward_kernel(blocks, reduction, going, place, q_ref, d_ref, lse_ref, *refs):
    kv_refs, refs = refs[:blocks], refs[blocks:]
    turns = []
    linked = reduction is not None
    if linked:
        arrays = len(reduction.arrays)
        kept, given, refs = refs[:arrays], refs[arrays:2 * arrays], refs[2 * arrays:]
        rows, refs = refs[:len(going.items)], refs[len(going.items):]
        dq_ref, out_ref, refs = refs[0], refs[1], refs[2:]
        results, refs = refs[:arrays], refs[arrays:]
        homes, refs = refs[:going.count], refs[going.count:]
        dq_pad, bias, grads, from_core, from_pair, send, recv = refs[:7]
        going.bind(rows, homes, refs[7:10])
        reduction.bind(kept, given, results, refs[10:])
        along, beside = pair_places()
        reduction.open()
        greet(*reduction.peers(), *going.peers())
        reduction.give(0)
        reduction.give(1)
        going.start()
        turns = reduction.turns()
    else:
        dq_ref, refs = refs[0], refs[1:]
        out_refs, (dq_pad, bias, grads) = refs[:blocks], refs[blocks:]
    tokens = q_ref.shape[0]
    scale = HEAD_DIM ** -0.5
    dq_pad[...] = jnp.zeros(dq_pad.shape, dq_pad.dtype)
    for b in range(blocks):
        grads[b] = jnp.zeros(grads.shape[1:], grads.dtype)
    fill_bias(bias, place, 1)

    def one_head(group, head):
        lanes, inside = head_window(head, window_out(group, head), tokens)
        query = jnp.where(inside, q_ref[:, lanes], 0).astype(bf16)
        grad = jnp.where(inside, d_ref[:, lanes], 0).astype(bf16)
        lse = lse_ref[pl.ds(head, 1), :]
        probs = [
            jnp.exp(dot_nt(kv_refs[b][0, :, lanes], query) * scale + bias[b] - lse) for b in range(blocks)
        ]
        d_probs = [dot_nt(kv_refs[b][1, :, lanes], grad) for b in range(blocks)]
        inner = jnp.sum(sum_of([p * dp for p, dp in zip(probs, d_probs)]), axis=0, keepdims=True)
        d_query = None
        for b in range(blocks):
            d_score = (probs[b] * (d_probs[b] - inner) * scale).astype(bf16)
            grads[b, 0, :, lanes] = grads[b, 0, :, lanes] + dot_nn(d_score, query).astype(bf16)
            grads[b, 1, :, lanes] = grads[b, 1, :, lanes] + dot_nn(probs[b].astype(bf16), grad).astype(bf16)
            part = dot_tn(d_score, kv_refs[b][0, :, lanes])
            d_query = part if d_query is None else d_query + part
        dq_pad[:, lanes] = jnp.where(inside, d_query, dq_pad[:, lanes].astype(f32)).astype(bf16)

    def lanes_of(group):
        return (slice(None), slice(None), pl.ds(*LANES_OUT[group]))

    def to_core(group, k):
        lanes = lanes_of(group)
        return remote_copy(
            grads.at[2 + k].at[lanes], from_core.at[k].at[lanes], send.at[group, k], recv.at[group, k], **beside
        )

    def to_pair(group):
        lanes = lanes_of(group)
        return remote_copy(
            grads.at[1].at[lanes], from_pair.at[lanes], send.at[group, 2], recv.at[group, 2], **along
        )

    def add_core(group):
        lanes = lanes_of(group)
        for k in (1, 0):
            to_core(group, k).wait_recv()
            mine = grads.at[k]
            mine[lanes] = (mine[lanes].astype(f32) + from_core.at[k][lanes].astype(f32)).astype(bf16)
            if k == 1:
                to_pair(group).start()

    groups = range(len(HEAD_GROUPS))
    if not linked:
        for group in groups:
            heads_of(group, one_head)
        dq_ref[...] = dq_pad[...]
        for b in range(blocks):
            out_refs[b][...] = grads[b]
        return

    def last_add():
        for group in groups:
            lanes = lanes_of(group)
            to_pair(group).wait_recv()
            out_ref[lanes] = (grads.at[0][lanes].astype(f32) + from_pair[lanes].astype(f32)).astype(bf16)

    heads = [(group, (first + h) // 2) for group, (first, count) in enumerate(HEAD_GROUPS) for h in range(0, count, 2)]
    for step in BACKWARD_ORDER:
        if step == "p":
            two_heads(*heads.pop(0), one_head)
        elif step == "t":
            turns.pop(0)()
        elif step == "z":
            last_add()
        elif step[0] == "s":
            to_core(int(step[1]), 1).start()
            to_core(int(step[1]), 0).start()
        else:
            add_core(int(step[1]))
    for turn in turns:
        turn()
    dq_ref[...] = dq_pad[...]
    for group in groups:
        to_core(group, 0).wait_send()
        to_core(group, 1).wait_send()
        to_pair(group).wait_send()
    going.finish()


def attention_backward(place, query, d_out, lse_rows, kv_blocks, kept=(), given=(), parts=(), layers=(), rows=()):
    blocks = len(kv_blocks)
    tokens, width = query.shape
    one = jax.ShapeDtypeStruct((2, tokens, width), bf16)
    reduction = Reduction(kept, parts) if kept else None
    going = Homes([(layer, 0) for layer in layers]) if kept else None
    own = [one] * (1 if kept else blocks)
    dma = pltpu.SemaphoreType.DMA((len(HEAD_GROUPS), 3))
    linked = []
    if kept:
        linked = [pltpu.VMEM((2, 2, tokens, width), bf16), pltpu.VMEM((2, tokens, width), bf16), dma, dma]
        linked += going.scratch() + reduction.scratch()
    results = pl.pallas_call(
        functools.partial(attention_backward_kernel, blocks, reduction, going),
        out_shape=(jax.ShapeDtypeStruct((tokens, width), bf16),)
        + tuple(own)
        + (reduction.out_shapes() + going.out_shapes(rows[0]) if kept else ()),
        in_specs=[pl.BlockSpec(memory_space=pltpu.SMEM)] + vmem_specs(3 + blocks) + any_specs(2 * len(kept) + len(rows)),
        out_specs=tuple(vmem_specs(1 + len(own) + len(kept)) + any_specs(1 if kept else 0)),
        scratch_shapes=[
            pltpu.VMEM((tokens, width), bf16),
            pltpu.VMEM((blocks, tokens, tokens), f32),
            pltpu.VMEM((blocks, 2, tokens, width), bf16),
        ]
        + linked,
        compiler_params=pltpu.CompilerParams(
            vmem_limit_bytes=VMEM_LIMIT, **(dict(collective_id=4 + len(rows), has_side_effects=True) if kept else {})
        ),
        cost_estimate=pl.CostEstimate(
            flops=10 * HEADS * tokens * tokens * blocks * WINDOW,
            bytes_accessed=400_000_000 if kept else 100_000_000,
            transcendentals=HEADS * tokens * tokens * blocks,
        ),
        name="attention_backward",
    )(place, query, d_out, lse_rows, *kv_blocks, *kept, *given, *rows)
    first = 1 + len(own)
    return results[0], list(results[1:first]), list(results[first:first + len(kept)]), results[-1]


def last_kernel(reduction, going, early, layers, *refs):
    arrays, items = len(reduction.arrays), len(going.items)
    kept, given, refs = refs[:arrays], refs[arrays:2 * arrays], refs[2 * arrays:]
    rows, refs = refs[:items], refs[items:]
    sums, refs = (refs[:early], refs[early:2 * early]), refs[2 * early:]
    results, refs = refs[:arrays], refs[arrays:]
    homes, refs = refs[:going.count], refs[going.count:]
    other_half, refs = refs[:early + 1], refs[early + 1:]
    half_send, half_recv, chunk_send, chunk_recv = refs[:4]
    going.bind(rows, homes, refs[4:7])
    reduction.bind(kept, given, results, refs[7:])
    core = lax.axis_index("section")
    first_core = core == 0
    reduction.open()
    greet(*reduction.peers(), *going.peers())
    reduction.give(0)
    reduction.give(1)

    def half(i, layer):
        return remote_copy(sums[layer][i], other_half[i], half_send.at[i], half_recv.at[i], section=1 - core)

    def late_half(c):
        array, row, size = reduction.chunks[c]
        return remote_copy(
            results[array].at[pl.ds(row, size)],
            other_half[early].at[pl.ds(row, size)],
            chunk_send.at[c],
            chunk_recv.at[c],
            section=1 - core,
        )

    def settled(c):
        layer = layers[reduction.chunks[c][0]]
        if layer is not None:
            pl.when(core != layer)(late_half(c).start)

    reduction.settled = settled

    @pl.when(first_core)
    def second_layer():
        for i in range(early):
            half(i, 1).start()

    @pl.when(jnp.logical_not(first_core))
    def first_layer():
        for i in range(early):
            half(i, 0).start()

    going.start()
    for turn in reduction.turns():
        turn()
    for i in range(early):
        half(i, 0).wait()
    for c, (array, _, _) in enumerate(reduction.chunks):
        layer = layers[array]
        if layer is not None:
            pl.when(core != layer)(late_half(c).wait_send)
            pl.when(core == layer)(late_half(c).wait_recv)

    going.finish()


def reduce_last(kept, given, parts, layers, rows, first_sums, second_sums):
    reduction = Reduction(kept, parts)
    going = Homes([(0, 0)])
    early = len(first_sums)
    late = kept[layers.index(0)]
    halves = [jax.ShapeDtypeStruct(v.shape, v.dtype) for v in first_sums]
    halves.append(jax.ShapeDtypeStruct(late.shape[1:], late.dtype))
    n = reduction.count
    dma = pltpu.SemaphoreType.DMA
    out = pl.pallas_call(
        functools.partial(last_kernel, reduction, going, early, layers),
        out_shape=reduction.out_shapes() + going.out_shapes(rows) + tuple(halves),
        in_specs=any_specs(2 * len(kept) + 1 + 2 * early),
        out_specs=tuple(vmem_specs(len(kept)) + any_specs(early + 2)),
        scratch_shapes=[dma((early,)), dma((early,)), dma((n,)), dma((n,))] + going.scratch() + reduction.scratch(),
        compiler_params=pltpu.CompilerParams(
            collective_id=2, has_side_effects=True, vmem_limit_bytes=VMEM_LIMIT
        ),
        cost_estimate=pl.CostEstimate(flops=0, bytes_accessed=400_000_000, transcendentals=0),
        name="reduce_last",
    )(*kept, *given, rows, *first_sums, *second_sums)
    out = list(out)
    return out[:len(kept)], out[len(kept)], out[len(kept) + 1:]


def finish_kernel(parts, *refs):
    kinds = len(parts)
    first, second, other, targets, refs = refs[:kinds], refs[kinds:2 * kinds], refs[2 * kinds:3 * kinds], refs[3 * kinds:4 * kinds], refs[4 * kinds:]
    own, rest, stages, refs = refs[:kinds], refs[kinds:2 * kinds], refs[2 * kinds:3 * kinds], refs[3 * kinds:]
    sems, own_sems, rest_sems = refs
    first_core = lax.axis_index("section") == 0
    for k in range(kinds):
        pl.when(first_core)(pltpu.make_async_copy(first[k], own[k], own_sems.at[k]).start)
        pl.when(jnp.logical_not(first_core))(pltpu.make_async_copy(second[k], own[k], own_sems.at[k]).start)
        pltpu.make_async_copy(other[k], rest[k], rest_sems.at[k]).start()
    for k in range(kinds):
        rows, columns = targets[k].shape
        blocks = max(parts[k], 1)
        half, padded = first[k].shape[0], first[k].shape[1] // blocks
        size = columns // blocks
        pltpu.make_async_copy(first[k], own[k], own_sems.at[k]).wait()
        pltpu.make_async_copy(other[k], rest[k], rest_sems.at[k]).wait()

        def put(top, bottom, k=k, rows=rows, blocks=blocks, half=half, padded=padded, size=size):
            for b in range(blocks):
                here = pl.ds(b * size, size)
                stages[k][pl.ds(0, half), here] = top[:, pl.ds(b * padded, padded)].astype(f32)[:, :size]
                stages[k][pl.ds(half, rows - half), here] = bottom[:, pl.ds(b * padded, padded)].astype(f32)[:rows - half, :size]

        pl.when(first_core)(functools.partial(put, own[k], rest[k]))
        pl.when(jnp.logical_not(first_core))(functools.partial(put, rest[k], own[k]))
        pltpu.make_async_copy(stages[k], targets[k], sems.at[k]).start()
    for k in range(kinds):
        pltpu.make_async_copy(stages[k], targets[k], sems.at[k]).wait()


def finish(first, second, other, shapes, parts):
    kinds = len(first)
    return pl.pallas_call(
        functools.partial(finish_kernel, parts),
        out_shape=tuple(jax.ShapeDtypeStruct(s, f32) for s in shapes),
        in_specs=any_specs(3 * kinds),
        out_specs=tuple(any_specs(kinds)),
        scratch_shapes=[pltpu.VMEM(v.shape, bf16) for v in first] * 2
        + [pltpu.VMEM(s, f32) for s in shapes]
        + [pltpu.SemaphoreType.DMA((kinds,))] * 3,
        compiler_params=pltpu.CompilerParams(vmem_limit_bytes=VMEM_LIMIT),
        name="finish",
    )(*first, *second, *other)


def padded_shape(weight, parts):
    rows, columns = weight.shape
    rows = round_up(rows, LANES) if parts == 0 else round_up(rows, 32)
    return rows, columns if parts < 2 else parts * round_up(columns // parts, LANES)


STAGE_ROWS = 9


class Gather:
    def __init__(self, masters, parts, over_seq):
        self.parts, self.kinds, self.over_seq = parts, len(masters), over_seq
        self.shapes = [padded_shape(m, p) for m, p in zip(masters, parts)]
        self.wide_shapes = []
        for m in masters:
            rows = round_up(-(-m.shape[0] // STAGE_ROWS), 16)
            self.wide_shapes.append((2, rows, m.shape[1]))

    def out_shapes(self, ranks):
        return tuple(jax.ShapeDtypeStruct((ranks,) + s, bf16) for s in self.shapes) * 2

    def scratch(self):
        dma = pltpu.SemaphoreType.DMA
        n = 2 * self.kinds
        return (
            [pltpu.VMEM(s, f32) for s in self.wide_shapes]
            + [pltpu.VMEM(s, bf16) for s in self.shapes] * 2
            + [dma((self.kinds, 2)), dma((n,)), dma((n, 10)), dma((n, 10))]
        )

    def bind(self, masters, whole, scratch):
        n = self.kinds
        self.masters, self.whole = masters, whole
        self.wide, self.shares, self.got = scratch[:n], scratch[n:2 * n], scratch[2 * n:3 * n]
        self.wide_sem, self.own_sem, self.send, self.recv = scratch[3 * n:]
        self.core = lax.axis_index("section")
        self.rank = lax.axis_index("dp")
        z = lax.axis_index("seq")
        self.near, self.far, self.across = partners()
        self.parity = lax.rem(z, 2)
        self.pair_z = z + 1 - 2 * self.parity

    def peers(self):
        return [{"dp": self.near}, {"dp": self.far}, {"seq": self.pair_z}, {"section": 1 - self.core}]

    def rows_of(self, u, start, size):
        half = self.whole[u].shape[1] // 2
        return pl.ds(pl.multiple_of(self.core * half + start, 16), size)

    def copy(self, u, k, block, start, size, **place):
        ref = self.whole[u].at[block, self.rows_of(u, start, size)]
        return remote_copy(ref, ref, self.send.at[u, k], self.recv.at[u, k], **place)

    def sizes(self, u):
        half = self.whole[u].shape[1] // 2
        rest = round_up(half * self.over_seq[u] // 9, 16)
        return half - rest, rest

    def to_dp(self, u, k, source=None):
        size, rest = self.sizes(u)
        block, place = ((self.rank, self.near), (self.rank, self.far), (self.far, self.near))[k]
        rows = self.rows_of(u, self.parity * rest, size)
        target = self.whole[u].at[block, rows]
        source = target if source is None else source.at[rows]
        return remote_copy(source, target, self.send.at[u, k], self.recv.at[u, k], dp=place)

    def to_pair(self, u, k):
        size, rest = self.sizes(u)
        block = (self.near, self.far, self.across)[k]
        return self.copy(u, 3 + k, block, self.parity * size, rest, seq=self.pair_z)

    def to_core(self, u, k):
        half = self.whole[u].shape[1] // 2
        return self.copy(u, 6 + k, (self.near, self.far, self.across)[k], 0, half, section=1 - self.core)

    def given(self, u):
        kind = u % self.kinds
        return remote_copy(
            self.shares[kind], self.got[kind], self.send.at[u, 9], self.recv.at[u, 9], section=1 - self.core
        )

    def kept(self, u, source):
        return pltpu.make_async_copy(source[u % self.kinds], self.whole[u].at[self.rank], self.own_sem.at[u])

    def stages(self, kind):
        rows, step = self.masters[kind].shape[0], self.wide_shapes[kind][1]
        return [(i % 2, a, min(step, rows - a)) for i, a in enumerate(range(0, rows, step))]

    def load(self, kind, stage):
        slot, first, size = stage
        return pltpu.make_async_copy(
            self.masters[kind].at[pl.ds(first, size)],
            self.wide[kind].at[slot, pl.ds(0, size)],
            self.wide_sem.at[kind, slot],
        )

    def open(self):
        for kind in range(self.kinds):
            for stage in self.stages(kind)[:2]:
                self.load(kind, stage).start()

    def cast(self, kind):
        share, wide = self.shares[kind], self.wide[kind]
        blocks = max(self.parts[kind], 1)
        size, padded = wide.shape[2] // blocks, share.shape[1] // blocks
        share[...] = jnp.zeros(share.shape, bf16)
        stages = self.stages(kind)
        for i, (slot, first, count) in enumerate(stages):
            self.load(kind, stages[i]).wait()
            for b in range(blocks):
                value = wide[slot, pl.ds(0, count), b * size:(b + 1) * size]
                share[pl.ds(first, count), pl.ds(b * padded, size)] = value.astype(bf16)
            if i + 2 < len(stages):
                self.load(kind, stages[i + 2]).start()

    def first(self, u):
        if u < self.kinds:
            self.cast(u)
            pl.when(self.core == 0)(self.given(u).start)
        if 2 <= u < self.kinds + 2:
            pl.when(self.core == 1)(self.given(u + 2).start)

        def send_from(source):
            self.to_dp(u, 1, source[u % self.kinds]).start()
            self.to_dp(u, 0, source[u % self.kinds]).start()
            self.kept(u, source).start()

        @pl.when(self.core == u // self.kinds)
        def own():
            send_from(self.shares)

        @pl.when(self.core != u // self.kinds)
        def other():
            self.given(u).wait_recv()
            send_from(self.got)

    def second(self, u):
        self.to_dp(u, 1).wait_recv()
        self.to_dp(u, 2).start()
        self.to_pair(u, 1).start()
        self.to_dp(u, 0).wait_recv()
        self.to_pair(u, 0).start()

    def third(self, u):
        self.to_dp(u, 2).wait_recv()
        self.to_pair(u, 2).start()
        for k in (1, 0):
            self.to_pair(u, k).wait_recv()
            self.to_core(u, k).start()

    def fourth(self, u):
        self.to_pair(u, 2).wait_recv()
        self.to_core(u, 2).start()

    def last(self, u):
        for k in range(3):
            self.to_core(u, k).wait()
            self.to_pair(u, k).wait_send()
        self.to_dp(u, 0, self.shares[u % self.kinds]).wait_send()
        self.to_dp(u, 1, self.shares[u % self.kinds]).wait_send()
        self.to_dp(u, 2).wait_send()
        self.kept(u, self.shares).wait()

        @pl.when(self.core == u // self.kinds)
        def gave():
            self.given(u).wait_send()

    def turns(self):
        steps = (self.first, self.second, self.third, self.fourth, self.last)
        units = 2 * self.kinds

        def turn(number):
            for lag, step in enumerate(steps):
                if 0 <= number - lag < units:
                    step(number - lag)

        return [functools.partial(turn, number) for number in range(units + len(steps) - 1)]


def gather_kernel(gather, *refs):
    kinds = gather.kinds
    gather.bind(refs[:kinds], refs[kinds:3 * kinds], refs[3 * kinds:])
    gather.open()
    greet(*gather.peers())
    for turn in gather.turns():
        turn()


def gather_weights(masters, parts, ranks):
    kinds = len(masters)
    gather = Gather(masters, parts, (3,) * (2 * kinds))
    results = pl.pallas_call(
        functools.partial(gather_kernel, gather),
        out_shape=gather.out_shapes(ranks),
        in_specs=any_specs(kinds),
        out_specs=tuple(any_specs(2 * kinds)),
        scratch_shapes=gather.scratch(),
        compiler_params=pltpu.CompilerParams(
            collective_id=1, has_side_effects=True, vmem_limit_bytes=VMEM_LIMIT
        ),
        cost_estimate=pl.CostEstimate(flops=0, bytes_accessed=700_000_000, transcendentals=0),
        name="gather_weights",
    )(*masters)
    return results[:kinds], results[kinds:]


def norm_parts(values):
    center = values - jnp.mean(values, axis=-1, keepdims=True)
    inverse = lax.rsqrt(jnp.mean(center * center, axis=-1, keepdims=True) + EPS)
    return center * inverse, inverse


def norm_back(values, gain, upstream):
    unit, inverse = norm_parts(values)
    weighted = upstream * gain
    grad = inverse * (
        weighted
        - jnp.mean(weighted, axis=-1, keepdims=True)
        - unit * jnp.mean(weighted * unit, axis=-1, keepdims=True)
    )
    return grad, jnp.sum(upstream * unit, axis=0, keepdims=True), jnp.sum(upstream, axis=0, keepdims=True)


def block_loads(source, target, sems, row):
    return [
        pltpu.make_async_copy(source.at[b], target.at[b], sems.at[row, b]) for b in range(source.shape[0])
    ]


def split_columns(target, value, beside=None):
    ranks, _, padded = target.shape
    share = value.shape[1] // ranks
    target[...] = jnp.zeros(target.shape, target.dtype)
    if beside is not None:
        beside[...] = jnp.zeros(beside.shape, beside.dtype)
    for b in range(ranks):
        part = value[:, b * share:(b + 1) * share]
        target[b, :, pl.ds(0, share)] = part
        if beside is not None:
            beside[:, pl.ds(b * padded, share)] = part


def one_product(beside, weight):
    ranks, rows, columns = weight.shape
    return dot_nn(beside[...], weight.reshape(ranks * rows, columns))


def join_columns(target, parts):
    share = target.shape[1] // len(parts)
    for b, part in enumerate(parts):
        target[:, b * share:(b + 1) * share] = part[:, :share]


def qkv_kernel(h_ref, norm_ref, w_ref, a_ref, q_ref, kv_ref, w_mem, sems):
    ranks = w_ref.shape[0]
    loads = block_loads(w_ref, w_mem, sems, 0)
    load_all(loads)
    unit, _ = norm_parts(h_ref[...].astype(f32))
    split_columns(a_ref, (unit * norm_ref[0:1] + norm_ref[2:3]).astype(bf16))
    block = q_ref.shape[1]
    for copy in loads:
        copy.wait()
    for part, target in enumerate((q_ref, kv_ref.at[0], kv_ref.at[1])):
        total = sum_of([dot_nn(a_ref[b], w_mem[b, :, pl.ds(part * block, block)]) for b in range(ranks)])
        target[...] = total.astype(bf16)


def project_qkv(hidden, norm, weight):
    tokens = hidden.shape[0]
    ranks, rows, columns = weight.shape
    return pl.pallas_call(
        qkv_kernel,
        out_shape=(
            jax.ShapeDtypeStruct((ranks, tokens, rows), bf16),
            jax.ShapeDtypeStruct((tokens, columns // 3), bf16),
            jax.ShapeDtypeStruct((2, tokens, columns // 3), bf16),
        ),
        in_specs=vmem_specs(2) + any_specs(1),
        out_specs=tuple(vmem_specs(3)),
        scratch_shapes=[pltpu.VMEM(weight.shape, bf16), pltpu.SemaphoreType.DMA((1, ranks))],
        compiler_params=pltpu.CompilerParams(vmem_limit_bytes=VMEM_LIMIT),
        cost_estimate=pl.CostEstimate(
            flops=2 * tokens * weight.size, bytes_accessed=2 * weight.size, transcendentals=tokens
        ),
        name="project_qkv",
    )(hidden, norm, weight)


def mlp_kernel(
    o_ref, h_ref, norm_ref, wo_ref, wf_ref, wp_ref,
    ob_ref, r_ref, c_ref, slope_ref, g_ref, out_ref,
    wo, wf, wp, beside, sems,
):
    ranks = wo.shape[0]
    loads = [block_loads(s, t, sems, i) for i, (s, t) in enumerate(((wo_ref, wo), (wf_ref, wf), (wp_ref, wp)))]
    for some in loads:
        load_all(some)
    split_columns(ob_ref, o_ref[:, pl.ds(0, h_ref.shape[1])], beside)
    for copy in loads[0]:
        copy.wait()
    r_ref[...] = h_ref[...].astype(f32) + one_product(beside, wo[...])
    unit, _ = norm_parts(r_ref[...])
    split_columns(c_ref, (unit * norm_ref[1:2] + norm_ref[3:4]).astype(bf16), beside)
    for copy in loads[1]:
        copy.wait()
    block = g_ref.shape[2]
    step = block // 3

    def columns(i, carry):
        at = pl.multiple_of(i * step, LANES)
        pre = one_product(beside, wf[:, :, pl.ds(at, step)])
        within = pl.ds(pl.multiple_of(lax.rem(i, 3) * step, LANES), step)
        g_ref[i // 3, :, within], slope_ref[i // 3, :, within] = gelu_parts(pre)
        return carry

    lax.fori_loop(0, 3 * ranks, columns, 0)
    for copy in loads[2]:
        copy.wait()
    out_ref[...] = (r_ref[...] + sum_of([dot_nn(g_ref[b], wp[b]) for b in range(ranks)])).astype(bf16)


def out_and_mlp(attended, hidden, norm, w_out, w_fc, w_proj):
    tokens, width = hidden.shape
    ranks, rows, _ = w_out.shape
    ff = w_proj.shape[1]
    flat = jax.ShapeDtypeStruct((ranks, tokens, rows), bf16)
    size = w_out.size + w_fc.size + w_proj.size
    return pl.pallas_call(
        mlp_kernel,
        out_shape=(
            flat,
            jax.ShapeDtypeStruct((tokens, width), f32),
            flat,
            jax.ShapeDtypeStruct((ranks, tokens, ff), f32),
            jax.ShapeDtypeStruct((ranks, tokens, ff), bf16),
            jax.ShapeDtypeStruct((tokens, width), bf16),
        ),
        in_specs=vmem_specs(3) + any_specs(3),
        out_specs=tuple(vmem_specs(6)),
        scratch_shapes=[
            pltpu.VMEM(w_out.shape, bf16),
            pltpu.VMEM(w_fc.shape, bf16),
            pltpu.VMEM(w_proj.shape, bf16),
            pltpu.VMEM((tokens, ranks * rows), bf16),
            pltpu.SemaphoreType.DMA((3, ranks)),
        ],
        compiler_params=pltpu.CompilerParams(vmem_limit_bytes=VMEM_LIMIT),
        cost_estimate=pl.CostEstimate(
            flops=2 * tokens * size, bytes_accessed=2 * size, transcendentals=2 * tokens * ff * ranks
        ),
        name="out_and_mlp",
    )(attended, hidden, norm, w_out, w_fc, w_proj)


def gelu_parts(pre):
    below = 0.5 * (1.0 + lax.erf(pre * math.sqrt(0.5)))
    slope = below + pre * (jnp.exp(-0.5 * pre * pre) * (1.0 / math.sqrt(2.0 * math.pi)))
    return (pre * below).astype(bf16), slope


FORWARD_ORDER = (
    "f0", "f1", "s0", "f2", "t0", "s1", "s2", "40", "f3", "t1", "l0", "f4", "Q0", "t2", "f5", "S0", "s4",
    "s5", "41", "42", "s3", "l1", "O", "A00", "f6", "A01", "A02", "A03", "t3", "t5", "f7", "l2", "W", "43",
    "t4", "M", "44", "s6", "l3", "V", "B0", "B1", "s7", "B2", "45", "l4", "B3", "l5", "t6", "Q1", "S1", "t7",
    "46", "A10", "A11", "A12", "47", "l6", "A13", "l7",
)
FORWARD_OVER_SEQ = (3, 3, 3, 2, 3, 1, 2, 2)


def forward_kernel(gather, place, in_ref, cot_in, own_norms, *refs):
    kinds = gather.kinds
    masters, refs = refs[:kinds], refs[kinds:]
    whole, refs = refs[:2 * kinds], refs[2 * kinds:]
    (a_ref, q_ref, kv_ref, *others), refs = refs[:6], refs[6:]
    (lse_ref, ob_ref, r_ref, c_ref, slope_ref, g_ref, out_ref), refs = refs[:7], refs[7:]
    (first_norms, second_norms, h_ref, cot_ref, next_a, next_q, next_kv, *next_others), refs = refs[:10], refs[10:]
    (next_lse, next_o), refs = refs[:2], refs[2:]
    (rows_send, rows_recv, norm_sem, lse_mem, bias, links_send, links_recv, next_send, next_recv), refs = refs[:9], refs[9:]
    (total, beside, norm_ref, columns_mem, rows_mem, wo, slopes, gs), refs = refs[:8], refs[8:]
    (columns_sem, rows_sem, wo_sem, out_sem), refs = refs[:4], refs[4:]
    gather.bind(masters, whole, refs)
    gather.open()
    core = lax.axis_index("section")
    z = lax.axis_index("seq")
    group = z // 2
    swapped = z + 2 - 4 * group
    greet(*gather.peers(), {"seq": swapped})
    moves = ((in_ref, h_ref), (cot_in, cot_ref))

    def stay(i):
        return pltpu.make_async_copy(moves[i][0].at[group, 0], moves[i][1], rows_send.at[i])

    def move(i):
        return remote_copy(moves[i][0].at[1 - group, 0], moves[i][1], rows_send.at[i], rows_recv.at[i], seq=swapped)

    norms_here = pltpu.make_async_copy(own_norms, norm_ref.at[core], norm_sem.at[0])
    norms_there = remote_copy(own_norms, norm_ref.at[core], norm_sem.at[1], norm_sem.at[2], section=1 - core)
    norms_here.start()
    norms_there.start()

    def rows_arrive(i):
        pl.when(core == 0)(stay(i).wait)
        pl.when(core == 1)(move(i).wait)

    for i in range(2):
        pl.when(core == 0)(stay(i).start)
        pl.when(core == 1)(move(i).start)
    ranks, tokens, rows = a_ref.shape
    block = q_ref.shape[1]

    def load_columns(weight, part):
        slot = part % 2
        return [
            pltpu.make_async_copy(
                weight.at[b, :, pl.ds(part * block, block)], columns_mem.at[slot, b], columns_sem.at[slot, b]
            )
            for b in range(ranks)
        ]

    def load_rows(weight, b):
        return [pltpu.make_async_copy(weight.at[b], rows_mem.at[b % 2], rows_sem.at[b % 2])]

    def wait_all(copies):
        for copy in copies:
            copy.wait()

    def project(hidden, norms, weight, a, q, kv):
        for part in range(2):
            load_all(load_columns(weight, part))
        unit, _ = norm_parts(hidden)
        split_columns(a, (unit * norms[0:1] + norms[2:3]).astype(bf16), beside)
        for part, target in enumerate((q, kv.at[0], kv.at[1])):
            wait_all(load_columns(weight, part))
            target[...] = one_product(beside, columns_mem[part % 2]).astype(bf16)
            if part == 0:
                load_all(load_columns(weight, 2))

    def put_out(b):
        slot = b % 2
        return [
            pltpu.make_async_copy(slopes.at[slot], slope_ref.at[b], out_sem.at[slot, 0]),
            pltpu.make_async_copy(gs.at[slot], g_ref.at[b], out_sem.at[slot, 1]),
        ]

    def mlp_block(b):
        slot = b % 2
        if b >= 2:
            wait_all(put_out(b - 2))
        wait_all(load_columns(whole[2], b))
        third = block // 3

        def some_columns(i, carry):
            at = pl.ds(pl.multiple_of(i * third, LANES), third)
            pre = one_product(beside, columns_mem[slot, :, :, at])
            gs[slot, :, at], slopes[slot, :, at] = gelu_parts(pre)
            return carry

        lax.fori_loop(0, 3, some_columns, 0)
        load_all(put_out(b))
        if b + 2 < ranks:
            load_all(load_columns(whole[2], b + 2))
        wait_all(load_rows(whole[3], b))
        total[...] = total[...] + dot_nn(gs[slot], rows_mem[slot])
        if b + 2 < ranks:
            load_all(load_rows(whole[3], b + 2))

    def attention(layer):
        if layer == 0:
            return attention_steps(
                place, q_ref, [kv_ref] + others, next_o, lse_ref, lse_mem, bias, (links_send, links_recv)
            )
        return attention_steps(
            place, next_q, [next_kv] + next_others, next_o, next_lse, lse_mem, bias, (next_send, next_recv)
        )

    out_loads = [pltpu.make_async_copy(whole[1].at[b], wo.at[b], wo_sem.at[b]) for b in range(ranks)]

    def middle():
        attention(0)[2]()
        split_columns(ob_ref, next_o[:, pl.ds(0, h_ref.shape[1])], beside)
        wait_all(out_loads)
        r_ref[...] = h_ref[...].astype(f32) + one_product(beside, wo[...])
        unit, _ = norm_parts(r_ref[...])
        split_columns(c_ref, (unit * norm_ref[0, 1:2] + norm_ref[0, 3:4]).astype(bf16), beside)
        total[...] = r_ref[...]

    def qkv(layer):
        if layer == 0:
            rows_arrive(0)
            norms_here.wait()
            norms_there.wait()
            first_norms[...] = norm_ref[0]
            second_norms[...] = norm_ref[1]
            project(h_ref[...].astype(f32), norm_ref.at[0], whole[0], a_ref, q_ref, kv_ref)
            return
        for b in range(2, ranks):
            wait_all(put_out(b))
        out_ref[...] = total[...].astype(bf16)
        project(out_ref[...].astype(f32), norm_ref.at[1], whole[kinds], next_a, next_q, next_kv)

    steps = {"f": gather.first, "s": gather.second, "t": gather.third, "4": gather.fourth, "l": gather.last}
    steps.update({"Q": qkv, "S": lambda layer: attention(layer)[0](), "B": mlp_block})
    for step in FORWARD_ORDER:
        if step == "M":
            middle()
        elif step == "O":
            load_all(out_loads)
        elif step == "W":
            for b in range(2):
                load_all(load_columns(whole[2], b))
        elif step == "V":
            for b in range(2):
                load_all(load_rows(whole[3], b))
        elif step[0] == "A":
            attention(int(step[1]))[1](int(step[2]))
        else:
            steps[step[0]](int(step[1]))
    attention(1)[2]()
    rows_arrive(1)


def gather_and_forward(place, layer_in, cotangent, norms, masters, parts, ranks):
    tokens, width = layer_in.shape[2:]
    kinds = len(masters)
    gather = Gather(masters, parts, FORWARD_OVER_SEQ)
    shapes = gather.shapes
    rows, block = shapes[1][0], shapes[0][1] // 3
    ff = shapes[3][0]

    def array(dtype, *shape):
        return jax.ShapeDtypeStruct(shape, dtype)

    flat, two = array(bf16, ranks, tokens, rows), array(bf16, 2, tokens, block)
    one = array(bf16, tokens, block)
    saved = (flat, one, two, two, two, two, array(f32, LANES, tokens), flat, array(f32, tokens, width), flat)
    wide = (array(f32, ranks, tokens, ff), array(bf16, ranks, tokens, ff))
    hidden = array(bf16, tokens, width)
    norm = array(f32, 4, width)
    after = (hidden, norm, norm, hidden, hidden, flat, one, two, two, two, two, array(f32, LANES, tokens), one)
    dma = pltpu.SemaphoreType.DMA
    links = dma((len(HEAD_GROUPS), 3))
    out = pl.pallas_call(
        functools.partial(forward_kernel, gather),
        out_shape=gather.out_shapes(ranks) + saved + wide + after,
        in_specs=[pl.BlockSpec(memory_space=pltpu.SMEM)] + any_specs(2) + vmem_specs(1) + any_specs(kinds),
        out_specs=tuple(
            any_specs(2 * kinds)
            + vmem_specs(len(saved))
            + any_specs(2)
            + vmem_specs(4)
            + any_specs(1)
            + vmem_specs(len(after) - 5)
        ),
        scratch_shapes=[
            dma((2,)),
            dma((2,)),
            dma((3,)),
            pltpu.VMEM((tokens, LANES), f32),
            pltpu.VMEM((LINKED, tokens, tokens), f32),
            links,
            links,
            links,
            links,
            pltpu.VMEM((tokens, width), f32),
            pltpu.VMEM((tokens, ranks * rows), bf16),
            pltpu.VMEM((2, 4, width), f32),
            pltpu.VMEM((2, ranks, rows, block), bf16),
            pltpu.VMEM((2, ff, width), bf16),
            pltpu.VMEM((ranks, rows, width), bf16),
            pltpu.VMEM((2, tokens, ff), f32),
            pltpu.VMEM((2, tokens, ff), bf16),
            dma((2, ranks)),
            dma((2,)),
            dma((ranks,)),
            dma((2, 2)),
        ]
        + gather.scratch(),
        compiler_params=pltpu.CompilerParams(
            collective_id=1, has_side_effects=True, vmem_limit_bytes=VMEM_LIMIT
        ),
        cost_estimate=pl.CostEstimate(flops=0, bytes_accessed=700_000_000, transcendentals=0),
        name="gather_and_forward",
    )(place, layer_in, cotangent, norms, *masters)
    weights, out = (out[:kinds], out[kinds:2 * kinds]), out[2 * kinds:]
    normed, query, own, along, beside, both, lse, attended, residual, second, slope, activated, *out = out
    result, *norms, hidden, cotangent = out[:5]
    out = out[5:]
    saved = (hidden, normed, query, [own, along, beside, both], attended, lse, residual, second, slope, activated)
    normed, query, own, along, beside, both, lse, attended = out
    return weights, norms, cotangent, saved, result, (normed, query, [own, along, beside, both], lse, attended)


class Writer:
    def __init__(self, slots, sems):
        self.slots, self.sems, self.last = slots, sems, [(), ()]
        self.turn = 0

    def put(self, make, keep, give):
        slot = self.turn % 2
        self.turn += 1
        for copy in self.last[slot]:
            copy.wait()
        make(self.slots.at[slot])
        core = lax.axis_index("section")
        half = self.slots.shape[1] // 2
        copies = []
        for i, (target, which) in enumerate(((keep, core), (give, 1 - core))):
            part = self.slots.at[slot, pl.ds(pl.multiple_of(which * half, 16), half)]
            copies.append(pltpu.make_async_copy(part, target, self.sems.at[slot, i]))
        load_all(copies)
        self.last[slot] = copies

    def finish(self):
        for copies in self.last:
            for copy in copies:
                copy.wait()


def all_rows(value, weight):
    ranks, rows, columns = weight.shape
    product = dot_nt(value, weight[...].reshape(ranks * rows, columns))
    return [product[:, b * rows:(b + 1) * rows] for b in range(ranks)]


def product_into(stage, left, right, step):
    columns = right.shape[1]
    for a in range(0, columns, step):
        n = min(step, columns - a)
        stage[:, pl.ds(a, n)] = dot_tn(left[...], right[:, pl.ds(a, n)]).astype(bf16)


def mlp_back_kernel(
    e_ref, slope_ref, g_ref, c_ref, ob_ref, r_ref, norm_ref, wo_ref, wf_ref, wp_ref,
    res_ref, att_ref, vec_ref, p_keep, p_give, f_keep, f_give, o_keep, o_give,
    wo, wf, wp, pre, d_sec, branch, att_mem, p_slots, f_slots, o_slots, sems, p_sems, f_sems, o_sems,
):
    ranks = wo.shape[0]
    loads = [block_loads(s, t, sems, i) for i, (s, t) in enumerate(((wp_ref, wp), (wf_ref, wf), (wo_ref, wo)))]
    for some in loads:
        load_all(some)
    writer = Writer(p_slots, p_sems)
    rows, ff = c_ref.shape[2], g_ref.shape[2]
    width = e_ref.shape[1]
    for b in range(ranks):
        loads[0][b].wait()
        pre[:, pl.ds(b * ff, ff)] = (dot_nt(e_ref[...], wp[b]) * slope_ref[b]).astype(bf16)
        writer.put(
            lambda s, b=b: product_into(s, g_ref.at[b], e_ref, width), p_keep.at[b], p_give.at[b]
        )
    for b in range(ranks):
        loads[1][b].wait()
    join_columns(d_sec, all_rows(pre[...], wf))
    grad, gain, bias = norm_back(r_ref[...], norm_ref[1:2], d_sec[...])
    vec_ref[0:1] = gain
    vec_ref[1:2] = bias
    total = e_ref[...].astype(f32) + grad
    res_ref[...] = total
    branch[...] = total.astype(bf16)
    for b in range(ranks):
        loads[2][b].wait()
    join_columns(att_mem, all_rows(branch[...], wo))
    att_ref[...] = jnp.zeros(att_ref.shape, bf16)
    att_ref[:, pl.ds(0, width)] = att_mem[...].astype(bf16)
    f_writer = Writer(f_slots, f_sems)
    o_writer = Writer(o_slots, o_sems)
    for b in range(ranks):
        f_writer.put(
            lambda s, b=b: product_into(s, c_ref.at[b], pre, ff), f_keep.at[b], f_give.at[b]
        )
        o_writer.put(
            lambda s, b=b: product_into(s, ob_ref.at[b], branch, width), o_keep.at[b], o_give.at[b]
        )
    writer.finish()
    f_writer.finish()
    o_writer.finish()


def half_rows(weight):
    return jax.ShapeDtypeStruct((weight.shape[0], weight.shape[1] // 2, weight.shape[2]), bf16)


def mlp_back(upstream, slope, activated, second, attended, residual, norm, w_out, w_fc, w_proj):
    tokens, width = upstream.shape
    ranks, rows, _ = w_out.shape
    size = w_out.size + w_fc.size + w_proj.size
    return pl.pallas_call(
        mlp_back_kernel,
        out_shape=(
            jax.ShapeDtypeStruct((tokens, width), f32),
            jax.ShapeDtypeStruct((tokens, round_up(width, LANES)), bf16),
            jax.ShapeDtypeStruct((2, width), f32),
        )
        + tuple(half_rows(w) for w in (w_proj, w_proj, w_fc, w_fc, w_out, w_out)),
        in_specs=vmem_specs(7) + any_specs(3),
        out_specs=tuple(vmem_specs(3) + any_specs(6)),
        scratch_shapes=[
            pltpu.VMEM(w_out.shape, bf16),
            pltpu.VMEM(w_fc.shape, bf16),
            pltpu.VMEM(w_proj.shape, bf16),
            pltpu.VMEM((tokens, w_fc.shape[2]), bf16),
            pltpu.VMEM((tokens, width), f32),
            pltpu.VMEM((tokens, width), bf16),
            pltpu.VMEM((tokens, width), f32),
            pltpu.VMEM((2,) + w_proj.shape[1:], bf16),
            pltpu.VMEM((2,) + w_fc.shape[1:], bf16),
            pltpu.VMEM((2,) + w_out.shape[1:], bf16),
            pltpu.SemaphoreType.DMA((3, ranks)),
            pltpu.SemaphoreType.DMA((2, 2)),
            pltpu.SemaphoreType.DMA((2, 2)),
            pltpu.SemaphoreType.DMA((2, 2)),
        ],
        compiler_params=pltpu.CompilerParams(vmem_limit_bytes=VMEM_LIMIT),
        cost_estimate=pl.CostEstimate(
            flops=4 * tokens * size, bytes_accessed=4 * size, transcendentals=tokens
        ),
        name="mlp_backward",
    )(upstream, slope, activated, second, attended, residual, norm, w_out, w_fc, w_proj)


def qkv_back_kernel(
    dq_ref, dkv_ref, a_ref, h_ref, res_ref, norm_ref, w_ref,
    sent_ref, vec_ref, keep, give,
    w_mem, d_proj, d_normed, slots, sems, out_sems,
):
    ranks, rows, columns = w_ref.shape
    loads = block_loads(w_ref, w_mem, sems, 0)
    load_all(loads)
    writer = Writer(slots, out_sems)
    block = columns // 3
    d_proj[:, pl.ds(0, block)] = dq_ref[...]
    d_proj[:, pl.ds(block, block)] = dkv_ref[0]
    d_proj[:, pl.ds(2 * block, block)] = dkv_ref[1]
    for b in range(ranks):
        writer.put(
            lambda s, b=b: product_into(s, a_ref.at[b], d_proj, block), keep.at[b], give.at[b]
        )
    for copy in loads:
        copy.wait()
    join_columns(d_normed, all_rows(d_proj[...], w_mem))
    grad, gain, bias = norm_back(h_ref[...].astype(f32), norm_ref[0:1], d_normed[...])
    vec_ref[0:1] = gain
    vec_ref[1:2] = bias
    sent_ref[...] = (res_ref[...] + grad).astype(bf16)
    writer.finish()


def qkv_back(d_query, d_pair, normed, hidden, residual_grad, norm, weight):
    tokens, width = hidden.shape
    ranks, rows, columns = weight.shape
    return pl.pallas_call(
        qkv_back_kernel,
        out_shape=(
            jax.ShapeDtypeStruct((tokens, width), bf16),
            jax.ShapeDtypeStruct((2, width), f32),
            half_rows(weight),
            half_rows(weight),
        ),
        in_specs=vmem_specs(6) + any_specs(1),
        out_specs=tuple(vmem_specs(2) + any_specs(2)),
        scratch_shapes=[
            pltpu.VMEM(weight.shape, bf16),
            pltpu.VMEM((tokens, columns), bf16),
            pltpu.VMEM((tokens, width), f32),
            pltpu.VMEM((2, rows, columns), bf16),
            pltpu.SemaphoreType.DMA((1, ranks)),
            pltpu.SemaphoreType.DMA((2, 2)),
        ],
        compiler_params=pltpu.CompilerParams(vmem_limit_bytes=VMEM_LIMIT),
        cost_estimate=pl.CostEstimate(
            flops=4 * tokens * weight.size, bytes_accessed=4 * weight.size, transcendentals=tokens
        ),
        name="qkv_backward",
    )(d_query, d_pair, normed, hidden, residual_grad, norm, weight)


def swap_cores(value):
    return lax.ppermute(value, "section", [(0, 1), (1, 0)])


def send_joint(value, axis, route):
    size = lax.axis_size(axis)
    pairs = []
    for core in range(2):
        for index in range(size):
            to = route(core, index)
            if to is not None:
                pairs.append((core * size + index, to[0] * size + to[1]))
    return lax.ppermute(value, ("section", axis), pairs)


def on_device(
    layer_in, cotangent, lengths, block_order, w_qkv, w_out, w_fc, w_proj, norm_gains, norm_biases
):
    tokens, width = layer_in.shape[2:]
    blocks = lax.axis_size("seq")
    ranks = lax.axis_size("dp")
    half = blocks // 2
    core = lax.axis_index("section")
    place_dp = lax.axis_index("dp")
    place_seq = lax.axis_index("seq")
    first_core = core == 0
    group = place_seq // half
    linked = blocks == LINKED and ranks == LINKED

    def per_core(left, right):
        return jnp.where(first_core, left, right)

    def after(value, *others):
        return lax.optimization_barrier((value, others))[0]

    def own_rows(value):
        value = value[:, 0]
        mine = lax.dynamic_index_in_dim(value, group, 0, False)
        other = lax.dynamic_index_in_dim(value, 1 - group, 0, False)
        moved = send_joint(other, "seq", lambda c, z: (1, z ^ half) if c == 1 else None)
        return per_core(mine, moved)

    def back_home(first, second):
        crossed = send_joint(
            per_core(second, first), "seq", lambda c, z: (1, z) if c == 0 else (0, z ^ half)
        )
        along = send_joint(second, "seq", lambda c, z: (1, z ^ half) if c == 1 else None)
        mine = per_core(first, crossed)
        other = per_core(crossed, along)
        return jnp.where(group == 0, jnp.stack([mine, other]), jnp.stack([other, mine]))

    steps = []
    bit = 1
    while bit < half:
        steps.append(bit)
        bit *= 2
    my_block = per_core(place_seq, place_seq ^ half)
    block_ids = [my_block]
    for bit in steps:
        block_ids = block_ids + [b ^ bit for b in block_ids]
    block_ids = block_ids + [b ^ half for b in block_ids]
    limit = lax.dynamic_index_in_dim(lengths[:, 0], group, 0, False)
    starts = block_order[jnp.stack(block_ids)] * tokens
    place = jnp.concatenate([limit[None], starts]).astype(jnp.int32)

    def gather_keys(own):
        parts = [own]
        for bit in steps:
            route = [(z, z ^ bit) for z in range(blocks)]
            parts = parts + [lax.ppermute(p, "seq", route) for p in parts]
        return parts + [swap_cores(p) for p in parts]

    def scatter_keys(parts):
        cut = len(parts) // 2
        moved = [swap_cores(p) for p in parts[cut:]]
        parts = [(p.astype(f32) + m.astype(f32)).astype(bf16) for p, m in zip(parts[:cut], moved)]
        for bit in reversed(steps):
            cut = len(parts) // 2
            route = [(z, z ^ bit) for z in range(blocks)]
            moved = [lax.ppermute(p, "seq", route) for p in parts[cut:]]
            parts = [(p.astype(f32) + m.astype(f32)).astype(bf16) for p, m in zip(parts[:cut], moved)]
        return parts[0]

    masters = (w_qkv[0], w_out[0], w_fc[0], w_proj[0])
    parts = (3, 1, ranks, 0)
    own_norms = jnp.concatenate([norm_gains[0], norm_biases[0]])

    def attend(projected):
        normed, query, own_keys = projected
        keys = gather_keys(own_keys)
        attended, lse, keys = attention_forward(place, query, keys, blocks)
        return normed, query, keys, lse, attended

    def forward(hidden, layer, attention):
        _, wout, wfc, wproj = weights[layer]
        normed, query, keys, lse, attended = attention
        attended, residual, second, slope, activated, result = out_and_mlp(
            attended, hidden, norms[layer], wout, wfc, wproj
        )
        return result, (hidden, normed, query, keys, attended, lse, residual, second, slope, activated)

    if linked:
        weights, norms, rows_cot, saved_first, first_out, attention = gather_and_forward(
            place, layer_in, cotangent, own_norms, masters, parts, ranks
        )
    else:
        other_norms = swap_cores(own_norms)
        norms = (per_core(own_norms, other_norms), per_core(other_norms, own_norms))
        rows_in, rows_cot = own_rows(layer_in), own_rows(cotangent)
        weights = gather_weights(masters, parts, ranks)
        first_out, saved_first = forward(rows_in, 0, attend(project_qkv(rows_in, norms[0], weights[0][0])))
        attention = attend(project_qkv(first_out, norms[1], weights[1][0]))
    second_out, saved_second = forward(first_out, 1, attention)

    def backward(upstream, saved, layer, layers, rows):
        wqkv, wout, wfc, wproj = weights[layer]
        hidden, normed, query, keys, attended, lse, residual, second, slope, activated = saved
        d_residual, d_att, vectors_two, *mlp_grads = mlp_back(
            upstream, slope, activated, second, attended, residual, norms[layer], wout, wfc, wproj
        )
        kept, given = mlp_grads[0::2], mlp_grads[1::2]
        if linked:
            d_query, d_keys, sums, home = attention_backward(
                place, query, d_att, lse, keys, kept, given, (4, 5, 2), layers, rows
            )
            d_pair = d_keys[0]
        else:
            d_query, d_keys, _, home = attention_backward(place, query, d_att, lse, keys)
            d_pair = scatter_keys(d_keys)
            sums = plain_sums(kept, given)
        sent, vectors_one, *qkv_grads = qkv_back(d_query, d_pair, normed, hidden, d_residual, norms[layer], wqkv)
        return sent, sums, home, qkv_grads, jnp.stack([vectors_one[0], vectors_two[0], vectors_one[1], vectors_two[1]])

    def plain_sums(kept, given):
        total = [(k.astype(f32) + swap_cores(g).astype(f32)).astype(k.dtype) for k, g in zip(kept, given)]
        return [lax.psum(lax.psum_scatter(t, "dp", scatter_dimension=0), "seq") for t in total]

    def by_rank(vectors):
        return vectors.reshape(4, ranks, -1).transpose(1, 0, 2)

    second_grad, second_sums, layer_results, second_qkv, second_vectors = backward(
        rows_cot, saved_second, 1, (0, 1), (first_out, second_out)
    )
    first_grad, first_sums, grad_home, first_qkv, first_vectors = backward(
        second_grad, saved_first, 0, (1,), (second_grad,)
    )
    kept = [second_qkv[0], by_rank(per_core(first_vectors, second_vectors)), first_qkv[0]]
    given = [second_qkv[1], by_rank(per_core(second_vectors, first_vectors)), first_qkv[1]]
    if linked:
        (second_last, vectors, first_last), first_home, other = reduce_last(
            kept, given, (5, 1, 5), (1, None, 0), first_grad, first_sums, second_sums
        )
        grad_results = per_core(first_home, grad_home)
    else:
        second_last, vectors, first_last = plain_sums(kept, given)
        layer_results = back_home(first_out, second_out)
        grad_results = back_home(first_grad, second_grad)
    first_sums = list(first_sums) + [first_last]
    second_sums = list(second_sums) + [second_last]
    if not linked:
        other = [swap_cores(per_core(b, a)) for a, b in zip(first_sums, second_sums)]
    shapes = [w_proj.shape[1:], w_fc.shape[1:], w_out.shape[1:], w_qkv.shape[1:]]
    g_proj, g_fc, g_out, g_qkv = finish(first_sums, second_sums, other, shapes, (1, ranks, 1, 3))
    return (
        layer_results[None, :, None],
        grad_results[None, :, None],
        g_qkv[None],
        g_out[None],
        g_fc[None],
        g_proj[None],
        vectors[:2][None],
        vectors[2:][None],
    )


def solution(mesh):
    return jax.shard_map(
        on_device,
        mesh=mesh,
        in_specs=(
            P(None, "dp", "seq", None),
            P(None, "dp", "seq", None),
            P(None, "dp"),
            P(),
            P("section", "dp", None),
            P("section", "dp", None),
            P("section", "dp", None),
            P("section", "dp", None),
            P("section", None, None),
            P("section", None, None),
        ),
        out_specs=(
            P("section", None, "dp", "seq", None),
            P("section", None, "dp", "seq", None),
            P("section", "dp", None),
            P("section", "dp", None),
            P("section", "dp", None),
            P("section", "dp", None),
            P("section", None, "dp"),
            P("section", None, "dp"),
        ),
        check_vma=False,
    )
```
